256 devices in a mesh: fluid: 128 (over z, x, y_lo, core), group: 2 (over y_hi).
Axes of the slice: x: 4, y: 4 (y_hi: 2, y_lo: 2; y = y_hi * 2 + y_lo), z: 8, core: 2. Of those that a mesh axis runs over, the one named last changes fastest.
Arguments:
- populations: float32 [19, 256, 128, 128], P(None, 'fluid', 'group'), may hold values from 0.01 to 0.25
- relax_rates: float32 [19], replicated, may hold values from 0.5 to 1.9
- slab: int32 [131072, 1], P(('fluid', 'group')), may hold values from 0 to 127; in each aligned block of 512 rows (0 to 511, 512 to 1023, ...) at most 8 rows name the same one
- stencil_base: int32 [131072], P(('fluid', 'group')), may hold values from 0 to 8063, as said below
- frac: float32 [3, 131072], P(None, ('fluid', 'group')), may hold values from 0.45 to 0.55
- atom_vel: float32 [3, 131072], P(None, ('fluid', 'group')), may hold values from -2 to 2
- friction: float32 [131072], P(('fluid', 'group')), may hold values from 2 to 20
- features: bfloat16 [128, 131072], P(None, ('fluid', 'group')), may hold values from -6 to 6
- neighbors: int32 [131072, 16], P(('fluid', 'group')), may hold values from 0 to 1535
- bonds: float32 [3, 131072, 16], P(None, ('fluid', 'group')), may hold values from -3 to 3
- w_self: bfloat16 [128, 128], replicated, may hold values from -0.5 to 0.5
- w_nbr: bfloat16 [128, 128], replicated, may hold values from -0.5 to 0.5
- w_rbf: float32 [128, 16], replicated, may hold values from -1.5 to 1.5
- w_out: float32 [128], replicated, may hold values from -0.5 to 0.5
Outputs:
- new_pops: float32 [19, 256, 128, 128], P(None, 'fluid', 'group')
- atom_force: float32 [3, 131072], P(None, ('fluid', 'group'))
- new_features: bfloat16 [128, 131072], P(None, ('fluid', 'group'))
The draws below stay inside these ranges and needn't reach their ends.
Inputs may be any that keep to these rules, and one draw needn't show every extreme that they name: In the rows of one device no slab is named by more than 8 atoms; in some such blocks one slab is named by exactly 8. `stencil_base`: each value is (z0 * 64 + x0) * 128 + y0 with z0 at most 0, x0 at most 62 and y0 below 128.
All inputs are finite; a program needn't handle non-finite values.
Results may differ from the reference program's by a relative error of at most 0.0023.
Values may be sent and summed in bfloat16 or wider, within the bound.
No kernel may reach another device: no remote copies, remote signals or barrier semaphores. Data moves between devices by JAX's collectives and lax.ppermute only.
A program may use at most 64 MiB of HBM per device.

```python
import math
import jax
import jax.numpy as jnp
import numpy as np
from jax import lax

CZ = 2
CX = 64
NY = 128
A_DEV = 512
F = 128
K = 16
R = 16
CAP = 8
NZ = 256
NX = 128
ATOMS = 131072
N_FLUID = 128
N_GROUP = 2


def draw_stencil_base(key, part):
    key = jax.random.fold_in(key, 11)
    first, second, third = jax.random.split(key, 3)
    plane = jax.random.randint(first, (ATOMS,), 0, CZ - 1)
    column = jax.random.randint(second, (ATOMS,), 0, CX - 1)
    row = jax.random.randint(third, (ATOMS,), 0, NY)
    return ((plane * CX + column) * NY + row).astype(jnp.int32)


def plant(entries, key, smallest, largest):
    extent = entries.shape
    spot = [jax.random.randint(jax.random.fold_in(key, axis), (), 0, extent[axis]) for axis in range(len(extent))]
    entries = entries.at[tuple(spot)].set(smallest)
    longest = extent.index(max(extent))
    spot[longest] = (spot[longest] + 1) % extent[longest]
    return entries.at[tuple(spot)].set(largest)


def block_levels(key, shape, shards, smallest, largest):
    def one(axis_at, blocks):
        draws = jax.random.uniform(jax.random.fold_in(jax.random.fold_in(key, 6), axis_at), (blocks,), jnp.float32, smallest / len(shards), largest / len(shards))
        return jnp.repeat(jnp.exp(draws), shape[axis_at] // blocks).reshape((-1,) + (1,) * (len(shape) - axis_at - 1))

    loudness = one(*shards[0])
    for cut in shards[1:]:
        loudness = loudness * one(*cut)
    return loudness


def routed_block(rng, own, number, rows, number_of, top, reach, lean):
    ranking = jax.random.permutation(rng, number_of)
    heavy_load, ordinary = load_shares(number_of, rows * top, reach, lean, True), load_shares(number_of, rows * top, reach, lean, False)
    places = jnp.arange(number_of)

    def named(tallies, rotation):
        used = int((tallies > 0).sum())
        fixed = max(1, used // 4)
        moved = fixed + (places - fixed + rotation * (used - fixed)) % max(1, number_of - fixed)
        return jnp.zeros((number_of,), jnp.int32).at[ranking[jnp.where(places < fixed, places, moved)]].set(jnp.asarray(tallies, jnp.int32))

    tallies = jnp.where(number % 4 == 0, named(heavy_load, number // 4), named(ordinary, number - number // 4 - 1))
    mixed = jax.random.permutation(jax.random.fold_in(own, 3), number_of)
    giver, sink = mixed[0:number_of // 2 * 2:2], mixed[1:number_of // 2 * 2:2]
    margin = jnp.minimum(tallies[giver] - 1, reach - tallies[sink]) // 2
    margin = jnp.where((giver == ranking[0]) | (sink == ranking[0]) | (tallies[sink] == 0), 0, jnp.maximum(margin, 0))
    moved = jax.random.randint(jax.random.fold_in(own, 4), (number_of // 2,), 0, 1 << 20) % (margin + 1)
    tallies = tallies.at[giver].add(-moved).at[sink].add(moved)
    members = jnp.searchsorted(jnp.cumsum(tallies), jnp.arange(rows * top), side="right").astype(jnp.int32)
    listing = members.reshape(top, rows).T
    listing = listing[jax.random.permutation(jax.random.fold_in(own, 1), rows)]
    rotation = jax.random.randint(jax.random.fold_in(own, 2), (rows, 1), 0, top)
    return jnp.take_along_axis(listing, (jnp.arange(top)[None, :] + rotation) % top, axis=1)


def load_shares(count, total, bound, skew, full):
    weights = [(1 << 20) // math.isqrt(standing ** skew) + 1 for standing in range(1, count + 1)]
    largest = bound if full else min(bound, max(-(-total // count), total * weights[0] // sum(weights)))
    least = 1 if total - largest >= count - 1 else 0
    given, rest = [largest] + [least] * (count - 1), total - largest - least * (count - 1)
    while rest > 0:
        movable = [i for i in range(1, count) if given[i] < largest] or [i for i in range(1, count) if given[i] < bound]
        mass, budget = sum([weights[i] for i in movable]), rest
        for i in movable:
            addition = min(bound - given[i], max(1, budget * weights[i] // mass), rest)
            given[i] = given[i] + addition
            rest = rest - addition
    return np.array(given)


def centred(key, extent, scale, reach, cuts=(), kind=jnp.bfloat16):
    factor_of = block_levels(key, extent, cuts, -0.22, 0.18) if cuts else 1.0
    drawn = jax.random.normal(key, extent, jnp.float32) * scale * factor_of
    return jnp.minimum(jnp.maximum(drawn, -reach), reach).astype(kind)


def setup_inputs(seed: int = 0) -> dict:
    seeds = jax.random.split(jax.random.key(seed), 15)
    populations = jnp.clip(0.01 + 0.24 * jax.random.uniform(seeds[0], (19, NZ, NX, NY), jnp.float32) ** block_levels(seeds[0], (19, NZ, NX, NY), ((1, 128), (2, 2)), -0.2, 0.2), 0.01, 0.25)
    relax_rates = jnp.clip(jax.random.uniform(seeds[1], (19,), jnp.float32, 0.5, 1.9), 0.5, 1.9)
    slab_keys = jax.random.split(jax.random.fold_in(seeds[2], 1), ATOMS // A_DEV)
    slab_turns = jax.random.permutation(jax.random.fold_in(seeds[2], 3), ATOMS // A_DEV)
    slab = jax.vmap(lambda own, number: routed_block(jax.random.fold_in(seeds[2], 2), own, number, A_DEV, N_FLUID, 1, CAP, 2))(slab_keys, slab_turns).reshape((ATOMS, 1))
    stencil_base = draw_stencil_base(jax.random.fold_in(seeds[14], 71), 0)
    frac = jnp.clip(0.45 + 0.100000024 * jax.random.uniform(seeds[4], (3, ATOMS), jnp.float32) ** block_levels(seeds[4], (3, ATOMS), ((1, 256),), -0.2, 0.2), 0.45, 0.55)
    atom_vel = centred(seeds[5], (3, ATOMS), 0.15, 2.0, ((1, 256),), jnp.float32)
    friction = jnp.clip(jnp.exp(math.log(20.0) - 2.3025851 * jax.random.uniform(seeds[6], (ATOMS,), jnp.float32) ** block_levels(seeds[6], (ATOMS,), ((0, 256),), -0.2, 0.2)), 2.0, 20.0)
    features = centred(seeds[7], (F, ATOMS), 1.0, 6.0, ((1, 256),))
    neighbors = plant(jax.random.randint(seeds[8], (ATOMS, K), 0, 3 * A_DEV), jax.random.fold_in(seeds[8], 1), 0, (3 * A_DEV) - 1).astype(jnp.int32)
    bonds = centred(seeds[9], (3, ATOMS, K), 1.0, 3.0, ((1, 256),), jnp.float32)
    w_self = centred(seeds[10], (F, F), F ** -0.5, 0.5)
    w_nbr = centred(seeds[11], (F, F), F ** -0.5, 0.5)
    w_rbf = centred(seeds[12], (F, R), R ** -0.5, 1.5, (), jnp.float32)
    w_out = centred(seeds[13], (F,), F ** -0.5, 0.5, (), jnp.float32)
    return {"populations": populations, "relax_rates": relax_rates, "slab": slab, "stencil_base": stencil_base, "frac": frac, "atom_vel": atom_vel, "friction": friction, "features": features, "neighbors": neighbors, "bonds": bonds, "w_self": w_self, "w_nbr": w_nbr, "w_rbf": w_rbf, "w_out": w_out}


RADIAL_REACH = 4.0

def speed_list():
    return [[0, 0, 0], [1, 0, 0], [-1, 0, 0], [0, 1, 0], [0, -1, 0], [0, 0, 1], [0, 0, -1], [1, 1, 0], [-1, -1, 0], [1, -1, 0], [-1, 1, 0], [1, 0, 1], [-1, 0, -1], [1, 0, -1], [-1, 0, 1], [0, 1, 1], [0, -1, -1], [0, 1, -1], [0, -1, 1]]

def lattice_weights():
    return [1.0 / 3.0] + [1.0 / 18.0] * 6 + [1.0 / 36.0] * 12

def moment_table():
    tables = []
    for speed in speed_list():
        along_x = float(speed[0])
        along_y = float(speed[1])
        along_z = float(speed[2])
        tables.append([1.0, along_x, along_y, along_z, along_x * along_y, along_x * along_z, along_y * along_z, along_x * along_x, along_y * along_y, along_z * along_z, along_x * along_y * along_y, along_x * along_z * along_z, along_x * along_x * along_y, along_x * along_x * along_z, along_y * along_y * along_z, along_y * along_z * along_z, along_x * along_x * along_y * along_y, along_x * along_x * along_z * along_z, along_y * along_y * along_z * along_z])
    return [[tables[column][moment] for column in range(19)] for moment in range(19)]

def invert_rows(matrix):
    order = len(matrix)
    joined = [list(matrix[place]) + [1.0 if other == place else 0.0 for other in range(order)] for place in range(order)]
    for column in range(order):
        pivot_place = max(range(column, order), key=lambda place: abs(joined[place][column]))
        joined[column], joined[pivot_place] = (joined[pivot_place], joined[column])
        pivot = joined[column][column]
        joined[column] = [entry / pivot for entry in joined[column]]
        for place in range(order):
            if place != column:
                factor = joined[place][column]
                if factor != 0.0:
                    joined[place] = [entry - factor * upper for entry, upper in zip(joined[place], joined[column])]
    return [joined[place][order:] for place in range(order)]

def moment_inverse():
    return invert_rows(moment_table())

def fluid_moments(pops):
    lattice = jnp.asarray(np.array(speed_list()).T, jnp.float32)
    density = lax.optimization_barrier(jnp.sum(pops, axis=0))
    velocity = jnp.dot(lattice, pops, precision=lax.Precision.HIGHEST) / density
    return (density, velocity)

def collide(pops, density, velocity, force, rates):
    lattice = jnp.asarray(np.array(speed_list()), jnp.float32)
    weights = jnp.asarray(np.array(lattice_weights()), jnp.float32)[:, None]
    along = jnp.dot(lattice, velocity, precision=lax.Precision.HIGHEST)
    speed_sq = lax.optimization_barrier(jnp.sum(velocity * velocity, axis=0))
    equilibrium = weights * density * (1.0 + 3.0 * along + 4.5 * along * along - 1.5 * speed_sq)
    moments = jnp.dot(jnp.asarray(moment_table(), jnp.float32), pops - equilibrium, precision=lax.Precision.HIGHEST)
    inverse = jnp.asarray(moment_inverse(), jnp.float32)
    relaxed = jnp.dot(inverse, rates[:, None] * moments, precision=lax.Precision.HIGHEST)
    forcing = jnp.dot(inverse[:, 1:4], force, precision=lax.Precision.HIGHEST)
    return pops - relaxed + forcing

def stencil(plane, column, row, frac, width, depth):
    nodes = []
    weights = []
    for lift_z in (0, 1):
        for lift_x in (0, 1):
            for lift_y in (0, 1):
                node = ((plane + lift_z) * width + column + lift_x) * depth + (row + lift_y) % depth
                factor_x = frac[0] if lift_x else 1.0 - frac[0]
                factor_y = frac[1] if lift_y else 1.0 - frac[1]
                factor_z = frac[2] if lift_z else 1.0 - frac[2]
                nodes.append(node.astype(jnp.int32))
                weights.append(factor_x * factor_y * factor_z)
    return (jnp.stack(nodes), jnp.stack(weights))

def interpolate(velocity, nodes, weights):
    return lax.optimization_barrier(jnp.sum(weights[None] * velocity[:, nodes], axis=1))

def spread(drag, nodes, weights, cells):
    terms = (-weights[None] * drag[:, None, :]).reshape(3, -1)
    return jnp.zeros((3, cells), jnp.float32).at[:, nodes.reshape(-1)].add(terms)

def potential(window, own, nbrs, bonds, w_self, w_nbr, w_rbf, w_out):
    own_proj = jnp.dot(w_self, own, preferred_element_type=jnp.float32)
    projected = jnp.dot(w_nbr, window, preferred_element_type=jnp.float32).astype(jnp.bfloat16)
    picked = projected[:, nbrs.reshape(-1)].reshape(own.shape[0], nbrs.shape[0], nbrs.shape[1])
    length = jnp.sqrt(lax.optimization_barrier(jnp.sum(bonds * bonds, axis=0)) + 1e-06)
    basis = w_rbf.shape[1]
    spacing = RADIAL_REACH / (basis - 1)
    centers = jnp.arange(basis).astype(jnp.float32) * spacing
    scaled = (length[None] - centers[:, None, None]) / spacing
    radial = jnp.exp(-scaled * scaled)
    edge = jnp.einsum('fr,rak->fak', w_rbf, radial, precision=lax.Precision.HIGHEST)
    hidden = jax.nn.silu(own_proj[:, :, None] + picked.astype(jnp.float32) + edge)
    scalar = jnp.einsum('f,fak->ak', w_out, hidden, precision=lax.Precision.HIGHEST)
    force = jnp.einsum('ak,cak->ca', scalar, bonds, precision=lax.Precision.HIGHEST)
    updated = (own.astype(jnp.float32) + lax.optimization_barrier(jnp.mean(hidden, axis=2))).astype(jnp.bfloat16)
    return (force, updated)

def reference(populations, relax_rates, slab, stencil_base, frac, atom_vel, friction, features, neighbors, bonds, w_self, w_nbr, w_rbf, w_out):
    speeds = speed_list()
    cells = NZ * NX * NY
    flat = populations.reshape(19, cells)
    density, velocity = fluid_moments(flat)
    target = slab[:, 0]
    group_of = jnp.arange(ATOMS, dtype=jnp.int32) // A_DEV % N_GROUP
    plane = target * CZ + stencil_base // (NY * CX)
    column = group_of * CX + stencil_base // NY % CX
    row = stencil_base % NY
    nodes, weights = stencil(plane, column, row, frac, NX, NY)
    drag = friction * (interpolate(velocity, nodes, weights) - atom_vel)
    force_field = spread(drag, nodes, weights, cells)
    post = collide(flat, density, velocity, force_field, relax_rates).reshape(19, NZ, NX, NY)
    moved = []
    for number in range(19):
        shift_x = speeds[number][0]
        shift_y = speeds[number][1]
        shift_z = speeds[number][2]
        moved.append(jnp.roll(post[number], (shift_z, shift_x, shift_y), axis=(0, 1, 2)))
    new_pops = jnp.stack(moved)
    blocks = features.reshape(F, N_FLUID, N_GROUP, A_DEV).transpose(1, 2, 0, 3)
    windows = jnp.concatenate([jnp.roll(blocks, 1, axis=0), blocks, jnp.roll(blocks, -1, axis=0)], axis=3).reshape(-1, F, 3 * A_DEV)
    own_blocks = blocks.reshape(-1, F, A_DEV)
    nbr_blocks = neighbors.reshape(-1, A_DEV, K)
    bond_blocks = bonds.reshape(3, -1, A_DEV, K).transpose(1, 0, 2, 3)
    forces, updated = lax.map(lambda items: potential(items[0], items[1], items[2], items[3], w_self, w_nbr, w_rbf, w_out), (windows, own_blocks, nbr_blocks, bond_blocks))
    conservative = forces.transpose(1, 0, 2).reshape(3, ATOMS)
    new_features = updated.transpose(1, 0, 2).reshape(F, ATOMS)
    return (new_pops, conservative + drag, new_features)
```

```python
import functools

import jax
import jax.numpy as jnp
from jax import lax
from jax.experimental import pallas as pl
from jax.experimental.pallas import tpu as pltpu
from jax.sharding import PartitionSpec as P

F32 = jnp.float32
BF16 = jnp.bfloat16
I32 = jnp.int32

RADIAL_REACH = 4.0
SLOTS = 8

SPEEDS = (
    (0, 0, 0),
    (1, 0, 0),
    (-1, 0, 0),
    (0, 1, 0),
    (0, -1, 0),
    (0, 0, 1),
    (0, 0, -1),
    (1, 1, 0),
    (-1, -1, 0),
    (1, -1, 0),
    (-1, 1, 0),
    (1, 0, 1),
    (-1, 0, -1),
    (1, 0, -1),
    (-1, 0, 1),
    (0, 1, 1),
    (0, -1, -1),
    (0, 1, -1),
    (0, -1, 1),
)
RISING = (11, 14, 15, 18)
FALLING = (12, 13, 16, 17)
FLAT = (0, 7, 8, 9, 10)
CALM = (0, 7, 8, 9, 10, 11, 12, 13, 14, 15, 16, 17, 18)

VMEM_LIMIT = 48 * 1024 * 1024


def halves(value):
    high = value.astype(BF16)
    low = (value - high.astype(F32)).astype(BF16)
    return high, low


def thirds(value):
    high = value.astype(BF16)
    rest = value - high.astype(F32)
    middle = rest.astype(BF16)
    low = (rest - middle.astype(F32)).astype(BF16)
    return high, middle, low


def mm(a, b):
    return jnp.dot(a, b, preferred_element_type=F32)


def mm_nt(a, b):
    return lax.dot_general(a, b, (((1,), (1,)), ((), ())), preferred_element_type=F32)


def iota(shape, dim):
    return lax.broadcasted_iota(I32, shape, dim)


def pack_kernel(slab_ref, base_ref, frac_ref, vel_ref, fric_ref, out_ref, rank_ref):
    atoms = slab_ref.shape[1]
    slabs = out_ref.shape[0]
    named = iota((slabs, atoms), 0) == slab_ref[...]
    one_hot = jnp.where(named, 1.0, 0.0)
    one_hot_b = one_hot.astype(BF16)
    earlier = jnp.where(iota((atoms, atoms), 0) < iota((atoms, atoms), 1), 1.0, 0.0).astype(BF16)
    before = mm(one_hot_b, earlier)
    rank = jnp.sum(one_hot * before, axis=0, keepdims=True)
    rank_ref[...] = rank
    mine = iota((SLOTS, atoms), 0).astype(F32) == rank
    rows = [frac_ref[c : c + 1, :] for c in range(3)]
    rows += [vel_ref[c : c + 1, :] for c in range(3)]
    rows += [fric_ref[...], base_ref[...].astype(F32)]
    spread = [jnp.where(mine, row, 0.0) for row in rows]
    spread.append(jnp.zeros((128 - SLOTS * len(rows), atoms), F32))
    high, middle, low = thirds(jnp.concatenate(spread, axis=0))
    out_ref[...] = mm_nt(one_hot_b, high) + (mm_nt(one_hot_b, middle) + mm_nt(one_hot_b, low))


def pack(slab, base, frac, vel, fric, slabs):
    atoms = slab.shape[1]
    return pl.pallas_call(
        pack_kernel,
        out_shape=(
            jax.ShapeDtypeStruct((slabs, 128), F32),
            jax.ShapeDtypeStruct((1, atoms), F32),
        ),
        name="pack",
        compiler_params=pltpu.CompilerParams(vmem_limit_bytes=VMEM_LIMIT),
        cost_estimate=pl.CostEstimate(flops=400_000_000, bytes_accessed=4_000_000, transcendentals=0),
    )(slab, base, frac, vel, fric)


def moments_of(d):
    m = [None] * 19
    quad = {}
    for name, (pp, nn, pn, np_) in dict(xy=(7, 8, 9, 10), xz=(11, 12, 13, 14), yz=(15, 16, 17, 18)).items():
        same, cross = d[pp] + d[nn], d[pn] + d[np_]
        odd_same, odd_cross = d[pp] - d[nn], d[pn] - d[np_]
        quad[name] = (same + cross, same - cross, odd_same + odd_cross, odd_same - odd_cross)
    sxy, m[4], m[10], m[12] = quad["xy"]
    sxz, m[5], m[11], m[13] = quad["xz"]
    syz, m[6], m[15], m[14] = quad["yz"]
    m[16], m[17], m[18] = sxy, sxz, syz
    ax, ay, az = d[1] + d[2], d[3] + d[4], d[5] + d[6]
    m[0] = (d[0] + ax) + (ay + az) + (sxy + (sxz + syz))
    m[1] = (d[1] - d[2]) + (m[10] + m[11])
    m[2] = (d[3] - d[4]) + (m[12] + m[15])
    m[3] = (d[5] - d[6]) + (m[13] + m[14])
    m[7] = ax + (sxy + sxz)
    m[8] = ay + (sxy + syz)
    m[9] = az + (sxz + syz)
    return m


def populations_of(m):
    f = [None] * 19
    for (pp, nn, pn, np_), (s, c, first, second) in (
        ((7, 8, 9, 10), (m[16], m[4], m[10], m[12])),
        ((11, 12, 13, 14), (m[17], m[5], m[11], m[13])),
        ((15, 16, 17, 18), (m[18], m[6], m[15], m[14])),
    ):
        same, cross = 0.25 * (s + c), 0.25 * (s - c)
        odd_same, odd_cross = 0.25 * (first + second), 0.25 * (first - second)
        f[pp], f[nn] = same + odd_same, same - odd_same
        f[pn], f[np_] = cross + odd_cross, cross - odd_cross
    for plus, minus, square, line, squares, lines in (
        (1, 2, m[7], m[1], (m[16], m[17]), (m[10], m[11])),
        (3, 4, m[8], m[2], (m[16], m[18]), (m[12], m[15])),
        (5, 6, m[9], m[3], (m[17], m[18]), (m[13], m[14])),
    ):
        even = 0.5 * (square - (squares[0] + squares[1]))
        odd = 0.5 * (line - (lines[0] + lines[1]))
        f[plus], f[minus] = even + odd, even - odd
    f[0] = m[0] - (m[7] + (m[8] + m[9])) + (m[16] + (m[17] + m[18]))
    return f


def equilibrium_of(density, u):
    ux, uy, uz = u
    rest = 1.0 - 1.5 * (ux * ux + uy * uy + uz * uz)
    eq = [None] * 19
    eq[0] = (1.0 / 3.0) * density * rest
    scale_axis, scale_diagonal = (1.0 / 18.0) * density, (1.0 / 36.0) * density
    for plus, minus, along, scale in (
        (1, 2, ux, scale_axis),
        (3, 4, uy, scale_axis),
        (5, 6, uz, scale_axis),
        (7, 8, ux + uy, scale_diagonal),
        (9, 10, ux - uy, scale_diagonal),
        (11, 12, ux + uz, scale_diagonal),
        (13, 14, ux - uz, scale_diagonal),
        (15, 16, uy + uz, scale_diagonal),
        (17, 18, uy - uz, scale_diagonal),
    ):
        even = rest + 4.5 * along * along
        odd = 3.0 * along
        eq[plus], eq[minus] = scale * (even + odd), scale * (even - odd)
    return eq


def shifted(plane, number):
    cx, cy, _ = SPEEDS[number]
    if cy:
        plane = pltpu.roll(plane, cy % plane.shape[1], 1)
    if cx:
        plane = pltpu.roll(plane, cx % plane.shape[0], 0)
    return plane


def edge(plane, number):
    width = plane.shape[0]
    return plane[0:1] if SPEEDS[number][0] > 0 else plane[width - 1 : width]


def relax_kernel(
    rates_ref, pops_ref, vel_ref, axis_ref, calm_ref, up_ref, down_ref, side_ref, side_up_ref, side_down_ref, post_ref
):
    cells = pops_ref.shape[1]
    width = cells // 2

    def chunk(step, carry):
        rows = pl.ds(pl.multiple_of(step * 8, 8), 8)
        f = [pops_ref[i, rows, :] for i in range(19)]
        low = moments_of(f)
        density = low[0]
        inverse = 1.0 / density
        u = [low[c] * inverse for c in (1, 2, 3)]
        for c in range(3):
            vel_ref[c, rows, :] = u[c]
        eq = equilibrium_of(density, u)
        m = moments_of([f[i] - eq[i] for i in range(19)])
        relaxed = populations_of([rates_ref[i] * m[i] for i in range(19)])
        for i in range(19):
            post_ref[i, rows, :] = f[i] - relaxed[i]
        return carry

    lax.fori_loop(0, cells // 8, chunk, 0)

    def plane(number, z):
        return shifted(post_ref[number, z * width : (z + 1) * width, :], number)

    axis_ref[...] = post_ref[1:7]
    edges = []
    for place, number in enumerate(CALM):
        if number in FLAT:
            for z in (0, 1):
                value = plane(number, z)
                calm_ref[place, z * width : (z + 1) * width, :] = value
                if number:
                    edges.append(edge(value, number))
    corners_up, corners_down = [], []
    for outgoing, numbers, stays, corners in (
        (up_ref, RISING, 1, corners_up),
        (down_ref, FALLING, 0, corners_down),
    ):
        for place, number in enumerate(numbers):
            value = plane(number, 1 - stays)
            calm_ref[CALM.index(number), stays * width : (stays + 1) * width, :] = value
            leaves = plane(number, stays)
            calm_ref[CALM.index(number), (1 - stays) * width : (2 - stays) * width, :] = leaves
            outgoing[place] = leaves
            if SPEEDS[number][0]:
                edges.append(edge(value, number))
                corners.append(edge(leaves, number))
    lanes = pops_ref.shape[2]
    side_ref[...] = jnp.concatenate(edges + [jnp.zeros((16 - len(edges), lanes), F32)], axis=0)
    side_up_ref[...] = jnp.concatenate(corners_up + [jnp.zeros((6, lanes), F32)], axis=0)
    side_down_ref[...] = jnp.concatenate(corners_down + [jnp.zeros((6, lanes), F32)], axis=0)


def relax(rates, pops):
    _, cells, lanes = pops.shape
    width = cells // 2
    vmem = pl.BlockSpec(memory_space=pltpu.VMEM)
    return pl.pallas_call(
        relax_kernel,
        in_specs=[pl.BlockSpec(memory_space=pltpu.SMEM), vmem],
        out_specs=[vmem] * 8,
        out_shape=(
            jax.ShapeDtypeStruct((3, cells, lanes), F32),
            jax.ShapeDtypeStruct((6, cells, lanes), F32),
            jax.ShapeDtypeStruct((13, cells, lanes), F32),
            jax.ShapeDtypeStruct((4, width, lanes), F32),
            jax.ShapeDtypeStruct((4, width, lanes), F32),
            jax.ShapeDtypeStruct((16, lanes), F32),
            jax.ShapeDtypeStruct((8, lanes), F32),
            jax.ShapeDtypeStruct((8, lanes), F32),
        ),
        scratch_shapes=[pltpu.VMEM((19, cells, lanes), F32)],
        name="relax",
        compiler_params=pltpu.CompilerParams(vmem_limit_bytes=VMEM_LIMIT),
        cost_estimate=pl.CostEstimate(flops=10_000_000, bytes_accessed=6_000_000, transcendentals=0),
    )(rates, pops)


def couple_kernel(mail_ref, vel_ref, reply_ref, force_ref, wy_hi, wy_lo, a_hi, a_lo):
    comps, cells, depth = vel_ref.shape
    width = cells // 2
    slots = mail_ref.shape[0]
    t = mail_ref[...].T
    field = lambda v: t[v * SLOTS : (v + 1) * SLOTS, :]
    fx, fy, fz = field(0), field(1), field(2)
    atom_vel = [field(3), field(4), field(5)]
    friction = field(6)
    base = field(7).astype(I32)
    x0 = (base // depth) % width
    y0 = base % depth
    y1 = (y0 + 1) % depth
    gx, gy, gz = 1.0 - fx, 1.0 - fy, 1.0 - fz
    row_y = iota((depth, slots), 0)
    row_x = iota((width, slots), 0)

    v_hi, v_lo = halves(vel_ref[...].reshape(comps * cells, depth))
    along_x = []
    replies = [[], [], []]
    for r in range(SLOTS):
        one = slice(r, r + 1)
        cols = slice(r * slots, (r + 1) * slots)
        wy = jnp.where(row_y == y0[one], gy[one], 0.0) + jnp.where(row_y == y1[one], fy[one], 0.0)
        wx = jnp.where(row_x == x0[one], gx[one], 0.0) + jnp.where(row_x == x0[one] + 1, fx[one], 0.0)
        hi, lo = halves(wy)
        wy_hi[:, cols] = hi
        wy_lo[:, cols] = lo
        seen = mm(v_hi, hi) + (mm(v_lo, hi) + mm(v_hi, lo))
        for c in range(3):
            near = seen[c * cells : c * cells + width]
            far = seen[c * cells + width : (c + 1) * cells]
            value = jnp.sum(wx * (near * gz[one] + far * fz[one]), axis=0, keepdims=True)
            replies[c].append(value)
            pull = friction[one] * (atom_vel[c][one] - value)
            for z, weight in ((0, gz[one]), (1, fz[one])):
                hi_a, lo_a = halves(wx * (weight * pull))
                start = c * cells + z * width
                a_hi[start : start + width, cols] = hi_a
                a_lo[start : start + width, cols] = lo_a
    rows = [row for c in range(3) for row in replies[c]]
    rows.append(jnp.zeros((128 - 3 * SLOTS, slots), F32))
    reply_ref[...] = jnp.concatenate(rows, axis=0).T
    spread = mm_nt(a_hi[...], wy_hi[...]) + (mm_nt(a_lo[...], wy_hi[...]) + mm_nt(a_hi[...], wy_lo[...]))
    force_ref[...] = spread.reshape(comps, cells, depth)


def couple(mail, vel):
    comps, cells, depth = vel.shape
    slabs = mail.shape[0]
    return pl.pallas_call(
        couple_kernel,
        out_shape=(
            jax.ShapeDtypeStruct((slabs, 128), F32),
            jax.ShapeDtypeStruct((comps, cells, depth), F32),
        ),
        scratch_shapes=[
            pltpu.VMEM((depth, SLOTS * slabs), BF16),
            pltpu.VMEM((depth, SLOTS * slabs), BF16),
            pltpu.VMEM((comps * cells, SLOTS * slabs), BF16),
            pltpu.VMEM((comps * cells, SLOTS * slabs), BF16),
        ],
        name="couple",
        compiler_params=pltpu.CompilerParams(vmem_limit_bytes=VMEM_LIMIT),
        cost_estimate=pl.CostEstimate(flops=1_000_000_000, bytes_accessed=6_000_000, transcendentals=0),
    )(mail, vel)


def push_kernel(axis_ref, force_ref, moved_ref, up_ref, down_ref, side_ref):
    cells = axis_ref.shape[1]
    width = cells // 2
    edges = []
    for number in (5, 6, 1, 2, 3, 4):
        place = number - 1
        sign = 0.5 if number % 2 else -0.5
        for z in (0, 1):
            rows = slice(z * width, (z + 1) * width)
            value = shifted(axis_ref[place, rows, :] + sign * force_ref[place // 2, rows, :], number)
            if number == 5:
                if z == 1:
                    up_ref[...] = value
                moved_ref[place, (1 - z) * width : (2 - z) * width, :] = value
            elif number == 6:
                if z == 0:
                    down_ref[...] = value
                moved_ref[place, (1 - z) * width : (2 - z) * width, :] = value
            else:
                moved_ref[place, rows, :] = value
                if number in (1, 2):
                    edges.append(edge(value, number))
    side_ref[...] = jnp.concatenate(edges + [jnp.zeros((4, axis_ref.shape[2]), F32)], axis=0)


def push(axis, force):
    _, cells, lanes = axis.shape
    width = cells // 2
    return pl.pallas_call(
        push_kernel,
        out_shape=(
            jax.ShapeDtypeStruct((6, cells, lanes), F32),
            jax.ShapeDtypeStruct((width, lanes), F32),
            jax.ShapeDtypeStruct((width, lanes), F32),
            jax.ShapeDtypeStruct((8, lanes), F32),
        ),
        name="push",
        compiler_params=pltpu.CompilerParams(vmem_limit_bytes=VMEM_LIMIT),
        cost_estimate=pl.CostEstimate(flops=200_000, bytes_accessed=1_500_000, transcendentals=0),
    )(axis, force)


def gather_kernel(calm_ref, moved_ref, up_ref, down_ref, side_ref, side_up_ref, side_down_ref, out_ref, near_ref):
    cells = calm_ref.shape[1]
    width = cells // 2
    for place, number in enumerate(CALM):
        out_ref[number] = calm_ref[place]
    for place in range(6):
        out_ref[place + 1] = moved_ref[place]
    at = 0
    for number in FLAT[1:]:
        row = 0 if SPEEDS[number][0] > 0 else width - 1
        for z in (0, 1):
            out_ref[number, z * width + row : z * width + row + 1, :] = side_ref[at : at + 1, :]
            at += 1
    for arrived, numbers, stays, corners in (
        (up_ref, RISING, 1, side_up_ref),
        (down_ref, FALLING, 0, side_down_ref),
    ):
        corner = 0
        for place, number in enumerate(numbers):
            start = (1 - stays) * width
            out_ref[number, start : start + width, :] = arrived[place]
            if SPEEDS[number][0]:
                row = 0 if SPEEDS[number][0] > 0 else width - 1
                out_ref[number, stays * width + row : stays * width + row + 1, :] = side_ref[at : at + 1, :]
                out_ref[number, start + row : start + row + 1, :] = corners[corner : corner + 1, :]
                at += 1
                corner += 1
    for place in (0, 1):
        for z in (0, 1):
            tile = z * width + (0 if place == 0 else width - 8)
            near_ref[2 * place + z] = moved_ref[place, tile : tile + 8, :]


def gather(calm, moved, up, down, side, side_up, side_down):
    _, cells, lanes = calm.shape
    return pl.pallas_call(
        gather_kernel,
        out_shape=(
            jax.ShapeDtypeStruct((19, cells, lanes), F32),
            jax.ShapeDtypeStruct((4, 8, lanes), F32),
        ),
        name="gather",
        compiler_params=pltpu.CompilerParams(vmem_limit_bytes=VMEM_LIMIT),
        cost_estimate=pl.CostEstimate(flops=1_000, bytes_accessed=3_000_000, transcendentals=0),
    )(calm, moved, up, down, side, side_up, side_down)


def finish_kernel(
    pops_ref,
    near_ref,
    up_ref,
    down_ref,
    side_ref,
    reply_ref,
    slab_ref,
    rank_ref,
    vel_ref,
    fric_ref,
    pull_ref,
    out_ref,
    force_ref,
    tiles,
    sems,
):
    cells = pops_ref.shape[1]
    width = cells // 2
    rows = iota((8, near_ref.shape[2]), 0)
    copies = []
    for place in (0, 1):
        for z in (0, 1):
            which = 2 * place + z
            kept = rows != (0 if place == 0 else 7)
            tiles[which] = jnp.where(kept, near_ref[which], side_ref[which : which + 1, :])
            start = z * width + (0 if place == 0 else width - 8)
            copies.append(
                pltpu.make_async_copy(tiles.at[which], out_ref.at[1 + place, pl.ds(start, 8), :], sems.at[which])
            )
    copies.append(pltpu.make_async_copy(up_ref, out_ref.at[5, pl.ds(0, width), :], sems.at[4]))
    copies.append(pltpu.make_async_copy(down_ref, out_ref.at[6, pl.ds(width, width), :], sems.at[5]))
    for copy in copies:
        copy.start()

    slabs, atoms = reply_ref.shape[0], slab_ref.shape[1]
    one_hot = jnp.where(iota((slabs, atoms), 0) == slab_ref[...], 1.0, 0.0).astype(BF16)
    high, middle, low = thirds(reply_ref[...].T)
    picked = mm(high, one_hot) + (mm(middle, one_hot) + mm(low, one_hot))
    mine = iota((SLOTS, atoms), 0).astype(F32) == rank_ref[...]
    for c in range(3):
        seen = jnp.sum(jnp.where(mine, picked[c * SLOTS : (c + 1) * SLOTS], 0.0), axis=0, keepdims=True)
        drag = fric_ref[...] * (seen - vel_ref[c : c + 1, :])
        force_ref[c : c + 1, :] = pull_ref[c : c + 1, :] + drag

    for copy in copies:
        copy.wait()


def finish(pops, near, up, down, side, reply, slab, rank, vel, fric, pull):
    atoms = slab.shape[1]
    vmem = pl.BlockSpec(memory_space=pltpu.VMEM)
    anywhere = pl.BlockSpec(memory_space=pl.ANY)
    return pl.pallas_call(
        finish_kernel,
        in_specs=[anywhere] + [vmem] * 10,
        out_specs=[anywhere, vmem],
        out_shape=(
            jax.ShapeDtypeStruct(pops.shape, F32),
            jax.ShapeDtypeStruct((3, atoms), F32),
        ),
        scratch_shapes=[pltpu.VMEM(near.shape, F32), pltpu.SemaphoreType.DMA((6,))],
        input_output_aliases={0: 0},
        name="finish",
        compiler_params=pltpu.CompilerParams(vmem_limit_bytes=VMEM_LIMIT),
        cost_estimate=pl.CostEstimate(flops=100_000_000, bytes_accessed=300_000, transcendentals=0),
    )(pops, near, up, down, side, reply, slab, rank, vel, fric, pull)


def potential_kernel(
    before_ref,
    own_ref,
    after_ref,
    nbr_ref,
    bond_ref,
    w_self_ref,
    w_nbr_ref,
    w_rbf_ref,
    w_out_ref,
    force_ref,
    new_ref,
    table,
    own_half,
    total,
):
    feats, atoms = own_ref.shape
    near, basis = nbr_ref.shape[0], w_rbf_ref.shape[1]
    block = 256
    for place, ref in enumerate((before_ref, own_ref, after_ref)):
        value = mm(w_nbr_ref[...], ref[...]).astype(BF16)
        table[place * feats : (place + 1) * feats, :] = (value.astype(F32) * 0.5).astype(BF16)
    own_half[...] = 0.5 * mm(w_self_ref[...], own_ref[...])
    total[...] = jnp.zeros_like(total)
    force_ref[...] = jnp.zeros_like(force_ref)
    rbf_hi, rbf_lo = halves(0.5 * w_rbf_ref[...])
    rbf = jnp.concatenate([rbf_hi, rbf_lo, rbf_hi], axis=1)
    spacing = RADIAL_REACH / (basis - 1)
    centers = iota((basis, block), 0).astype(F32) * spacing
    w_out = w_out_ref[...]
    rows = iota((atoms, block), 0)

    def one(k, carry):
        for part in range(atoms // block):
            cols = slice(part * block, (part + 1) * block)
            nbr = nbr_ref[pl.ds(k, 1), cols]
            place = nbr // atoms
            one_hot = jnp.where(rows == nbr % atoms, 1.0, 0.0).astype(BF16)
            seen = mm(table[...], one_hot)
            bond = [bond_ref[c, pl.ds(k, 1), cols] for c in range(3)]
            length = jnp.sqrt(bond[0] * bond[0] + bond[1] * bond[1] + bond[2] * bond[2] + 1e-6)
            scaled = (length - centers) * (1.0 / spacing)
            rad_hi, rad_lo = halves(jnp.exp(-scaled * scaled))
            radial = jnp.concatenate([rad_hi, rad_hi, rad_lo], axis=0)
            picked = jnp.where(
                place == 0, seen[:feats], jnp.where(place == 1, seen[feats : 2 * feats], seen[2 * feats :])
            )
            half = own_half[:, cols] + picked + mm(rbf, radial)
            hidden = half + half * jnp.tanh(half)
            total[:, cols] += hidden
            scalar = jnp.sum(hidden * w_out, axis=0, keepdims=True)
            for c in range(3):
                force_ref[c : c + 1, cols] += scalar * bond[c]
        return carry

    lax.fori_loop(0, near, one, 0)
    new_ref[...] = (own_ref[...].astype(F32) + total[...] * (1.0 / near)).astype(BF16)


def potential(before, own, after, nbrs, bonds, w_self, w_nbr, w_rbf, w_out):
    feats, atoms = own.shape
    return pl.pallas_call(
        potential_kernel,
        out_shape=(
            jax.ShapeDtypeStruct((3, atoms), F32),
            jax.ShapeDtypeStruct((feats, atoms), BF16),
        ),
        scratch_shapes=[
            pltpu.VMEM((3 * feats, atoms), BF16),
            pltpu.VMEM((feats, atoms), F32),
            pltpu.VMEM((feats, atoms), F32),
        ],
        name="potential",
        compiler_params=pltpu.CompilerParams(vmem_limit_bytes=VMEM_LIMIT),
        cost_estimate=pl.CostEstimate(flops=7_000_000_000, bytes_accessed=2_000_000, transcendentals=1_200_000),
    )(before, own, after, nbrs, bonds, w_self, w_nbr, w_rbf, w_out)


def body(
    slabs,
    populations,
    relax_rates,
    slab,
    stencil_base,
    frac,
    atom_vel,
    friction,
    features,
    neighbors,
    bonds,
    w_self,
    w_nbr,
    w_rbf,
    w_out,
):
    _, planes, width, depth = populations.shape
    atoms = slab.shape[0]
    up = [(i, (i + 1) % slabs) for i in range(slabs)]
    down = [(j, i) for i, j in up]
    across = [(0, 1), (1, 0)]
    both = ("fluid", "group")
    up_across = [(2 * i + g, 2 * j + 1 - g) for i, j in up for g in (0, 1)]
    down_across = [(2 * i + g, 2 * j + 1 - g) for i, j in down for g in (0, 1)]
    slab_row = slab.reshape(1, atoms)
    friction_row = friction.reshape(1, atoms)

    before = lax.ppermute(features, "fluid", up)
    after = lax.ppermute(features, "fluid", down)
    outgoing, rank = pack(slab_row, stencil_base.reshape(1, atoms), frac, atom_vel, friction_row, slabs)
    mail = lax.all_to_all(outgoing.reshape(slabs, 1, 128), "fluid", split_axis=0, concat_axis=0, tiled=True)

    vel, axis, calm, rising, falling, side, side_up, side_down = relax(
        relax_rates, populations.reshape(19, planes * width, depth)
    )
    rising = lax.ppermute(rising, "fluid", up)
    falling = lax.ppermute(falling, "fluid", down)
    side = lax.ppermute(side, "group", across)
    side_up = lax.ppermute(side_up, both, up_across)
    side_down = lax.ppermute(side_down, both, down_across)

    pull, new_features = potential(
        before,
        features,
        after,
        neighbors.T,
        bonds.transpose(0, 2, 1),
        w_self,
        w_nbr,
        w_rbf,
        w_out.reshape(-1, 1),
    )

    reply, force = couple(mail.reshape(slabs, 128), vel)
    reply = lax.all_to_all(reply.reshape(slabs, 1, 128), "fluid", split_axis=0, concat_axis=0, tiled=True)
    moved, late_up, late_down, late_side = push(axis, force)
    late_up = lax.ppermute(late_up, "fluid", up)
    late_down = lax.ppermute(late_down, "fluid", down)
    late_side = lax.ppermute(late_side, "group", across)
    pops, near = gather(calm, moved, rising, falling, side, side_up, side_down)
    pops, atom_force = finish(
        pops,
        near,
        late_up,
        late_down,
        late_side,
        reply.reshape(slabs, 128),
        slab_row,
        rank,
        atom_vel,
        friction_row,
        pull,
    )
    return pops.reshape(populations.shape), atom_force, new_features


def solution(mesh):
    in_specs = (
        P(None, "fluid", "group", None),
        P(),
        P(("fluid", "group"), None),
        P(("fluid", "group")),
        P(None, ("fluid", "group")),
        P(None, ("fluid", "group")),
        P(("fluid", "group")),
        P(None, ("fluid", "group")),
        P(("fluid", "group"), None),
        P(None, ("fluid", "group"), None),
        P(),
        P(),
        P(),
        P(),
    )
    out_specs = (
        P(None, "fluid", "group", None),
        P(None, ("fluid", "group")),
        P(None, ("fluid", "group")),
    )
    return jax.shard_map(
        functools.partial(body, mesh.shape["fluid"]),
        mesh=mesh,
        in_specs=in_specs,
        out_specs=out_specs,
        check_vma=False,
    )
```

```python
import functools

import jax
import jax.numpy as jnp
from jax import lax
from jax.experimental import pallas as pl
from jax.experimental.pallas import tpu as pltpu
from jax.sharding import PartitionSpec as P

F32 = jnp.float32
BF16 = jnp.bfloat16
I32 = jnp.int32

RADIAL_REACH = 4.0
SLOTS = 8

SPEEDS = (
    (0, 0, 0),
    (1, 0, 0),
    (-1, 0, 0),
    (0, 1, 0),
    (0, -1, 0),
    (0, 0, 1),
    (0, 0, -1),
    (1, 1, 0),
    (-1, -1, 0),
    (1, -1, 0),
    (-1, 1, 0),
    (1, 0, 1),
    (-1, 0, -1),
    (1, 0, -1),
    (-1, 0, 1),
    (0, 1, 1),
    (0, -1, -1),
    (0, 1, -1),
    (0, -1, 1),
)
RISING = (11, 14, 15, 18)
FALLING = (12, 13, 16, 17)
FLAT = (0, 7, 8, 9, 10)
CALM = (0, 7, 8, 9, 10, 11, 12, 13, 14, 15, 16, 17, 18)

VMEM_LIMIT = 48 * 1024 * 1024


def halves(value):
    high = value.astype(BF16)
    low = (value - high.astype(F32)).astype(BF16)
    return high, low


def thirds(value):
    high = value.astype(BF16)
    rest = value - high.astype(F32)
    middle = rest.astype(BF16)
    low = (rest - middle.astype(F32)).astype(BF16)
    return high, middle, low


def mm(a, b):
    return jnp.dot(a, b, preferred_element_type=F32)


def mm_nt(a, b):
    return lax.dot_general(a, b, (((1,), (1,)), ((), ())), preferred_element_type=F32)


def iota(shape, dim):
    return lax.broadcasted_iota(I32, shape, dim)


def packed(slab, base, frac_ref, vel_ref, fric, slabs):
    atoms = slab.shape[1]
    named = iota((slabs, atoms), 0) == slab
    one_hot = jnp.where(named, 1.0, 0.0)
    one_hot_b = one_hot.astype(BF16)
    earlier = jnp.where(iota((atoms, atoms), 0) < iota((atoms, atoms), 1), 1.0, 0.0).astype(BF16)
    before = mm(one_hot_b, earlier)
    rank = jnp.sum(one_hot * before, axis=0, keepdims=True)
    mine = iota((SLOTS, atoms), 0).astype(F32) == rank
    rows = [frac_ref[c : c + 1, :] for c in range(3)]
    rows += [vel_ref[c : c + 1, :] for c in range(3)]
    rows += [fric, base.astype(F32)]
    spread = [jnp.where(mine, row, 0.0) for row in rows]
    spread.append(jnp.zeros((128 - SLOTS * len(rows), atoms), F32))
    high, middle, low = thirds(jnp.concatenate(spread, axis=0))
    return mm_nt(one_hot_b, high) + (mm_nt(one_hot_b, middle) + mm_nt(one_hot_b, low)), rank


def moments_of(d):
    m = [None] * 19
    quad = {}
    for name, (pp, nn, pn, np_) in dict(xy=(7, 8, 9, 10), xz=(11, 12, 13, 14), yz=(15, 16, 17, 18)).items():
        same, cross = d[pp] + d[nn], d[pn] + d[np_]
        odd_same, odd_cross = d[pp] - d[nn], d[pn] - d[np_]
        quad[name] = (same + cross, same - cross, odd_same + odd_cross, odd_same - odd_cross)
    sxy, m[4], m[10], m[12] = quad["xy"]
    sxz, m[5], m[11], m[13] = quad["xz"]
    syz, m[6], m[15], m[14] = quad["yz"]
    m[16], m[17], m[18] = sxy, sxz, syz
    ax, ay, az = d[1] + d[2], d[3] + d[4], d[5] + d[6]
    m[0] = (d[0] + ax) + (ay + az) + (sxy + (sxz + syz))
    m[1] = (d[1] - d[2]) + (m[10] + m[11])
    m[2] = (d[3] - d[4]) + (m[12] + m[15])
    m[3] = (d[5] - d[6]) + (m[13] + m[14])
    m[7] = ax + (sxy + sxz)
    m[8] = ay + (sxy + syz)
    m[9] = az + (sxz + syz)
    return m


def populations_of(m):
    f = [None] * 19
    for (pp, nn, pn, np_), (s, c, first, second) in (
        ((7, 8, 9, 10), (m[16], m[4], m[10], m[12])),
        ((11, 12, 13, 14), (m[17], m[5], m[11], m[13])),
        ((15, 16, 17, 18), (m[18], m[6], m[15], m[14])),
    ):
        same, cross = 0.25 * (s + c), 0.25 * (s - c)
        odd_same, odd_cross = 0.25 * (first + second), 0.25 * (first - second)
        f[pp], f[nn] = same + odd_same, same - odd_same
        f[pn], f[np_] = cross + odd_cross, cross - odd_cross
    for plus, minus, square, line, squares, lines in (
        (1, 2, m[7], m[1], (m[16], m[17]), (m[10], m[11])),
        (3, 4, m[8], m[2], (m[16], m[18]), (m[12], m[15])),
        (5, 6, m[9], m[3], (m[17], m[18]), (m[13], m[14])),
    ):
        even = 0.5 * (square - (squares[0] + squares[1]))
        odd = 0.5 * (line - (lines[0] + lines[1]))
        f[plus], f[minus] = even + odd, even - odd
    f[0] = m[0] - (m[7] + (m[8] + m[9])) + (m[16] + (m[17] + m[18]))
    return f


def equilibrium_of(density, u):
    ux, uy, uz = u
    rest = 1.0 - 1.5 * (ux * ux + uy * uy + uz * uz)
    eq = [None] * 19
    eq[0] = (1.0 / 3.0) * density * rest
    scale_axis, scale_diagonal = (1.0 / 18.0) * density, (1.0 / 36.0) * density
    for plus, minus, along, scale in (
        (1, 2, ux, scale_axis),
        (3, 4, uy, scale_axis),
        (5, 6, uz, scale_axis),
        (7, 8, ux + uy, scale_diagonal),
        (9, 10, ux - uy, scale_diagonal),
        (11, 12, ux + uz, scale_diagonal),
        (13, 14, ux - uz, scale_diagonal),
        (15, 16, uy + uz, scale_diagonal),
        (17, 18, uy - uz, scale_diagonal),
    ):
        even = rest + 4.5 * along * along
        odd = 3.0 * along
        eq[plus], eq[minus] = scale * (even + odd), scale * (even - odd)
    return eq


def shifted(plane, number):
    cx, cy, _ = SPEEDS[number]
    if cy:
        plane = pltpu.roll(plane, cy % plane.shape[1], 1)
    if cx:
        plane = pltpu.roll(plane, cx % plane.shape[0], 0)
    return plane


def edge(plane, number):
    width = plane.shape[0]
    return plane[0:1] if SPEEDS[number][0] > 0 else plane[width - 1 : width]


def even_device():
    return lax.axis_index("fluid") % 2 == 0


def begin_kernel(
    rates_ref,
    pops_hbm,
    slab_hbm,
    base_hbm,
    frac_hbm,
    atom_vel_hbm,
    fric_hbm,
    feat_hbm,
    mail_ref,
    rank_ref,
    vel_ref,
    axis_ref,
    calm_ref,
    near_ref,
    far_ref,
    side_ref,
    pops_ref,
    post_ref,
    slab_ref,
    base_ref,
    frac_ref,
    atom_vel_ref,
    fric_ref,
    sems,
):
    cells = pops_ref.shape[1]
    width = cells // 2
    feats = feat_hbm.shape[0]
    pairs = (
        (slab_hbm, slab_ref),
        (base_hbm, base_ref),
        (frac_hbm, frac_ref),
        (atom_vel_hbm, atom_vel_ref),
        (fric_hbm, fric_ref),
        (pops_hbm, pops_ref),
        (feat_hbm, near_ref.at[pl.ds(0, feats), :]),
        (feat_hbm, far_ref.at[pl.ds(0, feats), :]),
    )
    copies = [pltpu.make_async_copy(src, dst, sems.at[at]) for at, (src, dst) in enumerate(pairs)]
    for copy in copies:
        copy.start()
    for copy in copies[:5]:
        copy.wait()
    mail, rank = packed(slab_ref[...], base_ref[...], frac_ref, atom_vel_ref, fric_ref[...], mail_ref.shape[0])
    mail_ref[...] = mail
    rank_ref[...] = rank
    copies[5].wait()

    def chunk(step, carry):
        rows = pl.ds(pl.multiple_of(step * 8, 8), 8)
        f = [pops_ref[i, rows, :] for i in range(19)]
        low = moments_of(f)
        density = low[0]
        inverse = 1.0 / density
        u = [low[c] * inverse for c in (1, 2, 3)]
        for c in range(3):
            vel_ref[c, rows, :] = u[c]
        eq = equilibrium_of(density, u)
        m = moments_of([f[i] - eq[i] for i in range(19)])
        relaxed = populations_of([rates_ref[i] * m[i] for i in range(19)])
        for i in range(19):
            post_ref[i, rows, :] = f[i] - relaxed[i]
        return carry

    lax.fori_loop(0, cells // 8, chunk, 0)

    def plane(number, z):
        return shifted(post_ref[number, z * width : (z + 1) * width, :], number)

    axis_ref[...] = post_ref[1:7]
    edges = []
    for place, number in enumerate(CALM):
        if number in FLAT:
            for z in (0, 1):
                value = plane(number, z)
                calm_ref[place, z * width : (z + 1) * width, :] = value
                if number:
                    edges.append(edge(value, number))
    lanes = pops_ref.shape[2]
    leaving = []
    for numbers, stays in ((RISING, 1), (FALLING, 0)):
        leaving.append([])
        for number in numbers:
            value = plane(number, 1 - stays)
            calm_ref[CALM.index(number), stays * width : (stays + 1) * width, :] = value
            leaving[-1].append(plane(number, stays))
            if SPEEDS[number][0]:
                edges.append(edge(value, number))
    even = even_device()
    for place, (rises, falls) in enumerate(zip(*leaving)):
        cols = slice(place * lanes, (place + 1) * lanes)
        near_ref[feats : feats + width, cols] = jnp.where(even, rises, falls).astype(BF16)
        far_ref[feats : feats + width, cols] = jnp.where(even, falls, rises).astype(BF16)
    side_ref[...] = jnp.concatenate(edges + [jnp.zeros((16 - len(edges), lanes), F32)], axis=0)
    for copy in copies[6:]:
        copy.wait()


def begin(rates, pops, slab, base, frac, atom_vel, fric, feat, slabs):
    _, cells, lanes = pops.shape
    width = cells // 2
    feats, atoms = feat.shape
    vmem = pl.BlockSpec(memory_space=pltpu.VMEM)
    outside = [pltpu.with_memory_space_constraint(x, pltpu.HBM) for x in (pops, slab, base, frac, atom_vel, fric, feat)]
    return pl.pallas_call(
        begin_kernel,
        in_specs=[pl.BlockSpec(memory_space=pltpu.SMEM)] + [pl.BlockSpec(memory_space=pltpu.HBM)] * 7,
        out_specs=[vmem] * 8,
        out_shape=(
            jax.ShapeDtypeStruct((slabs, 128), F32),
            jax.ShapeDtypeStruct((1, atoms), F32),
            jax.ShapeDtypeStruct((3, cells, lanes), F32),
            jax.ShapeDtypeStruct((6, cells, lanes), F32),
            jax.ShapeDtypeStruct((13, cells, lanes), F32),
            jax.ShapeDtypeStruct((feats + width, 4 * lanes), BF16),
            jax.ShapeDtypeStruct((feats + width, 4 * lanes), BF16),
            jax.ShapeDtypeStruct((16, lanes), F32),
        ),
        scratch_shapes=[
            pltpu.VMEM((19, cells, lanes), F32),
            pltpu.VMEM((19, cells, lanes), F32),
            pltpu.VMEM((1, atoms), I32),
            pltpu.VMEM((1, atoms), I32),
            pltpu.VMEM((3, atoms), F32),
            pltpu.VMEM((3, atoms), F32),
            pltpu.VMEM((1, atoms), F32),
            pltpu.SemaphoreType.DMA((8,)),
        ],
        name="begin",
        compiler_params=pltpu.CompilerParams(vmem_limit_bytes=VMEM_LIMIT),
        cost_estimate=pl.CostEstimate(flops=400_000_000, bytes_accessed=6_000_000, transcendentals=0),
    )(rates, *outside)


def look_kernel(mail_ref, vel_ref, reply_ref, slot_ref, wy_hi, wy_lo):
    comps, cells, depth = vel_ref.shape
    width = cells // 2
    slots = mail_ref.shape[0]
    t = mail_ref[...].T
    field = lambda v: t[v * SLOTS : (v + 1) * SLOTS, :]
    fx, fy, fz = field(0), field(1), field(2)
    atom_vel = [field(3), field(4), field(5)]
    friction = field(6)
    base = field(7).astype(I32)
    x0 = (base // depth) % width
    y0 = base % depth
    y1 = (y0 + 1) % depth
    gx, gy, gz = 1.0 - fx, 1.0 - fy, 1.0 - fz
    row_y = iota((depth, slots), 0)
    row_x = iota((width, slots), 0)

    v_hi, v_lo = halves(vel_ref[...].reshape(comps * cells, depth))
    values = [[], [], []]
    for r in range(SLOTS):
        one = slice(r, r + 1)
        cols = slice(r * slots, (r + 1) * slots)
        wy = jnp.where(row_y == y0[one], gy[one], 0.0) + jnp.where(row_y == y1[one], fy[one], 0.0)
        wx = jnp.where(row_x == x0[one], gx[one], 0.0) + jnp.where(row_x == x0[one] + 1, fx[one], 0.0)
        hi, lo = halves(wy)
        wy_hi[:, cols] = hi
        wy_lo[:, cols] = lo
        seen = mm(v_hi, hi) + (mm(v_lo, hi) + mm(v_hi, lo))
        for c in range(3):
            close = seen[c * cells : c * cells + width]
            beyond = seen[c * cells + width : (c + 1) * cells]
            values[c].append(jnp.sum(wx * (close * gz[one] + beyond * fz[one]), axis=0, keepdims=True))
    rows = jnp.concatenate([row for c in range(3) for row in values[c]], axis=0)
    reply_ref[...] = jnp.concatenate([rows, jnp.zeros((128 - 3 * SLOTS, slots), F32)], axis=0).T
    slot_ref[0:SLOTS, :] = x0.astype(F32)
    slot_ref[SLOTS : 2 * SLOTS, :] = fx
    slot_ref[2 * SLOTS : 3 * SLOTS, :] = fz
    for c in range(3):
        pull = friction * (atom_vel[c] - rows[c * SLOTS : (c + 1) * SLOTS])
        slot_ref[(3 + c) * SLOTS : (4 + c) * SLOTS, :] = pull


def look(mail, vel):
    _, _, depth = vel.shape
    slabs = mail.shape[0]
    return pl.pallas_call(
        look_kernel,
        out_shape=(
            jax.ShapeDtypeStruct((slabs, 128), F32),
            jax.ShapeDtypeStruct((6 * SLOTS, slabs), F32),
            jax.ShapeDtypeStruct((depth, SLOTS * slabs), BF16),
            jax.ShapeDtypeStruct((depth, SLOTS * slabs), BF16),
        ),
        name="look",
        compiler_params=pltpu.CompilerParams(vmem_limit_bytes=VMEM_LIMIT),
        cost_estimate=pl.CostEstimate(flops=500_000_000, bytes_accessed=1_000_000, transcendentals=0),
    )(mail, vel)


def halos(near_ref, far_ref, width):
    lanes = near_ref.shape[1] // 4
    even = even_device()
    below, above = [], []
    for place in range(4):
        cols = slice(place * lanes, (place + 1) * lanes)
        near = near_ref[near_ref.shape[0] - width :, cols].astype(F32)
        far = far_ref[far_ref.shape[0] - width :, cols].astype(F32)
        below.append(jnp.where(even, far, near))
        above.append(jnp.where(even, near, far))
    return below, above


def push_kernel(
    axis_ref,
    slot_ref,
    wy_hi,
    wy_lo,
    early_ref,
    near_ref,
    far_ref,
    moved_ref,
    late_near_ref,
    late_far_ref,
    side_ref,
    force_ref,
    a_hi,
    a_lo,
):
    cells = axis_ref.shape[1]
    width = cells // 2
    slots = slot_ref.shape[1]
    row_x = iota((width, slots), 0)
    for r in range(SLOTS):
        cols = slice(r * slots, (r + 1) * slots)
        row = lambda v: slot_ref[v * SLOTS + r : v * SLOTS + r + 1, :]
        x0, fx, fz = row(0).astype(I32), row(1), row(2)
        wx = jnp.where(row_x == x0, 1.0 - fx, 0.0) + jnp.where(row_x == x0 + 1, fx, 0.0)
        for c in range(3):
            for z, weight in ((0, 1.0 - fz), (1, fz)):
                hi, lo = halves(wx * (weight * row(3 + c)))
                start = c * cells + z * width
                a_hi[start : start + width, cols] = hi
                a_lo[start : start + width, cols] = lo
    for c in (2, 0, 1):
        rows = slice(c * cells, (c + 1) * cells)
        force_ref[c] = mm_nt(a_hi[rows], wy_hi[...]) + (mm_nt(a_lo[rows], wy_hi[...]) + mm_nt(a_hi[rows], wy_lo[...]))
    edges = []
    for number in (5, 6, 1, 2, 3, 4):
        place = number - 1
        sign = 0.5 if number % 2 else -0.5
        for z in (0, 1):
            rows = slice(z * width, (z + 1) * width)
            value = shifted(axis_ref[place, rows, :] + sign * force_ref[place // 2, rows, :], number)
            if number == 5:
                if z == 1:
                    rises = value
                moved_ref[place, (1 - z) * width : (2 - z) * width, :] = value
            elif number == 6:
                if z == 0:
                    falls = value
                moved_ref[place, (1 - z) * width : (2 - z) * width, :] = value
            else:
                moved_ref[place, rows, :] = value
                if number in (1, 2):
                    edges.append(edge(value, number))
    even = even_device()
    late_near_ref[...] = jnp.where(even, rises, falls)
    late_far_ref[...] = jnp.where(even, falls, rises)
    for planes, numbers in zip(halos(near_ref, far_ref, width), (RISING, FALLING)):
        for plane, number in zip(planes, numbers):
            if SPEEDS[number][0]:
                edges.append(edge(plane, number))
    side_ref[0:16, :] = early_ref[...]
    side_ref[16:24, :] = jnp.concatenate(edges, axis=0)


def push(axis, slot, wy_hi, wy_lo, early, near, far):
    _, cells, lanes = axis.shape
    slots = wy_hi.shape[1]
    width = cells // 2
    return pl.pallas_call(
        push_kernel,
        out_shape=(
            jax.ShapeDtypeStruct((6, cells, lanes), F32),
            jax.ShapeDtypeStruct((width, lanes), F32),
            jax.ShapeDtypeStruct((width, lanes), F32),
            jax.ShapeDtypeStruct((24, lanes), F32),
        ),
        scratch_shapes=[
            pltpu.VMEM((3, cells, lanes), F32),
            pltpu.VMEM((3 * cells, slots), BF16),
            pltpu.VMEM((3 * cells, slots), BF16),
        ],
        name="push",
        compiler_params=pltpu.CompilerParams(vmem_limit_bytes=VMEM_LIMIT),
        cost_estimate=pl.CostEstimate(flops=500_000_000, bytes_accessed=1_500_000, transcendentals=0),
    )(axis, slot, wy_hi, wy_lo, early, near, far)


def gather_kernel(calm_ref, moved_ref, near_ref, far_ref, side_ref, late_near_ref, late_far_ref, out_ref):
    cells = calm_ref.shape[1]
    width = cells // 2

    def put(number, z, at):
        row = z * width + (0 if SPEEDS[number][0] > 0 else width - 1)
        out_ref[number, row : row + 1, :] = side_ref[at : at + 1, :]

    for place, number in enumerate(CALM):
        if number in FLAT:
            out_ref[number] = calm_ref[place]
    for place in range(4):
        out_ref[place + 1] = moved_ref[place]
    even = even_device()
    out_ref[5, width:, :] = moved_ref[4, width:, :]
    out_ref[5, :width, :] = jnp.where(even, late_far_ref[...], late_near_ref[...])
    out_ref[6, :width, :] = moved_ref[5, :width, :]
    out_ref[6, width:, :] = jnp.where(even, late_near_ref[...], late_far_ref[...])
    at, corner = 0, 20
    for number in FLAT[1:]:
        for z in (0, 1):
            put(number, z, at)
            at += 1
    below, above = halos(near_ref, far_ref, width)
    for arrived, numbers, stays in ((below, RISING, 1), (above, FALLING, 0)):
        for place, number in enumerate(numbers):
            kept, new = stays * width, (1 - stays) * width
            out_ref[number, kept : kept + width, :] = calm_ref[CALM.index(number), kept : kept + width, :]
            out_ref[number, new : new + width, :] = arrived[place]
            if SPEEDS[number][0]:
                put(number, stays, at)
                put(number, 1 - stays, corner)
                at += 1
                corner += 1
    for number in (1, 2):
        for z in (0, 1):
            put(number, z, 16 + 2 * (number - 1) + z)


def gather(calm, moved, near, far, side, late_near, late_far):
    _, cells, lanes = calm.shape
    return pl.pallas_call(
        gather_kernel,
        out_shape=jax.ShapeDtypeStruct((19, cells, lanes), F32),
        name="gather",
        compiler_params=pltpu.CompilerParams(vmem_limit_bytes=VMEM_LIMIT),
        cost_estimate=pl.CostEstimate(flops=1_000, bytes_accessed=3_000_000, transcendentals=0),
    )(calm, moved, near, far, side, late_near, late_far)


def finish_kernel(reply_ref, slab_ref, rank_ref, vel_ref, fric_ref, pull_ref, force_ref):
    slabs, atoms = reply_ref.shape[0], slab_ref.shape[1]
    one_hot = jnp.where(iota((slabs, atoms), 0) == slab_ref[...], 1.0, 0.0).astype(BF16)
    high, low = halves(reply_ref[...].T[: 3 * SLOTS])
    picked = mm(high, one_hot) + mm(low, one_hot)
    mine = iota((SLOTS, atoms), 0).astype(F32) == rank_ref[...]
    for c in range(3):
        seen = jnp.sum(jnp.where(mine, picked[c * SLOTS : (c + 1) * SLOTS], 0.0), axis=0, keepdims=True)
        drag = fric_ref[...] * (seen - vel_ref[c : c + 1, :])
        force_ref[c : c + 1, :] = pull_ref[c : c + 1, :] + drag


def finish(reply, slab, rank, vel, fric, pull):
    atoms = slab.shape[1]
    return pl.pallas_call(
        finish_kernel,
        out_shape=jax.ShapeDtypeStruct((3, atoms), F32),
        name="finish",
        compiler_params=pltpu.CompilerParams(vmem_limit_bytes=VMEM_LIMIT),
        cost_estimate=pl.CostEstimate(flops=20_000_000, bytes_accessed=100_000, transcendentals=0),
    )(reply, slab, rank, vel, fric, pull)


def potential_kernel(
    near_ref,
    own_ref,
    far_ref,
    nbr_ref,
    bond_ref,
    w_self_ref,
    w_nbr_ref,
    w_rbf_ref,
    w_out_ref,
    force_ref,
    new_ref,
    table,
    own_half,
):
    feats, atoms = own_ref.shape
    count, basis = nbr_ref.shape[0], w_rbf_ref.shape[1]
    block = 256
    above = jnp.where(even_device(), 2 * feats, 0)
    for start, ref in ((above, near_ref), (feats, own_ref), (2 * feats - above, far_ref)):
        value = mm(w_nbr_ref[...], ref[0:feats, :]).astype(BF16)
        rows = pl.ds(start if isinstance(start, int) else pl.multiple_of(start, feats), feats)
        table[rows, :] = (value.astype(F32) * 0.5).astype(BF16)
    own_half[...] = 0.5 * mm(w_self_ref[...], own_ref[...])
    rbf_hi, rbf_lo = halves(0.5 * w_rbf_ref[...])
    rbf = jnp.concatenate([rbf_hi, rbf_lo, rbf_hi], axis=1)
    spacing = RADIAL_REACH / (basis - 1)
    centers = iota((basis, block), 0).astype(F32) * spacing
    w_out = w_out_ref[...]
    rows = iota((atoms, block), 0)

    def one(part, carry):
        cols = pl.ds(pl.multiple_of(part * block, block), block)
        total, force = None, None
        for k in range(count):
            nbr = nbr_ref[k : k + 1, cols]
            place = nbr // atoms
            one_hot = jnp.where(rows == nbr % atoms, 1.0, 0.0).astype(BF16)
            bond = [bond_ref[c, k : k + 1, cols] for c in range(3)]
            length = jnp.sqrt(bond[0] * bond[0] + bond[1] * bond[1] + bond[2] * bond[2] + 1e-6)
            scaled = (length - centers) * (1.0 / spacing)
            rad_hi, rad_lo = halves(jnp.exp(-scaled * scaled))
            radial = jnp.concatenate([rad_hi, rad_hi, rad_lo], axis=0)
            seen = mm(table[...], one_hot)
            picked = jnp.where(
                place == 0, seen[:feats], jnp.where(place == 1, seen[feats : 2 * feats], seen[2 * feats :])
            )
            half = own_half[:, cols] + picked + mm(rbf, radial)
            hidden = half + half * jnp.tanh(half)
            scalar = jnp.sum(hidden * w_out, axis=0, keepdims=True)
            terms = [scalar * b for b in bond]
            total = hidden if total is None else total + hidden
            force = terms if force is None else [f + t for f, t in zip(force, terms)]
        for c in range(3):
            force_ref[c : c + 1, cols] = force[c]
        new_ref[:, cols] = (own_ref[:, cols].astype(F32) + total * (1.0 / count)).astype(BF16)
        return carry

    lax.fori_loop(0, atoms // block, one, 0)


def potential(near, own, far, nbrs, bonds, w_self, w_nbr, w_rbf, w_out):
    feats, atoms = own.shape
    return pl.pallas_call(
        potential_kernel,
        out_shape=(
            jax.ShapeDtypeStruct((3, atoms), F32),
            jax.ShapeDtypeStruct((feats, atoms), BF16),
        ),
        scratch_shapes=[
            pltpu.VMEM((3 * feats, atoms), BF16),
            pltpu.VMEM((feats, atoms), F32),
        ],
        name="potential",
        compiler_params=pltpu.CompilerParams(vmem_limit_bytes=VMEM_LIMIT),
        cost_estimate=pl.CostEstimate(flops=1_000_000, bytes_accessed=100_000, transcendentals=0),
    )(near, own, far, nbrs, bonds, w_self, w_nbr, w_rbf, w_out)


def body(
    slabs,
    populations,
    relax_rates,
    slab,
    stencil_base,
    frac,
    atom_vel,
    friction,
    features,
    neighbors,
    bonds,
    w_self,
    w_nbr,
    w_rbf,
    w_out,
):
    _, planes, width, depth = populations.shape
    atoms = slab.shape[0]
    chip = [(i, i ^ 1) for i in range(slabs)]
    link = [(i, (i - 1 if i % 2 == 0 else i + 1) % slabs) for i in range(slabs)]
    across = [(0, 1), (1, 0)]
    slab_row = slab.reshape(1, atoms)
    friction_row = friction.reshape(1, atoms)

    mail, rank, vel, axis, calm, near, far, side = begin(
        relax_rates,
        populations.reshape(19, planes * width, depth),
        slab_row,
        stencil_base.reshape(1, atoms),
        frac,
        atom_vel,
        friction_row,
        features,
        slabs,
    )
    mail = lax.all_to_all(mail.reshape(slabs, 1, 128), "fluid", split_axis=0, concat_axis=0, tiled=True)
    far = lax.ppermute(far, "fluid", link)
    near = lax.ppermute(near, "fluid", chip)
    pull, new_features = potential(
        near,
        features,
        far,
        neighbors.T,
        bonds.transpose(0, 2, 1),
        w_self,
        w_nbr,
        w_rbf,
        w_out.reshape(-1, 1),
    )
    mail, pull = lax.optimization_barrier((mail, pull))

    reply, slot, wy_hi, wy_lo = look(mail.reshape(slabs, 128), vel)
    reply = lax.all_to_all(reply.reshape(slabs, 1, 128), "fluid", split_axis=0, concat_axis=0, tiled=True)
    moved, late_near, late_far, side = push(axis, slot, wy_hi, wy_lo, side, near, far)
    side = lax.ppermute(side, "group", across)
    late_far = lax.ppermute(late_far, "fluid", link)
    late_near = lax.ppermute(late_near, "fluid", chip)
    pops = gather(calm, moved, near, far, side, late_near, late_far)
    atom_force = finish(reply.reshape(slabs, 128), slab_row, rank, atom_vel, friction_row, pull)
    return pops.reshape(populations.shape), atom_force, new_features


def solution(mesh):
    in_specs = (
        P(None, "fluid", "group", None),
        P(),
        P(("fluid", "group"), None),
        P(("fluid", "group")),
        P(None, ("fluid", "group")),
        P(None, ("fluid", "group")),
        P(("fluid", "group")),
        P(None, ("fluid", "group")),
        P(("fluid", "group"), None),
        P(None, ("fluid", "group"), None),
        P(),
        P(),
        P(),
        P(),
    )
    out_specs = (
        P(None, "fluid", "group", None),
        P(None, ("fluid", "group")),
        P(None, ("fluid", "group")),
    )
    return jax.shard_map(
        functools.partial(body, mesh.shape["fluid"]),
        mesh=mesh,
        in_specs=in_specs,
        out_specs=out_specs,
        check_vma=False,
    )
```

```python
import functools

import jax
import jax.numpy as jnp
from jax import lax
from jax.experimental import pallas as pl
from jax.experimental.pallas import tpu as pltpu
from jax.sharding import PartitionSpec as P

F32 = jnp.float32
BF16 = jnp.bfloat16
I32 = jnp.int32

RADIAL_REACH = 4.0
SLOTS = 8

SPEEDS = (
    (0, 0, 0),
    (1, 0, 0),
    (-1, 0, 0),
    (0, 1, 0),
    (0, -1, 0),
    (0, 0, 1),
    (0, 0, -1),
    (1, 1, 0),
    (-1, -1, 0),
    (1, -1, 0),
    (-1, 1, 0),
    (1, 0, 1),
    (-1, 0, -1),
    (1, 0, -1),
    (-1, 0, 1),
    (0, 1, 1),
    (0, -1, -1),
    (0, 1, -1),
    (0, -1, 1),
)
RISING = (11, 14, 15, 18)
FALLING = (12, 13, 16, 17)
FLAT = (0, 7, 8, 9, 10)
CALM = (0, 7, 8, 9, 10, 11, 12, 13, 14, 15, 16, 17, 18)

VMEM_LIMIT = 48 * 1024 * 1024
STREAM_FLOPS = 4_000_000_000
FIRST_FLOPS = 3_500_000_000
SECOND_FLOPS = 500_000_000


def halves(value):
    high = value.astype(BF16)
    low = (value - high.astype(F32)).astype(BF16)
    return high, low


def thirds(value):
    high = value.astype(BF16)
    rest = value - high.astype(F32)
    middle = rest.astype(BF16)
    low = (rest - middle.astype(F32)).astype(BF16)
    return high, middle, low


def mm(a, b):
    return jnp.dot(a, b, preferred_element_type=F32)


def mm_nt(a, b):
    return lax.dot_general(a, b, (((1,), (1,)), ((), ())), preferred_element_type=F32)


def iota(shape, dim):
    return lax.broadcasted_iota(I32, shape, dim)


def packed(slab, base, frac_ref, vel_ref, fric, slabs, earlier):
    atoms = slab.shape[1]
    named = iota((slabs, atoms), 0) == slab
    one_hot = jnp.where(named, 1.0, 0.0)
    one_hot_b = one_hot.astype(BF16)
    before = mm(one_hot_b, earlier)
    rank = jnp.sum(one_hot * before, axis=0, keepdims=True)
    mine = iota((SLOTS, atoms), 0).astype(F32) == rank
    rows = [frac_ref[c : c + 1, :] for c in range(3)]
    rows += [vel_ref[c : c + 1, :] for c in range(3)]
    rows += [fric, base.astype(F32)]
    spread = [jnp.where(mine, row, 0.0) for row in rows]
    high, middle, low = thirds(jnp.concatenate(spread, axis=0))
    return mm_nt(one_hot_b, high) + (mm_nt(one_hot_b, middle) + mm_nt(one_hot_b, low)), rank


def moments_of(d):
    m = [None] * 19
    quad = {}
    for name, (pp, nn, pn, np_) in dict(xy=(7, 8, 9, 10), xz=(11, 12, 13, 14), yz=(15, 16, 17, 18)).items():
        same, cross = d[pp] + d[nn], d[pn] + d[np_]
        odd_same, odd_cross = d[pp] - d[nn], d[pn] - d[np_]
        quad[name] = (same + cross, same - cross, odd_same + odd_cross, odd_same - odd_cross)
    sxy, m[4], m[10], m[12] = quad["xy"]
    sxz, m[5], m[11], m[13] = quad["xz"]
    syz, m[6], m[15], m[14] = quad["yz"]
    m[16], m[17], m[18] = sxy, sxz, syz
    ax, ay, az = d[1] + d[2], d[3] + d[4], d[5] + d[6]
    m[0] = (d[0] + ax) + (ay + az) + (sxy + (sxz + syz))
    m[1] = (d[1] - d[2]) + (m[10] + m[11])
    m[2] = (d[3] - d[4]) + (m[12] + m[15])
    m[3] = (d[5] - d[6]) + (m[13] + m[14])
    m[7] = ax + (sxy + sxz)
    m[8] = ay + (sxy + syz)
    m[9] = az + (sxz + syz)
    return m


def populations_of(m):
    f = [None] * 19
    for (pp, nn, pn, np_), (s, c, first, second) in (
        ((7, 8, 9, 10), (m[16], m[4], m[10], m[12])),
        ((11, 12, 13, 14), (m[17], m[5], m[11], m[13])),
        ((15, 16, 17, 18), (m[18], m[6], m[15], m[14])),
    ):
        same, cross = 0.25 * (s + c), 0.25 * (s - c)
        odd_same, odd_cross = 0.25 * (first + second), 0.25 * (first - second)
        f[pp], f[nn] = same + odd_same, same - odd_same
        f[pn], f[np_] = cross + odd_cross, cross - odd_cross
    for plus, minus, square, line, squares, lines in (
        (1, 2, m[7], m[1], (m[16], m[17]), (m[10], m[11])),
        (3, 4, m[8], m[2], (m[16], m[18]), (m[12], m[15])),
        (5, 6, m[9], m[3], (m[17], m[18]), (m[13], m[14])),
    ):
        even = 0.5 * (square - (squares[0] + squares[1]))
        odd = 0.5 * (line - (lines[0] + lines[1]))
        f[plus], f[minus] = even + odd, even - odd
    f[0] = m[0] - (m[7] + (m[8] + m[9])) + (m[16] + (m[17] + m[18]))
    return f


def equilibrium_of(density, u):
    ux, uy, uz = u
    rest = 1.0 - 1.5 * (ux * ux + uy * uy + uz * uz)
    eq = [None] * 19
    eq[0] = (1.0 / 3.0) * density * rest
    scale_axis, scale_diagonal = (1.0 / 18.0) * density, (1.0 / 36.0) * density
    for plus, minus, along, scale in (
        (1, 2, ux, scale_axis),
        (3, 4, uy, scale_axis),
        (5, 6, uz, scale_axis),
        (7, 8, ux + uy, scale_diagonal),
        (9, 10, ux - uy, scale_diagonal),
        (11, 12, ux + uz, scale_diagonal),
        (13, 14, ux - uz, scale_diagonal),
        (15, 16, uy + uz, scale_diagonal),
        (17, 18, uy - uz, scale_diagonal),
    ):
        even = rest + 4.5 * along * along
        odd = 3.0 * along
        eq[plus], eq[minus] = scale * (even + odd), scale * (even - odd)
    return eq


def shifted(plane, number):
    cx, cy, _ = SPEEDS[number]
    if cy:
        plane = pltpu.roll(plane, cy % plane.shape[1], 1)
    if cx:
        plane = pltpu.roll(plane, cx % plane.shape[0], 0)
    return plane


def edge(plane, number):
    width = plane.shape[0]
    return plane[0:1] if SPEEDS[number][0] > 0 else plane[width - 1 : width]


def pack_kernel(
    slab_hbm, base_hbm, frac_hbm, vel_hbm, fric_hbm, mail_ref, rank_ref, slab_ref, base_ref, frac_ref, vel_ref, fric_ref, sems
):
    pairs = (
        (slab_hbm, slab_ref),
        (base_hbm, base_ref),
        (frac_hbm, frac_ref),
        (vel_hbm, vel_ref),
        (fric_hbm, fric_ref),
    )
    copies = [pltpu.make_async_copy(src, dst, sems.at[at]) for at, (src, dst) in enumerate(pairs)]
    for copy in copies:
        copy.start()
    atoms = slab_ref.shape[1]
    earlier = jnp.where(iota((atoms, atoms), 0) < iota((atoms, atoms), 1), 1.0, 0.0).astype(BF16)
    for copy in copies:
        copy.wait()
    mail, rank = packed(
        slab_ref[...], base_ref[...], frac_ref, vel_ref, fric_ref[...], mail_ref.shape[0], earlier
    )
    filled = mail.shape[1]
    mail_ref[:, :filled] = mail
    mail_ref[:, filled:] = jnp.zeros((mail.shape[0], mail_ref.shape[1] - filled), F32)
    rank_ref[...] = rank


def pack(slab, base, frac, vel, fric, slabs):
    atoms = slab.shape[1]
    vmem = pl.BlockSpec(memory_space=pltpu.VMEM)
    outside = [pltpu.with_memory_space_constraint(x, pltpu.HBM) for x in (slab, base, frac, vel, fric)]
    return pl.pallas_call(
        pack_kernel,
        in_specs=[pl.BlockSpec(memory_space=pltpu.HBM)] * 5,
        out_specs=[vmem] * 2,
        out_shape=(
            jax.ShapeDtypeStruct((slabs, 128), F32),
            jax.ShapeDtypeStruct((1, atoms), F32),
        ),
        scratch_shapes=[
            pltpu.VMEM((1, atoms), I32),
            pltpu.VMEM((1, atoms), I32),
            pltpu.VMEM((3, atoms), F32),
            pltpu.VMEM((3, atoms), F32),
            pltpu.VMEM((1, atoms), F32),
            pltpu.SemaphoreType.DMA((5,)),
        ],
        name="pack",
        compiler_params=pltpu.CompilerParams(vmem_limit_bytes=VMEM_LIMIT),
        cost_estimate=pl.CostEstimate(flops=400_000_000, bytes_accessed=4_000_000, transcendentals=0),
    )(*outside)


def even_device():
    return lax.axis_index("fluid") % 2 == 0


def relax_kernel(rates_ref, pops_ref, rest_ref, axis_ref, vel_ref, near_ref, far_ref):
    cells = pops_ref.shape[1]
    width = cells // 2

    def chunk(step, carry):
        rows = pl.ds(pl.multiple_of(step * 8, 8), 8)
        f = [pops_ref[i, rows, :] for i in range(19)]
        low = moments_of(f)
        density = low[0]
        inverse = 1.0 / density
        u = [low[c] * inverse for c in (1, 2, 3)]
        for c in range(3):
            vel_ref[c, rows, :] = u[c]
        eq = equilibrium_of(density, u)
        m = moments_of([f[i] - eq[i] for i in range(19)])
        relaxed = populations_of([rates_ref[i] * m[i] for i in range(19)])
        for i in range(19):
            if i in CALM:
                rest_ref[CALM.index(i), rows, :] = f[i] - relaxed[i]
            else:
                axis_ref[i - 1, rows, :] = f[i] - relaxed[i]
        return carry

    lax.fori_loop(0, cells // 8, chunk, 0)

    lanes = pops_ref.shape[2]
    even = even_device()
    for place, (rising, falling) in enumerate(zip(RISING, FALLING)):
        cols = slice(place * lanes, (place + 1) * lanes)
        rises = shifted(rest_ref[CALM.index(rising), width:, :], rising)
        falls = shifted(rest_ref[CALM.index(falling), :width, :], falling)
        near_ref[:, cols] = jnp.where(even, rises, falls).astype(BF16)
        far_ref[:, cols] = jnp.where(even, falls, rises).astype(BF16)


def stream_kernel(rest_ref, calm_ref, side_ref):
    cells, lanes = rest_ref.shape[1:]
    width = cells // 2

    def plane(number, z):
        return shifted(rest_ref[CALM.index(number), z * width : (z + 1) * width, :], number)

    edges = []
    for place, number in enumerate(CALM):
        if number in FLAT:
            for z in (0, 1):
                value = plane(number, z)
                calm_ref[place, z * width : (z + 1) * width, :] = value
                if number:
                    edges.append(edge(value, number))
    for numbers, stays in ((RISING, 1), (FALLING, 0)):
        for number in numbers:
            value = plane(number, 1 - stays)
            calm_ref[CALM.index(number), stays * width : (stays + 1) * width, :] = value
            if SPEEDS[number][0]:
                edges.append(edge(value, number))
    side_ref[...] = jnp.concatenate(edges + [jnp.zeros((16 - len(edges), lanes), F32)], axis=0)


def stream(rest):
    _, cells, lanes = rest.shape
    return pl.pallas_call(
        stream_kernel,
        out_shape=(
            jax.ShapeDtypeStruct((13, cells, lanes), F32),
            jax.ShapeDtypeStruct((16, lanes), F32),
        ),
        name="stream",
        compiler_params=pltpu.CompilerParams(vmem_limit_bytes=VMEM_LIMIT),
        cost_estimate=pl.CostEstimate(flops=STREAM_FLOPS, bytes_accessed=100_000, transcendentals=0),
    )(rest)


def relax(rates, pops):
    _, cells, lanes = pops.shape
    width = cells // 2
    vmem = pl.BlockSpec(memory_space=pltpu.VMEM)
    return pl.pallas_call(
        relax_kernel,
        in_specs=[pl.BlockSpec(memory_space=pltpu.SMEM), vmem],
        out_specs=[vmem] * 5,
        out_shape=(
            jax.ShapeDtypeStruct((13, cells, lanes), F32),
            jax.ShapeDtypeStruct((6, cells, lanes), F32),
            jax.ShapeDtypeStruct((3, cells, lanes), F32),
            jax.ShapeDtypeStruct((width, 4 * lanes), BF16),
            jax.ShapeDtypeStruct((width, 4 * lanes), BF16),
        ),
        name="relax",
        compiler_params=pltpu.CompilerParams(vmem_limit_bytes=VMEM_LIMIT),
        cost_estimate=pl.CostEstimate(flops=10_000_000, bytes_accessed=6_000_000, transcendentals=0),
    )(rates, pops)


def look_kernel(mail_ref, vel_ref, reply_ref, slot_ref, wy_hi, wy_lo):
    comps, cells, depth = vel_ref.shape
    width = cells // 2
    slots = mail_ref.shape[0]
    t = mail_ref[...].T
    field = lambda v: t[v * SLOTS : (v + 1) * SLOTS, :]
    fx, fy, fz = field(0), field(1), field(2)
    atom_vel = [field(3), field(4), field(5)]
    friction = field(6)
    base = field(7).astype(I32)
    x0 = (base // depth) % width
    y0 = base % depth
    y1 = (y0 + 1) % depth
    gx, gy, gz = 1.0 - fx, 1.0 - fy, 1.0 - fz
    row_y = iota((depth, slots), 0)
    row_x = iota((width, slots), 0)

    v_hi, v_lo = halves(vel_ref[...].reshape(comps * cells, depth))
    values = [[], [], []]
    for r in range(SLOTS):
        one = slice(r, r + 1)
        cols = slice(r * slots, (r + 1) * slots)
        wy = jnp.where(row_y == y0[one], gy[one], 0.0) + jnp.where(row_y == y1[one], fy[one], 0.0)
        wx = jnp.where(row_x == x0[one], gx[one], 0.0) + jnp.where(row_x == x0[one] + 1, fx[one], 0.0)
        hi, lo = halves(wy)
        wy_hi[:, cols] = hi
        wy_lo[:, cols] = lo
        seen = mm(v_hi, hi) + (mm(v_lo, hi) + mm(v_hi, lo))
        for c in range(3):
            close = seen[c * cells : c * cells + width]
            beyond = seen[c * cells + width : (c + 1) * cells]
            values[c].append(jnp.sum(wx * (close * gz[one] + beyond * fz[one]), axis=0, keepdims=True))
    rows = jnp.concatenate([row for c in range(3) for row in values[c]], axis=0)
    reply_ref[...] = jnp.concatenate([rows, jnp.zeros((128 - 3 * SLOTS, slots), F32)], axis=0).T
    slot_ref[0:SLOTS, :] = x0.astype(F32)
    slot_ref[SLOTS : 2 * SLOTS, :] = fx
    slot_ref[2 * SLOTS : 3 * SLOTS, :] = fz
    for c in range(3):
        pull = friction * (atom_vel[c] - rows[c * SLOTS : (c + 1) * SLOTS])
        slot_ref[(3 + c) * SLOTS : (4 + c) * SLOTS, :] = pull


def look(mail, vel):
    _, _, depth = vel.shape
    slabs = mail.shape[0]
    return pl.pallas_call(
        look_kernel,
        out_shape=(
            jax.ShapeDtypeStruct((slabs, 128), F32),
            jax.ShapeDtypeStruct((6 * SLOTS, slabs), F32),
            jax.ShapeDtypeStruct((depth, SLOTS * slabs), BF16),
            jax.ShapeDtypeStruct((depth, SLOTS * slabs), BF16),
        ),
        name="look",
        compiler_params=pltpu.CompilerParams(vmem_limit_bytes=VMEM_LIMIT),
        cost_estimate=pl.CostEstimate(flops=500_000_000, bytes_accessed=1_000_000, transcendentals=0),
    )(mail, vel)


def halos(near_ref, far_ref):
    lanes = near_ref.shape[1] // 4
    even = even_device()
    below, above = [], []
    for place in range(4):
        cols = slice(place * lanes, (place + 1) * lanes)
        near = near_ref[:, cols].astype(F32)
        far = far_ref[:, cols].astype(F32)
        below.append(jnp.where(even, far, near))
        above.append(jnp.where(even, near, far))
    return below, above


def push_kernel(
    axis_ref,
    slot_ref,
    wy_hi,
    wy_lo,
    early_ref,
    near_ref,
    far_ref,
    moved_ref,
    late_near_ref,
    late_far_ref,
    side_ref,
    force_ref,
    a_hi,
    a_lo,
):
    cells = axis_ref.shape[1]
    width = cells // 2
    slots = slot_ref.shape[1]
    row_x = iota((width, slots), 0)
    for r in range(SLOTS):
        cols = slice(r * slots, (r + 1) * slots)
        row = lambda v: slot_ref[v * SLOTS + r : v * SLOTS + r + 1, :]
        x0, fx, fz = row(0).astype(I32), row(1), row(2)
        wx = jnp.where(row_x == x0, 1.0 - fx, 0.0) + jnp.where(row_x == x0 + 1, fx, 0.0)
        for c in range(3):
            for z, weight in ((0, 1.0 - fz), (1, fz)):
                hi, lo = halves(wx * (weight * row(3 + c)))
                start = c * cells + z * width
                a_hi[start : start + width, cols] = hi
                a_lo[start : start + width, cols] = lo
    for c in (2, 0, 1):
        rows = slice(c * cells, (c + 1) * cells)
        force_ref[c] = mm_nt(a_hi[rows], wy_hi[...]) + (mm_nt(a_lo[rows], wy_hi[...]) + mm_nt(a_hi[rows], wy_lo[...]))
    edges = []
    for number in (5, 6, 1, 2, 3, 4):
        place = number - 1
        sign = 0.5 if number % 2 else -0.5
        for z in (0, 1):
            rows = slice(z * width, (z + 1) * width)
            value = shifted(axis_ref[place, rows, :] + sign * force_ref[place // 2, rows, :], number)
            if number == 5:
                if z == 1:
                    rises = value
                moved_ref[place, (1 - z) * width : (2 - z) * width, :] = value
            elif number == 6:
                if z == 0:
                    falls = value
                moved_ref[place, (1 - z) * width : (2 - z) * width, :] = value
            else:
                moved_ref[place, rows, :] = value
                if number in (1, 2):
                    edges.append(edge(value, number))
    even = even_device()
    late_near_ref[...] = jnp.where(even, rises, falls)
    late_far_ref[...] = jnp.where(even, falls, rises)
    for planes, numbers in zip(halos(near_ref, far_ref), (RISING, FALLING)):
        for plane, number in zip(planes, numbers):
            if SPEEDS[number][0]:
                edges.append(edge(plane, number))
    side_ref[0:16, :] = early_ref[...]
    side_ref[16:24, :] = jnp.concatenate(edges, axis=0)


def push(axis, slot, wy_hi, wy_lo, early, near, far):
    _, cells, lanes = axis.shape
    slots = wy_hi.shape[1]
    width = cells // 2
    return pl.pallas_call(
        push_kernel,
        out_shape=(
            jax.ShapeDtypeStruct((6, cells, lanes), F32),
            jax.ShapeDtypeStruct((width, lanes), F32),
            jax.ShapeDtypeStruct((width, lanes), F32),
            jax.ShapeDtypeStruct((24, lanes), F32),
        ),
        scratch_shapes=[
            pltpu.VMEM((3, cells, lanes), F32),
            pltpu.VMEM((3 * cells, slots), BF16),
            pltpu.VMEM((3 * cells, slots), BF16),
        ],
        name="push",
        compiler_params=pltpu.CompilerParams(vmem_limit_bytes=VMEM_LIMIT),
        cost_estimate=pl.CostEstimate(flops=500_000_000, bytes_accessed=1_500_000, transcendentals=0),
    )(axis, slot, wy_hi, wy_lo, early, near, far)


def gather_kernel(calm_ref, moved_ref, near_ref, far_ref, side_ref, late_near_ref, late_far_ref, out_ref):
    cells = calm_ref.shape[1]
    width = cells // 2

    def put(number, z, at):
        row = z * width + (0 if SPEEDS[number][0] > 0 else width - 1)
        out_ref[number, row : row + 1, :] = side_ref[at : at + 1, :]

    for place, number in enumerate(CALM):
        if number in FLAT:
            out_ref[number] = calm_ref[place]
    for place in range(4):
        out_ref[place + 1] = moved_ref[place]
    even = even_device()
    out_ref[5, width:, :] = moved_ref[4, width:, :]
    out_ref[5, :width, :] = jnp.where(even, late_far_ref[...], late_near_ref[...])
    out_ref[6, :width, :] = moved_ref[5, :width, :]
    out_ref[6, width:, :] = jnp.where(even, late_near_ref[...], late_far_ref[...])
    at, corner = 0, 20
    for number in FLAT[1:]:
        for z in (0, 1):
            put(number, z, at)
            at += 1
    below, above = halos(near_ref, far_ref)
    for arrived, numbers, stays in ((below, RISING, 1), (above, FALLING, 0)):
        for place, number in enumerate(numbers):
            kept, new = stays * width, (1 - stays) * width
            out_ref[number, kept : kept + width, :] = calm_ref[CALM.index(number), kept : kept + width, :]
            out_ref[number, new : new + width, :] = arrived[place]
            if SPEEDS[number][0]:
                put(number, stays, at)
                put(number, 1 - stays, corner)
                at += 1
                corner += 1
    for number in (1, 2):
        for z in (0, 1):
            put(number, z, 16 + 2 * (number - 1) + z)


def gather(calm, moved, near, far, side, late_near, late_far):
    _, cells, lanes = calm.shape
    return pl.pallas_call(
        gather_kernel,
        out_shape=jax.ShapeDtypeStruct((19, cells, lanes), F32),
        name="gather",
        compiler_params=pltpu.CompilerParams(vmem_limit_bytes=VMEM_LIMIT),
        cost_estimate=pl.CostEstimate(flops=1_000, bytes_accessed=3_000_000, transcendentals=0),
    )(calm, moved, near, far, side, late_near, late_far)


def finish_kernel(reply_ref, slab_ref, rank_ref, vel_ref, fric_ref, pull_ref, force_ref):
    slabs, atoms = reply_ref.shape[0], slab_ref.shape[1]
    one_hot = jnp.where(iota((slabs, atoms), 0) == slab_ref[...], 1.0, 0.0).astype(BF16)
    high, low = halves(reply_ref[...].T[: 3 * SLOTS])
    picked = mm(high, one_hot) + mm(low, one_hot)
    mine = iota((SLOTS, atoms), 0).astype(F32) == rank_ref[...]
    for c in range(3):
        seen = jnp.sum(jnp.where(mine, picked[c * SLOTS : (c + 1) * SLOTS], 0.0), axis=0, keepdims=True)
        drag = fric_ref[...] * (seen - vel_ref[c : c + 1, :])
        force_ref[c : c + 1, :] = pull_ref[c : c + 1, :] + drag


def finish(reply, slab, rank, vel, fric, pull):
    atoms = slab.shape[1]
    return pl.pallas_call(
        finish_kernel,
        out_shape=jax.ShapeDtypeStruct((3, atoms), F32),
        name="finish",
        compiler_params=pltpu.CompilerParams(vmem_limit_bytes=VMEM_LIMIT),
        cost_estimate=pl.CostEstimate(flops=20_000_000, bytes_accessed=100_000, transcendentals=0),
    )(reply, slab, rank, vel, fric, pull)


def message(table, own_half, rbf, w_out, nbrs, bonds, spacing, basis):
    feats, block = own_half.shape
    atoms = table.shape[1]
    centers = iota((basis, block), 0).astype(F32) * spacing
    rows = iota((atoms, block), 0)
    total, force = None, None
    for nbr, bond in zip(nbrs, bonds):
        place = nbr // atoms
        one_hot = jnp.where(rows == nbr % atoms, 1.0, 0.0).astype(BF16)
        length = jnp.sqrt(bond[0] * bond[0] + bond[1] * bond[1] + bond[2] * bond[2] + 1e-6)
        scaled = (length - centers) * (1.0 / spacing)
        rad_hi, rad_lo = halves(jnp.exp(-scaled * scaled))
        radial = jnp.concatenate([rad_hi, rad_hi, rad_lo, jnp.zeros((feats - 3 * basis, block), BF16)], axis=0)
        seen = mm(table[...], one_hot)
        picked = jnp.where(place == 0, seen[:feats], jnp.where(place == 1, seen[feats : 2 * feats], seen[2 * feats :]))
        half = own_half + picked + mm(rbf, radial)
        hidden = half + half * jnp.tanh(half)
        scalar = jnp.sum(hidden * w_out, axis=0, keepdims=True)
        terms = [scalar * b for b in bond]
        total = hidden if total is None else total + hidden
        force = terms if force is None else [f + t for f, t in zip(force, terms)]
    return total, force


def potential_table(near_ref, own_ref, far_ref, w_self_ref, w_nbr_ref, table, own_half):
    feats = own_ref.shape[0]
    above = jnp.where(even_device(), 2 * feats, 0)
    for start, ref in ((above, near_ref), (feats, own_ref), (2 * feats - above, far_ref)):
        value = mm(w_nbr_ref[...], ref[...]).astype(BF16)
        rows = pl.ds(start if isinstance(start, int) else pl.multiple_of(start, feats), feats)
        table[rows, :] = (value.astype(F32) * 0.5).astype(BF16)
    own_half[...] = 0.5 * mm(w_self_ref[...], own_ref[...])


def potential_first_kernel(
    near_ref,
    own_ref,
    far_ref,
    nbr_ref,
    bond_ref,
    w_self_ref,
    w_nbr_ref,
    w_rbf_ref,
    w_out_ref,
    force_ref,
    new_ref,
    table,
    own_half,
):
    potential_table(near_ref, own_ref, far_ref, w_self_ref, w_nbr_ref, table, own_half)
    potential_block(0, own_ref, nbr_ref, bond_ref, w_rbf_ref, w_out_ref, table, own_half, force_ref, new_ref)


def potential_block(start, own_ref, nbr_ref, bond_ref, w_rbf_ref, w_out_ref, table_ref, half_ref, force_ref, new_ref):
    block = force_ref.shape[1] - start
    count, basis = nbr_ref.shape[0], w_rbf_ref.shape[0]
    cols = slice(start, start + block)
    feats = own_ref.shape[0]
    rbf_hi, rbf_lo = halves(0.5 * w_rbf_ref[...])
    rbf_hi, rbf_lo = rbf_hi.astype(F32), rbf_lo.astype(F32)
    rest = jnp.zeros((feats - 3 * basis, feats), F32)
    rbf = jnp.concatenate([rbf_hi, rbf_lo, rbf_hi, rest], axis=0).T.astype(BF16)
    w_out = jnp.broadcast_to(w_out_ref[...], (8, feats)).T[:, 0:1]
    total, force = message(
        table_ref,
        half_ref[:, cols],
        rbf,
        w_out,
        [nbr_ref[k : k + 1, cols] for k in range(count)],
        [[bond_ref[c, k : k + 1, cols] for c in range(3)] for k in range(count)],
        RADIAL_REACH / (basis - 1),
        basis,
    )
    for c in range(3):
        force_ref[c : c + 1, cols] = force[c]
    new_ref[:, cols] = (own_ref[:, cols].astype(F32) + total * (1.0 / count)).astype(BF16)


def potential_second_kernel(
    near_ref,
    own_ref,
    far_ref,
    nbr_ref,
    bond_ref,
    w_self_ref,
    w_nbr_ref,
    w_rbf_ref,
    w_out_ref,
    first_force_ref,
    first_new_ref,
    force_ref,
    new_ref,
    table,
    own_half,
):
    half = first_new_ref.shape[1]
    force_ref[:, :half] = first_force_ref[...]
    new_ref[:, :half] = first_new_ref[...]
    potential_table(near_ref, own_ref, far_ref, w_self_ref, w_nbr_ref, table, own_half)
    potential_block(half, own_ref, nbr_ref, bond_ref, w_rbf_ref, w_out_ref, table, own_half, force_ref, new_ref)


def potential(kernel, name, columns, flops, *args):
    feats, atoms = args[1].shape
    return pl.pallas_call(
        kernel,
        out_shape=(
            jax.ShapeDtypeStruct((3, columns), F32),
            jax.ShapeDtypeStruct((feats, columns), BF16),
        ),
        scratch_shapes=[
            pltpu.VMEM((3 * feats, atoms), BF16),
            pltpu.VMEM((feats, atoms), F32),
        ],
        name=name,
        compiler_params=pltpu.CompilerParams(vmem_limit_bytes=VMEM_LIMIT),
        cost_estimate=pl.CostEstimate(flops=flops, bytes_accessed=100_000, transcendentals=0),
    )(*args)


def body(
    slabs,
    populations,
    relax_rates,
    slab,
    stencil_base,
    frac,
    atom_vel,
    friction,
    features,
    neighbors,
    bonds,
    w_self,
    w_nbr,
    w_rbf,
    w_out,
):
    _, planes, width, depth = populations.shape
    atoms = slab.shape[0]
    chip = [(i, i ^ 1) for i in range(slabs)]
    link = [(i, (i - 1 if i % 2 == 0 else i + 1) % slabs) for i in range(slabs)]
    across = [(0, 1), (1, 0)]
    slab_row = slab.reshape(1, atoms)
    friction_row = friction.reshape(1, atoms)

    mail, rank = pack(slab_row, stencil_base.reshape(1, atoms), frac, atom_vel, friction_row, slabs)
    sent = features
    near_features = lax.ppermute(sent, "fluid", chip)
    far_features = lax.ppermute(sent, "fluid", link)
    mail = lax.all_to_all(mail.reshape(slabs, 1, 128), "fluid", split_axis=0, concat_axis=0, tiled=True)
    rest, axis, vel, near, far = relax(relax_rates, populations.reshape(19, planes * width, depth))
    calm, side = stream(rest)
    far = lax.ppermute(far, "fluid", link)
    near = lax.ppermute(near, "fluid", chip)
    nbrs, bonds, w_rbf, w_out = neighbors.T, bonds.transpose(0, 2, 1), w_rbf.T, w_out.reshape(1, -1)
    around = (near_features, features, far_features, nbrs, bonds, w_self, w_nbr, w_rbf, w_out)
    first_pull, first_new = potential(potential_first_kernel, "potential_first", atoms // 2, FIRST_FLOPS, *around)
    mail, first_pull, side = lax.optimization_barrier((mail, first_pull, side))

    reply, slot, wy_hi, wy_lo = look(mail.reshape(slabs, 128), vel)
    reply = lax.all_to_all(reply.reshape(slabs, 1, 128), "fluid", split_axis=0, concat_axis=0, tiled=True)
    moved, late_near, late_far, side = push(axis, slot, wy_hi, wy_lo, side, near, far)
    side = lax.ppermute(side, "group", across)
    late_far = lax.ppermute(late_far, "fluid", link)
    late_near = lax.ppermute(late_near, "fluid", chip)
    first_pull, moved = lax.optimization_barrier((first_pull, moved))
    pull, new_features = potential(
        potential_second_kernel, "potential_second", atoms, SECOND_FLOPS, *around, first_pull, first_new
    )
    pops = gather(calm, moved, near, far, side, late_near, late_far)
    atom_force = finish(reply.reshape(slabs, 128), slab_row, rank, atom_vel, friction_row, pull)
    return pops.reshape(populations.shape), atom_force, new_features


def solution(mesh):
    in_specs = (
        P(None, "fluid", "group", None),
        P(),
        P(("fluid", "group"), None),
        P(("fluid", "group")),
        P(None, ("fluid", "group")),
        P(None, ("fluid", "group")),
        P(("fluid", "group")),
        P(None, ("fluid", "group")),
        P(("fluid", "group"), None),
        P(None, ("fluid", "group"), None),
        P(),
        P(),
        P(),
        P(),
    )
    out_specs = (
        P(None, "fluid", "group", None),
        P(None, ("fluid", "group")),
        P(None, ("fluid", "group")),
    )
    return jax.shard_map(
        functools.partial(body, mesh.shape["fluid"]),
        mesh=mesh,
        in_specs=in_specs,
        out_specs=out_specs,
        check_vma=False,
    )
```

```python
import functools

import jax
import jax.numpy as jnp
from jax import lax
from jax.experimental import pallas as pl
from jax.experimental.pallas import tpu as pltpu
from jax.sharding import PartitionSpec as P

F32 = jnp.float32
BF16 = jnp.bfloat16
I32 = jnp.int32

RADIAL_REACH = 4.0
SLOTS = 8

SPEEDS = (
    (0, 0, 0),
    (1, 0, 0),
    (-1, 0, 0),
    (0, 1, 0),
    (0, -1, 0),
    (0, 0, 1),
    (0, 0, -1),
    (1, 1, 0),
    (-1, -1, 0),
    (1, -1, 0),
    (-1, 1, 0),
    (1, 0, 1),
    (-1, 0, -1),
    (1, 0, -1),
    (-1, 0, 1),
    (0, 1, 1),
    (0, -1, -1),
    (0, 1, -1),
    (0, -1, 1),
)
RISING = (11, 14, 15, 18)
FALLING = (12, 13, 16, 17)
FLAT = (0, 7, 8, 9, 10)
CALM = (0, 7, 8, 9, 10, 11, 12, 13, 14, 15, 16, 17, 18)

VMEM_LIMIT = 48 * 1024 * 1024
STREAM_FLOPS = 4_000_000_000
FIRST_FLOPS = 3_500_000_000
SECOND_FLOPS = 500_000_000


def halves(value):
    high = value.astype(BF16)
    low = (value - high.astype(F32)).astype(BF16)
    return high, low


def thirds(value):
    high = value.astype(BF16)
    rest = value - high.astype(F32)
    middle = rest.astype(BF16)
    low = (rest - middle.astype(F32)).astype(BF16)
    return high, middle, low


def mm(a, b):
    return jnp.dot(a, b, preferred_element_type=F32)


def mm_nt(a, b):
    return lax.dot_general(a, b, (((1,), (1,)), ((), ())), preferred_element_type=F32)


def iota(shape, dim):
    return lax.broadcasted_iota(I32, shape, dim)


def packed(slab, base, frac_ref, vel_ref, fric, slabs, earlier):
    atoms = slab.shape[1]
    named = iota((slabs, atoms), 0) == slab
    one_hot = jnp.where(named, 1.0, 0.0)
    one_hot_b = one_hot.astype(BF16)
    before = mm(one_hot_b, earlier)
    rank = jnp.sum(one_hot * before, axis=0, keepdims=True)
    mine = iota((SLOTS, atoms), 0).astype(F32) == rank
    rows = [frac_ref[c : c + 1, :] for c in range(3)]
    rows += [vel_ref[c : c + 1, :] for c in range(3)]
    rows += [fric, base.astype(F32)]
    spread = [jnp.where(mine, row, 0.0) for row in rows]
    high, middle, low = thirds(jnp.concatenate(spread, axis=0))
    return mm_nt(one_hot_b, high) + (mm_nt(one_hot_b, middle) + mm_nt(one_hot_b, low)), rank


def moments_of(d):
    m = [None] * 19
    quad = {}
    for name, (pp, nn, pn, np_) in dict(xy=(7, 8, 9, 10), xz=(11, 12, 13, 14), yz=(15, 16, 17, 18)).items():
        same, cross = d[pp] + d[nn], d[pn] + d[np_]
        odd_same, odd_cross = d[pp] - d[nn], d[pn] - d[np_]
        quad[name] = (same + cross, same - cross, odd_same + odd_cross, odd_same - odd_cross)
    sxy, m[4], m[10], m[12] = quad["xy"]
    sxz, m[5], m[11], m[13] = quad["xz"]
    syz, m[6], m[15], m[14] = quad["yz"]
    m[16], m[17], m[18] = sxy, sxz, syz
    ax, ay, az = d[1] + d[2], d[3] + d[4], d[5] + d[6]
    m[0] = (d[0] + ax) + (ay + az) + (sxy + (sxz + syz))
    m[1] = (d[1] - d[2]) + (m[10] + m[11])
    m[2] = (d[3] - d[4]) + (m[12] + m[15])
    m[3] = (d[5] - d[6]) + (m[13] + m[14])
    m[7] = ax + (sxy + sxz)
    m[8] = ay + (sxy + syz)
    m[9] = az + (sxz + syz)
    return m


def populations_of(m):
    f = [None] * 19
    for (pp, nn, pn, np_), (s, c, first, second) in (
        ((7, 8, 9, 10), (m[16], m[4], m[10], m[12])),
        ((11, 12, 13, 14), (m[17], m[5], m[11], m[13])),
        ((15, 16, 17, 18), (m[18], m[6], m[15], m[14])),
    ):
        same, cross = 0.25 * (s + c), 0.25 * (s - c)
        odd_same, odd_cross = 0.25 * (first + second), 0.25 * (first - second)
        f[pp], f[nn] = same + odd_same, same - odd_same
        f[pn], f[np_] = cross + odd_cross, cross - odd_cross
    for plus, minus, square, line, squares, lines in (
        (1, 2, m[7], m[1], (m[16], m[17]), (m[10], m[11])),
        (3, 4, m[8], m[2], (m[16], m[18]), (m[12], m[15])),
        (5, 6, m[9], m[3], (m[17], m[18]), (m[13], m[14])),
    ):
        even = 0.5 * (square - (squares[0] + squares[1]))
        odd = 0.5 * (line - (lines[0] + lines[1]))
        f[plus], f[minus] = even + odd, even - odd
    f[0] = m[0] - (m[7] + (m[8] + m[9])) + (m[16] + (m[17] + m[18]))
    return f


def equilibrium_of(density, u):
    ux, uy, uz = u
    rest = 1.0 - 1.5 * (ux * ux + uy * uy + uz * uz)
    eq = [None] * 19
    eq[0] = (1.0 / 3.0) * density * rest
    scale_axis, scale_diagonal = (1.0 / 18.0) * density, (1.0 / 36.0) * density
    for plus, minus, along, scale in (
        (1, 2, ux, scale_axis),
        (3, 4, uy, scale_axis),
        (5, 6, uz, scale_axis),
        (7, 8, ux + uy, scale_diagonal),
        (9, 10, ux - uy, scale_diagonal),
        (11, 12, ux + uz, scale_diagonal),
        (13, 14, ux - uz, scale_diagonal),
        (15, 16, uy + uz, scale_diagonal),
        (17, 18, uy - uz, scale_diagonal),
    ):
        even = rest + 4.5 * along * along
        odd = 3.0 * along
        eq[plus], eq[minus] = scale * (even + odd), scale * (even - odd)
    return eq


def shifted(plane, number):
    cx, cy, _ = SPEEDS[number]
    if cy:
        plane = pltpu.roll(plane, cy % plane.shape[1], 1)
    if cx:
        plane = pltpu.roll(plane, cx % plane.shape[0], 0)
    return plane


def edge(plane, number):
    width = plane.shape[0]
    return plane[0:1] if SPEEDS[number][0] > 0 else plane[width - 1 : width]


def pack_kernel(
    slab_hbm, base_hbm, frac_hbm, vel_hbm, fric_hbm, mail_ref, rank_ref, slab_ref, base_ref, frac_ref, vel_ref, fric_ref, sems
):
    pairs = (
        (slab_hbm, slab_ref),
        (base_hbm, base_ref),
        (frac_hbm, frac_ref),
        (vel_hbm, vel_ref),
        (fric_hbm, fric_ref),
    )
    copies = [pltpu.make_async_copy(src, dst, sems.at[at]) for at, (src, dst) in enumerate(pairs)]
    for copy in copies:
        copy.start()
    atoms = slab_ref.shape[1]
    earlier = jnp.where(iota((atoms, atoms), 0) < iota((atoms, atoms), 1), 1.0, 0.0).astype(BF16)
    for copy in copies:
        copy.wait()
    mail, rank = packed(
        slab_ref[...], base_ref[...], frac_ref, vel_ref, fric_ref[...], mail_ref.shape[0], earlier
    )
    filled = mail.shape[1]
    mail_ref[:, :filled] = mail
    mail_ref[:, filled:] = jnp.zeros((mail.shape[0], mail_ref.shape[1] - filled), F32)
    rank_ref[...] = rank


def pack(slab, base, frac, vel, fric, slabs):
    atoms = slab.shape[1]
    vmem = pl.BlockSpec(memory_space=pltpu.VMEM)
    outside = [pltpu.with_memory_space_constraint(x, pltpu.HBM) for x in (slab, base, frac, vel, fric)]
    return pl.pallas_call(
        pack_kernel,
        in_specs=[pl.BlockSpec(memory_space=pltpu.HBM)] * 5,
        out_specs=[vmem] * 2,
        out_shape=(
            jax.ShapeDtypeStruct((slabs, 128), F32),
            jax.ShapeDtypeStruct((1, atoms), F32),
        ),
        scratch_shapes=[
            pltpu.VMEM((1, atoms), I32),
            pltpu.VMEM((1, atoms), I32),
            pltpu.VMEM((3, atoms), F32),
            pltpu.VMEM((3, atoms), F32),
            pltpu.VMEM((1, atoms), F32),
            pltpu.SemaphoreType.DMA((5,)),
        ],
        name="pack",
        compiler_params=pltpu.CompilerParams(vmem_limit_bytes=VMEM_LIMIT),
        cost_estimate=pl.CostEstimate(flops=400_000_000, bytes_accessed=4_000_000, transcendentals=0),
    )(*outside)


def even_device():
    return lax.axis_index("fluid") % 2 == 0


def relax_kernel(rates_ref, pops_ref, *refs):
    rest_ref, axis_ref, vel_ref, near_ref, far_ref = refs[-5:]
    cells = pops_ref.shape[1]
    width = cells // 2

    def chunk(step, carry):
        rows = pl.ds(pl.multiple_of(step * 8, 8), 8)
        f = [pops_ref[i, rows, :] for i in range(19)]
        low = moments_of(f)
        density = low[0]
        inverse = 1.0 / density
        u = [low[c] * inverse for c in (1, 2, 3)]
        for c in range(3):
            vel_ref[c, rows, :] = u[c]
        eq = equilibrium_of(density, u)
        m = moments_of([f[i] - eq[i] for i in range(19)])
        relaxed = populations_of([rates_ref[i] * m[i] for i in range(19)])
        for i in range(19):
            if i in CALM:
                rest_ref[CALM.index(i), rows, :] = f[i] - relaxed[i]
            else:
                axis_ref[i - 1, rows, :] = f[i] - relaxed[i]
        return carry

    lax.fori_loop(0, cells // 8, chunk, 0, unroll=4)

    lanes = pops_ref.shape[2]
    even = even_device()
    for place, (rising, falling) in enumerate(zip(RISING, FALLING)):
        cols = slice(place * lanes, (place + 1) * lanes)
        rises = shifted(rest_ref[CALM.index(rising), width:, :], rising)
        falls = shifted(rest_ref[CALM.index(falling), :width, :], falling)
        near_ref[:, cols] = jnp.where(even, rises, falls).astype(BF16)
        far_ref[:, cols] = jnp.where(even, falls, rises).astype(BF16)


def stream_kernel(rest_ref, calm_ref, side_ref):
    cells, lanes = rest_ref.shape[1:]
    width = cells // 2

    def plane(number, z):
        return shifted(rest_ref[CALM.index(number), z * width : (z + 1) * width, :], number)

    edges = []
    for place, number in enumerate(CALM):
        if number in FLAT:
            for z in (0, 1):
                value = plane(number, z)
                calm_ref[place, z * width : (z + 1) * width, :] = value
                if number:
                    edges.append(edge(value, number))
    for numbers, stays in ((RISING, 1), (FALLING, 0)):
        for number in numbers:
            value = plane(number, 1 - stays)
            calm_ref[CALM.index(number), stays * width : (stays + 1) * width, :] = value
            if SPEEDS[number][0]:
                edges.append(edge(value, number))
    side_ref[...] = jnp.concatenate(edges + [jnp.zeros((16 - len(edges), lanes), F32)], axis=0)


def stream(rest):
    _, cells, lanes = rest.shape
    return pl.pallas_call(
        stream_kernel,
        out_shape=(
            jax.ShapeDtypeStruct((13, cells, lanes), F32),
            jax.ShapeDtypeStruct((16, lanes), F32),
        ),
        name="stream",
        compiler_params=pltpu.CompilerParams(vmem_limit_bytes=VMEM_LIMIT),
        cost_estimate=pl.CostEstimate(flops=STREAM_FLOPS, bytes_accessed=100_000, transcendentals=0),
    )(rest)


def relax(rates, pops, *later):
    _, cells, lanes = pops.shape
    width = cells // 2
    vmem = pl.BlockSpec(memory_space=pltpu.VMEM)
    return pl.pallas_call(
        relax_kernel,
        in_specs=[pl.BlockSpec(memory_space=pltpu.SMEM)] + [vmem] * (1 + len(later)),
        out_specs=[vmem] * 5,
        out_shape=(
            jax.ShapeDtypeStruct((13, cells, lanes), F32),
            jax.ShapeDtypeStruct((6, cells, lanes), F32),
            jax.ShapeDtypeStruct((3, cells, lanes), F32),
            jax.ShapeDtypeStruct((width, 4 * lanes), BF16),
            jax.ShapeDtypeStruct((width, 4 * lanes), BF16),
        ),
        name="relax",
        compiler_params=pltpu.CompilerParams(vmem_limit_bytes=VMEM_LIMIT),
        cost_estimate=pl.CostEstimate(flops=10_000_000, bytes_accessed=6_000_000, transcendentals=0),
    )(rates, pops, *later)


def look_kernel(mail_ref, vel_ref, reply_ref, slot_ref, wy_hi, wy_lo):
    comps, cells, depth = vel_ref.shape
    width = cells // 2
    slots = mail_ref.shape[0]
    t = mail_ref[...].T
    field = lambda v: t[v * SLOTS : (v + 1) * SLOTS, :]
    fx, fy, fz = field(0), field(1), field(2)
    atom_vel = [field(3), field(4), field(5)]
    friction = field(6)
    base = field(7).astype(I32)
    x0 = (base // depth) % width
    y0 = base % depth
    y1 = (y0 + 1) % depth
    gx, gy, gz = 1.0 - fx, 1.0 - fy, 1.0 - fz
    row_y = iota((depth, slots), 0)
    row_x = iota((width, slots), 0)

    v_hi, v_lo = halves(vel_ref[...].reshape(comps * cells, depth))
    values = [[], [], []]
    for r in range(SLOTS):
        one = slice(r, r + 1)
        cols = slice(r * slots, (r + 1) * slots)
        wy = jnp.where(row_y == y0[one], gy[one], 0.0) + jnp.where(row_y == y1[one], fy[one], 0.0)
        wx = jnp.where(row_x == x0[one], gx[one], 0.0) + jnp.where(row_x == x0[one] + 1, fx[one], 0.0)
        hi, lo = halves(wy)
        wy_hi[:, cols] = hi
        wy_lo[:, cols] = lo
        seen = mm(v_hi, hi) + (mm(v_lo, hi) + mm(v_hi, lo))
        for c in range(3):
            close = seen[c * cells : c * cells + width]
            beyond = seen[c * cells + width : (c + 1) * cells]
            values[c].append(jnp.sum(wx * (close * gz[one] + beyond * fz[one]), axis=0, keepdims=True))
    rows = jnp.concatenate([row for c in range(3) for row in values[c]], axis=0)
    reply_ref[...] = jnp.concatenate([rows, jnp.zeros((128 - 3 * SLOTS, slots), F32)], axis=0).T
    slot_ref[0:SLOTS, :] = x0.astype(F32)
    slot_ref[SLOTS : 2 * SLOTS, :] = fx
    slot_ref[2 * SLOTS : 3 * SLOTS, :] = fz
    for c in range(3):
        pull = friction * (atom_vel[c] - rows[c * SLOTS : (c + 1) * SLOTS])
        slot_ref[(3 + c) * SLOTS : (4 + c) * SLOTS, :] = pull


def look(mail, vel):
    _, _, depth = vel.shape
    slabs = mail.shape[0]
    return pl.pallas_call(
        look_kernel,
        out_shape=(
            jax.ShapeDtypeStruct((slabs, 128), F32),
            jax.ShapeDtypeStruct((6 * SLOTS, slabs), F32),
            jax.ShapeDtypeStruct((depth, SLOTS * slabs), BF16),
            jax.ShapeDtypeStruct((depth, SLOTS * slabs), BF16),
        ),
        name="look",
        compiler_params=pltpu.CompilerParams(vmem_limit_bytes=VMEM_LIMIT),
        cost_estimate=pl.CostEstimate(flops=500_000_000, bytes_accessed=1_000_000, transcendentals=0),
    )(mail, vel)


def halos(near_ref, far_ref):
    lanes = near_ref.shape[1] // 4
    even = even_device()
    below, above = [], []
    for place in range(4):
        cols = slice(place * lanes, (place + 1) * lanes)
        near = near_ref[:, cols].astype(F32)
        far = far_ref[:, cols].astype(F32)
        below.append(jnp.where(even, far, near))
        above.append(jnp.where(even, near, far))
    return below, above


def push_kernel(
    axis_ref,
    slot_ref,
    wy_hi,
    wy_lo,
    early_ref,
    near_ref,
    far_ref,
    moved_ref,
    late_near_ref,
    late_far_ref,
    side_ref,
    force_ref,
    a_hi,
    a_lo,
):
    cells = axis_ref.shape[1]
    width = cells // 2
    slots = slot_ref.shape[1]
    row_x = iota((width, slots), 0)
    for r in range(SLOTS):
        cols = slice(r * slots, (r + 1) * slots)
        row = lambda v: slot_ref[v * SLOTS + r : v * SLOTS + r + 1, :]
        x0, fx, fz = row(0).astype(I32), row(1), row(2)
        wx = jnp.where(row_x == x0, 1.0 - fx, 0.0) + jnp.where(row_x == x0 + 1, fx, 0.0)
        for c in range(3):
            for z, weight in ((0, 1.0 - fz), (1, fz)):
                hi, lo = halves(wx * (weight * row(3 + c)))
                start = c * cells + z * width
                a_hi[start : start + width, cols] = hi
                a_lo[start : start + width, cols] = lo
    for c in (2, 0, 1):
        rows = slice(c * cells, (c + 1) * cells)
        force_ref[c] = mm_nt(a_hi[rows], wy_hi[...]) + (mm_nt(a_lo[rows], wy_hi[...]) + mm_nt(a_hi[rows], wy_lo[...]))
    edges = []
    for number in (5, 6, 1, 2, 3, 4):
        place = number - 1
        sign = 0.5 if number % 2 else -0.5
        for z in (0, 1):
            rows = slice(z * width, (z + 1) * width)
            value = shifted(axis_ref[place, rows, :] + sign * force_ref[place // 2, rows, :], number)
            if number == 5:
                if z == 1:
                    rises = value
                moved_ref[place, (1 - z) * width : (2 - z) * width, :] = value
            elif number == 6:
                if z == 0:
                    falls = value
                moved_ref[place, (1 - z) * width : (2 - z) * width, :] = value
            else:
                moved_ref[place, rows, :] = value
                if number in (1, 2):
                    edges.append(edge(value, number))
    even = even_device()
    late_near_ref[...] = jnp.where(even, rises, falls)
    late_far_ref[...] = jnp.where(even, falls, rises)
    for planes, numbers in zip(halos(near_ref, far_ref), (RISING, FALLING)):
        for plane, number in zip(planes, numbers):
            if SPEEDS[number][0]:
                edges.append(edge(plane, number))
    side_ref[0:16, :] = early_ref[...]
    side_ref[16:24, :] = jnp.concatenate(edges, axis=0)


def push(axis, slot, wy_hi, wy_lo, early, near, far):
    _, cells, lanes = axis.shape
    slots = wy_hi.shape[1]
    width = cells // 2
    return pl.pallas_call(
        push_kernel,
        out_shape=(
            jax.ShapeDtypeStruct((6, cells, lanes), F32),
            jax.ShapeDtypeStruct((width, lanes), F32),
            jax.ShapeDtypeStruct((width, lanes), F32),
            jax.ShapeDtypeStruct((24, lanes), F32),
        ),
        scratch_shapes=[
            pltpu.VMEM((3, cells, lanes), F32),
            pltpu.VMEM((3 * cells, slots), BF16),
            pltpu.VMEM((3 * cells, slots), BF16),
        ],
        name="push",
        compiler_params=pltpu.CompilerParams(vmem_limit_bytes=VMEM_LIMIT),
        cost_estimate=pl.CostEstimate(flops=500_000_000, bytes_accessed=1_500_000, transcendentals=0),
    )(axis, slot, wy_hi, wy_lo, early, near, far)


def gather_kernel(calm_ref, moved_ref, near_ref, far_ref, side_ref, late_near_ref, late_far_ref, out_ref):
    cells = calm_ref.shape[1]
    width = cells // 2

    def put(number, z, at):
        row = z * width + (0 if SPEEDS[number][0] > 0 else width - 1)
        out_ref[number, row : row + 1, :] = side_ref[at : at + 1, :]

    for place, number in enumerate(CALM):
        if number in FLAT:
            out_ref[number] = calm_ref[place]
    for place in range(4):
        out_ref[place + 1] = moved_ref[place]
    even = even_device()
    out_ref[5, width:, :] = moved_ref[4, width:, :]
    out_ref[5, :width, :] = jnp.where(even, late_far_ref[...], late_near_ref[...])
    out_ref[6, :width, :] = moved_ref[5, :width, :]
    out_ref[6, width:, :] = jnp.where(even, late_near_ref[...], late_far_ref[...])
    at, corner = 0, 20
    for number in FLAT[1:]:
        for z in (0, 1):
            put(number, z, at)
            at += 1
    below, above = halos(near_ref, far_ref)
    for arrived, numbers, stays in ((below, RISING, 1), (above, FALLING, 0)):
        for place, number in enumerate(numbers):
            kept, new = stays * width, (1 - stays) * width
            out_ref[number, kept : kept + width, :] = calm_ref[CALM.index(number), kept : kept + width, :]
            out_ref[number, new : new + width, :] = arrived[place]
            if SPEEDS[number][0]:
                put(number, stays, at)
                put(number, 1 - stays, corner)
                at += 1
                corner += 1
    for number in (1, 2):
        for z in (0, 1):
            put(number, z, 16 + 2 * (number - 1) + z)


def gather(calm, moved, near, far, side, late_near, late_far):
    _, cells, lanes = calm.shape
    return pl.pallas_call(
        gather_kernel,
        out_shape=jax.ShapeDtypeStruct((19, cells, lanes), F32),
        name="gather",
        compiler_params=pltpu.CompilerParams(vmem_limit_bytes=VMEM_LIMIT),
        cost_estimate=pl.CostEstimate(flops=1_000, bytes_accessed=3_000_000, transcendentals=0),
    )(calm, moved, near, far, side, late_near, late_far)


def finish_kernel(reply_ref, slab_ref, rank_ref, vel_ref, fric_ref, pull_ref, force_ref):
    slabs, atoms = reply_ref.shape[0], slab_ref.shape[1]
    one_hot = jnp.where(iota((slabs, atoms), 0) == slab_ref[...], 1.0, 0.0).astype(BF16)
    high, low = halves(reply_ref[...].T[: 3 * SLOTS])
    picked = mm(high, one_hot) + mm(low, one_hot)
    mine = iota((SLOTS, atoms), 0).astype(F32) == rank_ref[...]
    for c in range(3):
        seen = jnp.sum(jnp.where(mine, picked[c * SLOTS : (c + 1) * SLOTS], 0.0), axis=0, keepdims=True)
        drag = fric_ref[...] * (seen - vel_ref[c : c + 1, :])
        force_ref[c : c + 1, :] = pull_ref[c : c + 1, :] + drag


def finish(reply, slab, rank, vel, fric, pull):
    atoms = slab.shape[1]
    return pl.pallas_call(
        finish_kernel,
        out_shape=jax.ShapeDtypeStruct((3, atoms), F32),
        name="finish",
        compiler_params=pltpu.CompilerParams(vmem_limit_bytes=VMEM_LIMIT),
        cost_estimate=pl.CostEstimate(flops=20_000_000, bytes_accessed=100_000, transcendentals=0),
    )(reply, slab, rank, vel, fric, pull)


def message(table, own_half, rbf, w_out, nbrs, bonds, spacing, basis):
    feats, block = own_half.shape
    atoms = table.shape[1]
    centers = iota((basis, block), 0).astype(F32) * spacing
    rows = iota((atoms, block), 0)
    total, force = None, None
    for nbr, bond in zip(nbrs, bonds):
        place = nbr // atoms
        one_hot = jnp.where(rows == nbr % atoms, 1.0, 0.0).astype(BF16)
        length = jnp.sqrt(bond[0] * bond[0] + bond[1] * bond[1] + bond[2] * bond[2] + 1e-6)
        scaled = (length - centers) * (1.0 / spacing)
        rad_hi, rad_lo = halves(jnp.exp(-scaled * scaled))
        radial = jnp.concatenate([rad_hi, rad_hi, rad_lo, jnp.zeros((feats - 3 * basis, block), BF16)], axis=0)
        seen = mm(table[...], one_hot)
        picked = jnp.where(place == 0, seen[:feats], jnp.where(place == 1, seen[feats : 2 * feats], seen[2 * feats :]))
        half = own_half + picked + mm(rbf, radial)
        hidden = half + half * jnp.tanh(half)
        scalar = jnp.sum(hidden * w_out, axis=0, keepdims=True)
        terms = [scalar * b for b in bond]
        total = hidden if total is None else total + hidden
        force = terms if force is None else [f + t for f, t in zip(force, terms)]
    return total, force


def potential_table(near_ref, own_ref, far_ref, w_self_ref, w_nbr_ref, table, own_half):
    feats = own_ref.shape[0]
    above = jnp.where(even_device(), 2 * feats, 0)
    for start, ref in ((above, near_ref), (feats, own_ref), (2 * feats - above, far_ref)):
        value = mm(w_nbr_ref[...], ref[...]).astype(BF16)
        rows = pl.ds(start if isinstance(start, int) else pl.multiple_of(start, feats), feats)
        table[rows, :] = (value.astype(F32) * 0.5).astype(BF16)
    own_half[...] = 0.5 * mm(w_self_ref[...], own_ref[...])


def potential_first_kernel(
    far_ref,
    own_ref,
    near_ref,
    nbr_ref,
    bond_ref,
    w_self_ref,
    w_nbr_ref,
    w_rbf_ref,
    w_out_ref,
    force_ref,
    new_ref,
    table,
    own_half,
):
    potential_table(near_ref, own_ref, far_ref, w_self_ref, w_nbr_ref, table, own_half)
    potential_block(0, own_ref, nbr_ref, bond_ref, w_rbf_ref, w_out_ref, table, own_half, force_ref, new_ref)


def potential_block(start, own_ref, nbr_ref, bond_ref, w_rbf_ref, w_out_ref, table_ref, half_ref, force_ref, new_ref):
    block = force_ref.shape[1] - start
    count, basis = nbr_ref.shape[0], w_rbf_ref.shape[0]
    cols = slice(start, start + block)
    feats = own_ref.shape[0]
    rbf_hi, rbf_lo = halves(0.5 * w_rbf_ref[...])
    rbf_hi, rbf_lo = rbf_hi.astype(F32), rbf_lo.astype(F32)
    rest = jnp.zeros((feats - 3 * basis, feats), F32)
    rbf = jnp.concatenate([rbf_hi, rbf_lo, rbf_hi, rest], axis=0).T.astype(BF16)
    w_out = jnp.broadcast_to(w_out_ref[...], (8, feats)).T[:, 0:1]
    total, force = message(
        table_ref,
        half_ref[:, cols],
        rbf,
        w_out,
        [nbr_ref[k : k + 1, cols] for k in range(count)],
        [[bond_ref[c, k : k + 1, cols] for c in range(3)] for k in range(count)],
        RADIAL_REACH / (basis - 1),
        basis,
    )
    for c in range(3):
        force_ref[c : c + 1, cols] = force[c]
    new_ref[:, cols] = (own_ref[:, cols].astype(F32) + total * (1.0 / count)).astype(BF16)


def potential_second_kernel(
    far_ref,
    own_ref,
    near_ref,
    nbr_ref,
    bond_ref,
    w_self_ref,
    w_nbr_ref,
    w_rbf_ref,
    w_out_ref,
    first_force_ref,
    first_new_ref,
    force_ref,
    new_ref,
    table,
    own_half,
):
    half = first_new_ref.shape[1]
    force_ref[:, :half] = first_force_ref[...]
    new_ref[:, :half] = first_new_ref[...]
    potential_table(near_ref, own_ref, far_ref, w_self_ref, w_nbr_ref, table, own_half)
    potential_block(half, own_ref, nbr_ref, bond_ref, w_rbf_ref, w_out_ref, table, own_half, force_ref, new_ref)


def potential(kernel, name, columns, flops, *args):
    feats, atoms = args[1].shape
    return pl.pallas_call(
        kernel,
        out_shape=(
            jax.ShapeDtypeStruct((3, columns), F32),
            jax.ShapeDtypeStruct((feats, columns), BF16),
        ),
        scratch_shapes=[
            pltpu.VMEM((3 * feats, atoms), BF16),
            pltpu.VMEM((feats, atoms), F32),
        ],
        name=name,
        compiler_params=pltpu.CompilerParams(vmem_limit_bytes=VMEM_LIMIT),
        cost_estimate=pl.CostEstimate(flops=flops, bytes_accessed=100_000, transcendentals=0),
    )(*args)


def body(
    slabs,
    populations,
    relax_rates,
    slab,
    stencil_base,
    frac,
    atom_vel,
    friction,
    features,
    neighbors,
    bonds,
    w_self,
    w_nbr,
    w_rbf,
    w_out,
):
    _, planes, width, depth = populations.shape
    atoms = slab.shape[0]
    chip = [(i, i ^ 1) for i in range(slabs)]
    link = [(i, (i - 1 if i % 2 == 0 else i + 1) % slabs) for i in range(slabs)]
    across = [(0, 1), (1, 0)]
    slab_row = slab.reshape(1, atoms)
    friction_row = friction.reshape(1, atoms)

    mail, rank = pack(slab_row, stencil_base.reshape(1, atoms), frac, atom_vel, friction_row, slabs)
    sent = features
    near_features = lax.ppermute(sent, "fluid", chip)
    far_features = lax.ppermute(sent, "fluid", link)
    mail = lax.all_to_all(mail.reshape(slabs, 1, 128), "fluid", split_axis=0, concat_axis=0, tiled=True)
    nbrs, bonds, w_rbf, w_out = neighbors.T, bonds.transpose(0, 2, 1), w_rbf.T, w_out.reshape(1, -1)
    rest, axis, vel, near, far = relax(
        relax_rates,
        populations.reshape(19, planes * width, depth),
        features,
        nbrs,
        bonds,
        w_self,
        w_nbr,
        w_rbf,
        w_out,
    )
    calm, side = stream(rest)
    far = lax.ppermute(far, "fluid", link)
    near = lax.ppermute(near, "fluid", chip)
    around = (far_features, features, near_features, nbrs, bonds, w_self, w_nbr, w_rbf, w_out)
    first_pull, first_new = potential(potential_first_kernel, "potential_first", atoms // 2, FIRST_FLOPS, *around)
    mail, first_pull, side = lax.optimization_barrier((mail, first_pull, side))

    reply, slot, wy_hi, wy_lo = look(mail.reshape(slabs, 128), vel)
    reply = lax.all_to_all(reply.reshape(slabs, 1, 128), "fluid", split_axis=0, concat_axis=0, tiled=True)
    moved, late_near, late_far, side = push(axis, slot, wy_hi, wy_lo, side, near, far)
    side = lax.ppermute(side, "group", across)
    late_far = lax.ppermute(late_far, "fluid", link)
    late_near = lax.ppermute(late_near, "fluid", chip)
    first_pull, moved = lax.optimization_barrier((first_pull, moved))
    pull, new_features = potential(
        potential_second_kernel, "potential_second", atoms, SECOND_FLOPS, *around, first_pull, first_new
    )
    pops = gather(calm, moved, near, far, side, late_near, late_far)
    atom_force = finish(reply.reshape(slabs, 128), slab_row, rank, atom_vel, friction_row, pull)
    return pops.reshape(populations.shape), atom_force, new_features


def solution(mesh):
    in_specs = (
        P(None, "fluid", "group", None),
        P(),
        P(("fluid", "group"), None),
        P(("fluid", "group")),
        P(None, ("fluid", "group")),
        P(None, ("fluid", "group")),
        P(("fluid", "group")),
        P(None, ("fluid", "group")),
        P(("fluid", "group"), None),
        P(None, ("fluid", "group"), None),
        P(),
        P(),
        P(),
        P(),
    )
    out_specs = (
        P(None, "fluid", "group", None),
        P(None, ("fluid", "group")),
        P(None, ("fluid", "group")),
    )
    return jax.shard_map(
        functools.partial(body, mesh.shape["fluid"]),
        mesh=mesh,
        in_specs=in_specs,
        out_specs=out_specs,
        check_vma=False,
    )
```

```python
import functools

import jax
import jax.numpy as jnp
from jax import lax
from jax.experimental import pallas as pl
from jax.experimental.pallas import tpu as pltpu
from jax.sharding import PartitionSpec as P

F32 = jnp.float32
BF16 = jnp.bfloat16
I32 = jnp.int32

RADIAL_REACH = 4.0
SLOTS = 8

SPEEDS = (
    (0, 0, 0),
    (1, 0, 0),
    (-1, 0, 0),
    (0, 1, 0),
    (0, -1, 0),
    (0, 0, 1),
    (0, 0, -1),
    (1, 1, 0),
    (-1, -1, 0),
    (1, -1, 0),
    (-1, 1, 0),
    (1, 0, 1),
    (-1, 0, -1),
    (1, 0, -1),
    (-1, 0, 1),
    (0, 1, 1),
    (0, -1, -1),
    (0, 1, -1),
    (0, -1, 1),
)
RISING = (11, 14, 15, 18)
FALLING = (12, 13, 16, 17)
FLAT = (0, 7, 8, 9, 10)
CALM = (0, 7, 8, 9, 10, 11, 12, 13, 14, 15, 16, 17, 18)

VMEM_LIMIT = 48 * 1024 * 1024
STREAM_FLOPS = 4_000_000_000
FIRST_FLOPS = 3_500_000_000
SECOND_FLOPS = 500_000_000


def halves(value):
    high = value.astype(BF16)
    low = (value - high.astype(F32)).astype(BF16)
    return high, low


def mm(a, b):
    return jnp.dot(a, b, preferred_element_type=F32)


def mm_nt(a, b):
    return lax.dot_general(a, b, (((1,), (1,)), ((), ())), preferred_element_type=F32)


def iota(shape, dim):
    return lax.broadcasted_iota(I32, shape, dim)


def packed(slab, base, frac_ref, vel_ref, fric, slabs, earlier):
    atoms = slab.shape[1]
    named = iota((slabs, atoms), 0) == slab
    one_hot = jnp.where(named, 1.0, 0.0)
    one_hot_b = one_hot.astype(BF16)
    slab_rows, run = one_hot_b.shape[0], earlier.shape[0]
    runs = [one_hot_b[:, at : at + run] for at in range(0, atoms, run)]
    counts = mm(jnp.concatenate(runs, axis=0), earlier)
    before, total = [], 0.0
    for at in range(len(runs)):
        part = counts[at * slab_rows : (at + 1) * slab_rows]
        before.append(part[:, :run] + total)
        total = total + part[:, run:]
    before = jnp.concatenate(before, axis=1)
    rank = jnp.sum(one_hot * before, axis=0, keepdims=True)
    mine = iota((SLOTS, atoms), 0).astype(F32) == rank
    rows = [frac_ref[c : c + 1, :] for c in range(3)]
    rows += [vel_ref[c : c + 1, :] for c in range(3)]
    rows += [fric, base.astype(F32)]
    spread = [jnp.where(mine, row, 0.0) for row in rows]
    both = mm_nt(one_hot_b, jnp.concatenate(halves(jnp.concatenate(spread, axis=0)), axis=0))
    return both + pltpu.roll(both, both.shape[1] // 2, 1), rank


def moments_of(d):
    m = [None] * 19
    quad = {}
    for name, (pp, nn, pn, np_) in dict(xy=(7, 8, 9, 10), xz=(11, 12, 13, 14), yz=(15, 16, 17, 18)).items():
        same, cross = d[pp] + d[nn], d[pn] + d[np_]
        odd_same, odd_cross = d[pp] - d[nn], d[pn] - d[np_]
        quad[name] = (same + cross, same - cross, odd_same + odd_cross, odd_same - odd_cross)
    sxy, m[4], m[10], m[12] = quad["xy"]
    sxz, m[5], m[11], m[13] = quad["xz"]
    syz, m[6], m[15], m[14] = quad["yz"]
    m[16], m[17], m[18] = sxy, sxz, syz
    ax, ay, az = d[1] + d[2], d[3] + d[4], d[5] + d[6]
    m[0] = (d[0] + ax) + (ay + az) + (sxy + (sxz + syz))
    m[1] = (d[1] - d[2]) + (m[10] + m[11])
    m[2] = (d[3] - d[4]) + (m[12] + m[15])
    m[3] = (d[5] - d[6]) + (m[13] + m[14])
    m[7] = ax + (sxy + sxz)
    m[8] = ay + (sxy + syz)
    m[9] = az + (sxz + syz)
    return m


def populations_of(m):
    f = [None] * 19
    for (pp, nn, pn, np_), (s, c, first, second) in (
        ((7, 8, 9, 10), (m[16], m[4], m[10], m[12])),
        ((11, 12, 13, 14), (m[17], m[5], m[11], m[13])),
        ((15, 16, 17, 18), (m[18], m[6], m[15], m[14])),
    ):
        same, cross = 0.25 * (s + c), 0.25 * (s - c)
        odd_same, odd_cross = 0.25 * (first + second), 0.25 * (first - second)
        f[pp], f[nn] = same + odd_same, same - odd_same
        f[pn], f[np_] = cross + odd_cross, cross - odd_cross
    for plus, minus, square, line, squares, lines in (
        (1, 2, m[7], m[1], (m[16], m[17]), (m[10], m[11])),
        (3, 4, m[8], m[2], (m[16], m[18]), (m[12], m[15])),
        (5, 6, m[9], m[3], (m[17], m[18]), (m[13], m[14])),
    ):
        even = 0.5 * (square - (squares[0] + squares[1]))
        odd = 0.5 * (line - (lines[0] + lines[1]))
        f[plus], f[minus] = even + odd, even - odd
    f[0] = m[0] - (m[7] + (m[8] + m[9])) + (m[16] + (m[17] + m[18]))
    return f


def equilibrium_of(density, u):
    ux, uy, uz = u
    rest = 1.0 - 1.5 * (ux * ux + uy * uy + uz * uz)
    eq = [None] * 19
    eq[0] = (1.0 / 3.0) * density * rest
    scale_axis, scale_diagonal = (1.0 / 18.0) * density, (1.0 / 36.0) * density
    for plus, minus, along, scale in (
        (1, 2, ux, scale_axis),
        (3, 4, uy, scale_axis),
        (5, 6, uz, scale_axis),
        (7, 8, ux + uy, scale_diagonal),
        (9, 10, ux - uy, scale_diagonal),
        (11, 12, ux + uz, scale_diagonal),
        (13, 14, ux - uz, scale_diagonal),
        (15, 16, uy + uz, scale_diagonal),
        (17, 18, uy - uz, scale_diagonal),
    ):
        even = rest + 4.5 * along * along
        odd = 3.0 * along
        eq[plus], eq[minus] = scale * (even + odd), scale * (even - odd)
    return eq


def shifted(plane, number):
    cx, cy, _ = SPEEDS[number]
    if cy:
        plane = pltpu.roll(plane, cy % plane.shape[1], 1)
    if cx:
        plane = pltpu.roll(plane, cx % plane.shape[0], 0)
    return plane


def edge(plane, number):
    width = plane.shape[0]
    return plane[0:1] if SPEEDS[number][0] > 0 else plane[width - 1 : width]


def pack_kernel(
    slab_hbm, base_hbm, frac_hbm, vel_hbm, fric_hbm, mail_ref, rank_ref, slab_ref, base_ref, frac_ref, vel_ref, fric_ref, sems
):
    pairs = (
        (slab_hbm, slab_ref),
        (base_hbm, base_ref),
        (frac_hbm, frac_ref),
        (vel_hbm, vel_ref),
        (fric_hbm, fric_ref),
    )
    copies = [pltpu.make_async_copy(src, dst, sems.at[at]) for at, (src, dst) in enumerate(pairs)]
    for copy in copies:
        copy.start()
    earlier = jnp.where(iota((128, 256), 0) < iota((128, 256), 1), 1.0, 0.0).astype(BF16)
    for copy in copies:
        copy.wait()
    mail, rank = packed(
        slab_ref[...], base_ref[...], frac_ref, vel_ref, fric_ref[...], mail_ref.shape[0], earlier
    )
    mail_ref[...] = mail
    rank_ref[...] = rank


def pack(slab, base, frac, vel, fric, slabs):
    atoms = slab.shape[1]
    vmem = pl.BlockSpec(memory_space=pltpu.VMEM)
    outside = [pltpu.with_memory_space_constraint(x, pltpu.HBM) for x in (slab, base, frac, vel, fric)]
    return pl.pallas_call(
        pack_kernel,
        in_specs=[pl.BlockSpec(memory_space=pltpu.HBM)] * 5,
        out_specs=[vmem] * 2,
        out_shape=(
            jax.ShapeDtypeStruct((slabs, 128), F32),
            jax.ShapeDtypeStruct((1, atoms), F32),
        ),
        scratch_shapes=[
            pltpu.VMEM((1, atoms), I32),
            pltpu.VMEM((1, atoms), I32),
            pltpu.VMEM((3, atoms), F32),
            pltpu.VMEM((3, atoms), F32),
            pltpu.VMEM((1, atoms), F32),
            pltpu.SemaphoreType.DMA((5,)),
        ],
        name="pack",
        compiler_params=pltpu.CompilerParams(vmem_limit_bytes=VMEM_LIMIT),
        cost_estimate=pl.CostEstimate(flops=400_000_000, bytes_accessed=4_000_000, transcendentals=0),
    )(*outside)


def even_device():
    return lax.axis_index("fluid") % 2 == 0


def relax_kernel(rates_ref, pops_ref, *refs):
    rest_ref, axis_ref, vel_ref, near_ref, far_ref = refs[-5:]
    cells = pops_ref.shape[1]
    width = cells // 2

    def chunk(step, carry):
        rows = pl.ds(pl.multiple_of(step * 8, 8), 8)
        f = [pops_ref[i, rows, :] for i in range(19)]
        low = moments_of(f)
        density = low[0]
        inverse = 1.0 / density
        u = [low[c] * inverse for c in (1, 2, 3)]
        for c in range(3):
            vel_ref[c, rows, :] = u[c]
        eq = equilibrium_of(density, u)
        m = moments_of([f[i] - eq[i] for i in range(19)])
        relaxed = populations_of([rates_ref[i] * m[i] for i in range(19)])
        for i in range(19):
            if i in CALM:
                rest_ref[CALM.index(i), rows, :] = f[i] - relaxed[i]
            else:
                axis_ref[i - 1, rows, :] = f[i] - relaxed[i]
        return carry

    lax.fori_loop(0, cells // 8, chunk, 0, unroll=4)

    lanes = pops_ref.shape[2]
    even = even_device()
    for place, (rising, falling) in enumerate(zip(RISING, FALLING)):
        cols = slice(place * lanes, (place + 1) * lanes)
        rises = shifted(rest_ref[CALM.index(rising), width:, :], rising)
        falls = shifted(rest_ref[CALM.index(falling), :width, :], falling)
        near_ref[:, cols] = jnp.where(even, rises, falls).astype(BF16)
        far_ref[:, cols] = jnp.where(even, falls, rises).astype(BF16)


def stream_kernel(rest_ref, calm_ref, side_ref):
    cells, lanes = rest_ref.shape[1:]
    width = cells // 2

    def plane(number, z):
        return shifted(rest_ref[CALM.index(number), z * width : (z + 1) * width, :], number)

    edges = []
    for place, number in enumerate(CALM):
        if number in FLAT:
            for z in (0, 1):
                value = plane(number, z)
                calm_ref[place, z * width : (z + 1) * width, :] = value
                if number:
                    edges.append(edge(value, number))
    for numbers, stays in ((RISING, 1), (FALLING, 0)):
        for number in numbers:
            value = plane(number, 1 - stays)
            calm_ref[CALM.index(number), stays * width : (stays + 1) * width, :] = value
            if SPEEDS[number][0]:
                edges.append(edge(value, number))
    side_ref[...] = jnp.concatenate(edges + [jnp.zeros((16 - len(edges), lanes), F32)], axis=0)


def stream(rest):
    _, cells, lanes = rest.shape
    return pl.pallas_call(
        stream_kernel,
        out_shape=(
            jax.ShapeDtypeStruct((13, cells, lanes), F32),
            jax.ShapeDtypeStruct((16, lanes), F32),
        ),
        name="stream",
        compiler_params=pltpu.CompilerParams(vmem_limit_bytes=VMEM_LIMIT),
        cost_estimate=pl.CostEstimate(flops=STREAM_FLOPS, bytes_accessed=100_000, transcendentals=0),
    )(rest)


def relax(rates, pops, *later):
    _, cells, lanes = pops.shape
    width = cells // 2
    vmem = pl.BlockSpec(memory_space=pltpu.VMEM)
    return pl.pallas_call(
        relax_kernel,
        in_specs=[pl.BlockSpec(memory_space=pltpu.SMEM)] + [vmem] * (1 + len(later)),
        out_specs=[vmem] * 5,
        out_shape=(
            jax.ShapeDtypeStruct((13, cells, lanes), F32),
            jax.ShapeDtypeStruct((6, cells, lanes), F32),
            jax.ShapeDtypeStruct((3, cells, lanes), F32),
            jax.ShapeDtypeStruct((width, 4 * lanes), BF16),
            jax.ShapeDtypeStruct((width, 4 * lanes), BF16),
        ),
        name="relax",
        compiler_params=pltpu.CompilerParams(vmem_limit_bytes=VMEM_LIMIT),
        cost_estimate=pl.CostEstimate(flops=10_000_000, bytes_accessed=6_000_000, transcendentals=0),
    )(rates, pops, *later)


def look_kernel(mail_ref, vel_ref, reply_ref, slot_ref, wy_hi, wy_lo):
    comps, cells, depth = vel_ref.shape
    width = cells // 2
    slots = mail_ref.shape[0]
    t = mail_ref[...].T
    field = lambda v: t[v * SLOTS : (v + 1) * SLOTS, :]
    fx, fy, fz = field(0), field(1), field(2)
    atom_vel = [field(3), field(4), field(5)]
    friction = field(6)
    base = field(7).astype(I32)
    x0 = (base // depth) % width
    y0 = base % depth
    y1 = (y0 + 1) % depth
    gx, gy, gz = 1.0 - fx, 1.0 - fy, 1.0 - fz
    row_y = iota((depth, slots), 0)
    row_x = iota((width, slots), 0)

    v_hi, v_lo = halves(vel_ref[...].reshape(comps * cells, depth))
    v_parts = jnp.concatenate([v_hi, v_lo, v_hi], axis=1)
    values = [[], [], []]
    for first in range(0, SLOTS, 2):
        wx, weights = [], []
        for r in (first, first + 1):
            one = slice(r, r + 1)
            weights.append(
                jnp.where(row_y == y0[one], gy[one], 0.0) + jnp.where(row_y == y1[one], fy[one], 0.0)
            )
            wx.append(jnp.where(row_x == x0[one], gx[one], 0.0) + jnp.where(row_x == x0[one] + 1, fx[one], 0.0))
        hi, lo = halves(jnp.concatenate(weights, axis=1))
        cols = slice(first * slots, (first + 2) * slots)
        wy_hi[:, cols] = hi
        wy_lo[:, cols] = lo
        pair = mm(v_parts, jnp.concatenate([hi, hi, lo], axis=0))
        for r in (first, first + 1):
            one = slice(r, r + 1)
            seen = pair[:, (r - first) * slots : (r - first + 1) * slots]
            for c in range(3):
                close = seen[c * cells : c * cells + width]
                beyond = seen[c * cells + width : (c + 1) * cells]
                value = wx[r - first] * (close * gz[one] + beyond * fz[one])
                values[c].append(jnp.sum(value, axis=0, keepdims=True))
    rows = jnp.concatenate([row for c in range(3) for row in values[c]], axis=0)
    reply_ref[...] = jnp.concatenate([rows, jnp.zeros((128 - 3 * SLOTS, slots), F32)], axis=0).T
    slot_ref[0:SLOTS, :] = x0.astype(F32)
    slot_ref[SLOTS : 2 * SLOTS, :] = fx
    slot_ref[2 * SLOTS : 3 * SLOTS, :] = fz
    for c in range(3):
        pull = friction * (atom_vel[c] - rows[c * SLOTS : (c + 1) * SLOTS])
        slot_ref[(3 + c) * SLOTS : (4 + c) * SLOTS, :] = pull


def look(mail, vel):
    _, _, depth = vel.shape
    slabs = mail.shape[0]
    return pl.pallas_call(
        look_kernel,
        out_shape=(
            jax.ShapeDtypeStruct((slabs, 128), F32),
            jax.ShapeDtypeStruct((6 * SLOTS, slabs), F32),
            jax.ShapeDtypeStruct((depth, SLOTS * slabs), BF16),
            jax.ShapeDtypeStruct((depth, SLOTS * slabs), BF16),
        ),
        name="look",
        compiler_params=pltpu.CompilerParams(vmem_limit_bytes=VMEM_LIMIT),
        cost_estimate=pl.CostEstimate(flops=500_000_000, bytes_accessed=1_000_000, transcendentals=0),
    )(mail, vel)


def halos(near_ref, far_ref):
    lanes = near_ref.shape[1] // 4
    even = even_device()
    below, above = [], []
    for place in range(4):
        cols = slice(place * lanes, (place + 1) * lanes)
        near = near_ref[:, cols].astype(F32)
        far = far_ref[:, cols].astype(F32)
        below.append(jnp.where(even, far, near))
        above.append(jnp.where(even, near, far))
    return below, above


def push_kernel(
    axis_ref,
    slot_ref,
    wy_hi,
    wy_lo,
    early_ref,
    near_ref,
    far_ref,
    moved_ref,
    late_near_ref,
    late_far_ref,
    side_ref,
    force_ref,
    a_hi,
    a_lo,
):
    cells = axis_ref.shape[1]
    width = cells // 2
    slots = slot_ref.shape[1]
    row_x = iota((width, slots), 0)
    for r in range(SLOTS):
        cols = slice(r * slots, (r + 1) * slots)
        row = lambda v: slot_ref[v * SLOTS + r : v * SLOTS + r + 1, :]
        x0, fx, fz = row(0).astype(I32), row(1), row(2)
        wx = jnp.where(row_x == x0, 1.0 - fx, 0.0) + jnp.where(row_x == x0 + 1, fx, 0.0)
        for c in range(3):
            for z, weight in ((0, 1.0 - fz), (1, fz)):
                hi, lo = halves(wx * (weight * row(3 + c)))
                start = c * cells + z * width
                a_hi[start : start + width, cols] = hi
                a_lo[start : start + width, cols] = lo
    for c in (2, 0, 1):
        rows = slice(c * cells, (c + 1) * cells)
        force_ref[c] = mm_nt(a_hi[rows], wy_hi[...]) + (mm_nt(a_lo[rows], wy_hi[...]) + mm_nt(a_hi[rows], wy_lo[...]))
    edges = []
    for number in (5, 6, 1, 2, 3, 4):
        place = number - 1
        sign = 0.5 if number % 2 else -0.5
        for z in (0, 1):
            rows = slice(z * width, (z + 1) * width)
            value = shifted(axis_ref[place, rows, :] + sign * force_ref[place // 2, rows, :], number)
            if number == 5:
                if z == 1:
                    rises = value
                moved_ref[place, (1 - z) * width : (2 - z) * width, :] = value
            elif number == 6:
                if z == 0:
                    falls = value
                moved_ref[place, (1 - z) * width : (2 - z) * width, :] = value
            else:
                moved_ref[place, rows, :] = value
                if number in (1, 2):
                    edges.append(edge(value, number))
    even = even_device()
    late_near_ref[...] = jnp.where(even, rises, falls)
    late_far_ref[...] = jnp.where(even, falls, rises)
    for planes, numbers in zip(halos(near_ref, far_ref), (RISING, FALLING)):
        for plane, number in zip(planes, numbers):
            if SPEEDS[number][0]:
                edges.append(edge(plane, number))
    side_ref[0:16, :] = early_ref[...]
    side_ref[16:24, :] = jnp.concatenate(edges, axis=0)


def push(axis, slot, wy_hi, wy_lo, early, near, far):
    _, cells, lanes = axis.shape
    slots = wy_hi.shape[1]
    width = cells // 2
    return pl.pallas_call(
        push_kernel,
        out_shape=(
            jax.ShapeDtypeStruct((6, cells, lanes), F32),
            jax.ShapeDtypeStruct((width, lanes), F32),
            jax.ShapeDtypeStruct((width, lanes), F32),
            jax.ShapeDtypeStruct((24, lanes), F32),
        ),
        scratch_shapes=[
            pltpu.VMEM((3, cells, lanes), F32),
            pltpu.VMEM((3 * cells, slots), BF16),
            pltpu.VMEM((3 * cells, slots), BF16),
        ],
        name="push",
        compiler_params=pltpu.CompilerParams(vmem_limit_bytes=VMEM_LIMIT),
        cost_estimate=pl.CostEstimate(flops=500_000_000, bytes_accessed=1_500_000, transcendentals=0),
    )(axis, slot, wy_hi, wy_lo, early, near, far)


def gather_kernel(calm_ref, moved_ref, near_ref, far_ref, side_ref, late_near_ref, late_far_ref, out_ref):
    cells = calm_ref.shape[1]
    width = cells // 2

    def put(number, z, at):
        row = z * width + (0 if SPEEDS[number][0] > 0 else width - 1)
        out_ref[number, row : row + 1, :] = side_ref[at : at + 1, :]

    for place, number in enumerate(CALM):
        if number in FLAT:
            out_ref[number] = calm_ref[place]
    for place in range(4):
        out_ref[place + 1] = moved_ref[place]
    even = even_device()
    out_ref[5, width:, :] = moved_ref[4, width:, :]
    out_ref[5, :width, :] = jnp.where(even, late_far_ref[...], late_near_ref[...])
    out_ref[6, :width, :] = moved_ref[5, :width, :]
    out_ref[6, width:, :] = jnp.where(even, late_near_ref[...], late_far_ref[...])
    at, corner = 0, 20
    for number in FLAT[1:]:
        for z in (0, 1):
            put(number, z, at)
            at += 1
    below, above = halos(near_ref, far_ref)
    for arrived, numbers, stays in ((below, RISING, 1), (above, FALLING, 0)):
        for place, number in enumerate(numbers):
            kept, new = stays * width, (1 - stays) * width
            out_ref[number, kept : kept + width, :] = calm_ref[CALM.index(number), kept : kept + width, :]
            out_ref[number, new : new + width, :] = arrived[place]
            if SPEEDS[number][0]:
                put(number, stays, at)
                put(number, 1 - stays, corner)
                at += 1
                corner += 1
    for number in (1, 2):
        for z in (0, 1):
            put(number, z, 16 + 2 * (number - 1) + z)


def gather(calm, moved, near, far, side, late_near, late_far):
    _, cells, lanes = calm.shape
    return pl.pallas_call(
        gather_kernel,
        out_shape=jax.ShapeDtypeStruct((19, cells, lanes), F32),
        name="gather",
        compiler_params=pltpu.CompilerParams(vmem_limit_bytes=VMEM_LIMIT),
        cost_estimate=pl.CostEstimate(flops=1_000, bytes_accessed=3_000_000, transcendentals=0),
    )(calm, moved, near, far, side, late_near, late_far)


def finish_kernel(reply_ref, slab_ref, rank_ref, vel_ref, fric_ref, pull_ref, force_ref):
    slabs, atoms = reply_ref.shape[0], slab_ref.shape[1]
    one_hot = jnp.where(iota((slabs, atoms), 0) == slab_ref[...], 1.0, 0.0).astype(BF16)
    picked = mm(jnp.concatenate(halves(reply_ref[...].T[: 3 * SLOTS]), axis=0), one_hot)
    picked = picked[: 3 * SLOTS] + picked[3 * SLOTS :]
    mine = iota((SLOTS, atoms), 0).astype(F32) == rank_ref[...]
    for c in range(3):
        seen = jnp.sum(jnp.where(mine, picked[c * SLOTS : (c + 1) * SLOTS], 0.0), axis=0, keepdims=True)
        drag = fric_ref[...] * (seen - vel_ref[c : c + 1, :])
        force_ref[c : c + 1, :] = pull_ref[c : c + 1, :] + drag


def finish(reply, slab, rank, vel, fric, pull):
    atoms = slab.shape[1]
    return pl.pallas_call(
        finish_kernel,
        out_shape=jax.ShapeDtypeStruct((3, atoms), F32),
        name="finish",
        compiler_params=pltpu.CompilerParams(vmem_limit_bytes=VMEM_LIMIT),
        cost_estimate=pl.CostEstimate(flops=20_000_000, bytes_accessed=100_000, transcendentals=0),
    )(reply, slab, rank, vel, fric, pull)


def message(table, own_half, rbf, w_out, nbrs, bonds, spacing, basis):
    feats, block = own_half.shape
    atoms = table.shape[1]
    centers = iota((basis, block), 0).astype(F32) * spacing
    rows = iota((atoms, block), 0)
    total, force = None, None
    for nbr, bond in zip(nbrs, bonds):
        place = nbr // atoms
        one_hot = jnp.where(rows == nbr % atoms, 1.0, 0.0).astype(BF16)
        length = jnp.sqrt(bond[0] * bond[0] + bond[1] * bond[1] + bond[2] * bond[2] + 1e-6)
        scaled = (length - centers) * (1.0 / spacing)
        rad_hi, rad_lo = halves(jnp.exp(-scaled * scaled))
        radial = jnp.concatenate([rad_hi, rad_hi, rad_lo, jnp.zeros((feats - 3 * basis, block), BF16)], axis=0)
        seen = mm(table[...], one_hot)
        picked = jnp.where(place == 0, seen[:feats], jnp.where(place == 1, seen[feats : 2 * feats], seen[2 * feats :]))
        half = own_half + picked + mm(rbf, radial)
        hidden = half + half * jnp.tanh(half)
        scalar = jnp.sum(hidden * w_out, axis=0, keepdims=True)
        terms = [scalar * b for b in bond]
        total = hidden if total is None else total + hidden
        force = terms if force is None else [f + t for f, t in zip(force, terms)]
    return total, force


def potential_table(near_ref, own_ref, far_ref, w_self_ref, w_nbr_ref, table, own_half):
    feats = own_ref.shape[0]
    above = jnp.where(even_device(), 2 * feats, 0)
    for start, ref in ((above, near_ref), (feats, own_ref), (2 * feats - above, far_ref)):
        value = mm(w_nbr_ref[...], ref[...]).astype(BF16)
        rows = pl.ds(start if isinstance(start, int) else pl.multiple_of(start, feats), feats)
        table[rows, :] = (value.astype(F32) * 0.5).astype(BF16)
    own_half[...] = 0.5 * mm(w_self_ref[...], own_ref[...])


def potential_first_kernel(
    far_ref,
    own_ref,
    near_ref,
    nbr_ref,
    bond_ref,
    w_self_ref,
    w_nbr_ref,
    w_rbf_ref,
    w_out_ref,
    force_ref,
    new_ref,
    table,
    own_half,
):
    potential_table(near_ref, own_ref, far_ref, w_self_ref, w_nbr_ref, table, own_half)
    potential_block(0, own_ref, nbr_ref, bond_ref, w_rbf_ref, w_out_ref, table, own_half, force_ref, new_ref)


def potential_block(start, own_ref, nbr_ref, bond_ref, w_rbf_ref, w_out_ref, table_ref, half_ref, force_ref, new_ref):
    block = force_ref.shape[1] - start
    count, basis = nbr_ref.shape[0], w_rbf_ref.shape[0]
    cols = slice(start, start + block)
    feats = own_ref.shape[0]
    rbf_hi, rbf_lo = halves(0.5 * w_rbf_ref[...])
    rbf_hi, rbf_lo = rbf_hi.astype(F32), rbf_lo.astype(F32)
    rest = jnp.zeros((feats - 3 * basis, feats), F32)
    rbf = jnp.concatenate([rbf_hi, rbf_lo, rbf_hi, rest], axis=0).T.astype(BF16)
    w_out = jnp.broadcast_to(w_out_ref[...], (8, feats)).T[:, 0:1]
    total, force = message(
        table_ref,
        half_ref[:, cols],
        rbf,
        w_out,
        [nbr_ref[k : k + 1, cols] for k in range(count)],
        [[bond_ref[c, k : k + 1, cols] for c in range(3)] for k in range(count)],
        RADIAL_REACH / (basis - 1),
        basis,
    )
    for c in range(3):
        force_ref[c : c + 1, cols] = force[c]
    new_ref[:, cols] = (own_ref[:, cols].astype(F32) + total * (1.0 / count)).astype(BF16)


def potential_second_kernel(
    far_ref,
    own_ref,
    near_ref,
    nbr_ref,
    bond_ref,
    w_self_ref,
    w_nbr_ref,
    w_rbf_ref,
    w_out_ref,
    first_force_ref,
    first_new_ref,
    force_ref,
    new_ref,
    table,
    own_half,
):
    half = first_new_ref.shape[1]
    force_ref[:, :half] = first_force_ref[...]
    new_ref[:, :half] = first_new_ref[...]
    potential_table(near_ref, own_ref, far_ref, w_self_ref, w_nbr_ref, table, own_half)
    potential_block(half, own_ref, nbr_ref, bond_ref, w_rbf_ref, w_out_ref, table, own_half, force_ref, new_ref)


def potential(kernel, name, columns, flops, *args):
    feats, atoms = args[1].shape
    return pl.pallas_call(
        kernel,
        out_shape=(
            jax.ShapeDtypeStruct((3, columns), F32),
            jax.ShapeDtypeStruct((feats, columns), BF16),
        ),
        scratch_shapes=[
            pltpu.VMEM((3 * feats, atoms), BF16),
            pltpu.VMEM((feats, atoms), F32),
        ],
        name=name,
        compiler_params=pltpu.CompilerParams(vmem_limit_bytes=VMEM_LIMIT),
        cost_estimate=pl.CostEstimate(flops=flops, bytes_accessed=100_000, transcendentals=0),
    )(*args)


def body(
    slabs,
    populations,
    relax_rates,
    slab,
    stencil_base,
    frac,
    atom_vel,
    friction,
    features,
    neighbors,
    bonds,
    w_self,
    w_nbr,
    w_rbf,
    w_out,
):
    _, planes, width, depth = populations.shape
    atoms = slab.shape[0]
    chip = [(i, i ^ 1) for i in range(slabs)]
    link = [(i, (i - 1 if i % 2 == 0 else i + 1) % slabs) for i in range(slabs)]
    across = [(0, 1), (1, 0)]
    slab_row = slab.reshape(1, atoms)
    friction_row = friction.reshape(1, atoms)

    mail, rank = pack(slab_row, stencil_base.reshape(1, atoms), frac, atom_vel, friction_row, slabs)
    sent = features
    near_features = lax.ppermute(sent, "fluid", chip)
    far_features = lax.ppermute(sent, "fluid", link)
    mail = lax.all_to_all(mail.reshape(slabs, 1, 128), "fluid", split_axis=0, concat_axis=0, tiled=True)
    nbrs, bonds, w_rbf, w_out = neighbors.T, bonds.transpose(0, 2, 1), w_rbf.T, w_out.reshape(1, -1)
    rest, axis, vel, near, far = relax(
        relax_rates,
        populations.reshape(19, planes * width, depth),
        features,
        nbrs,
        bonds,
        w_self,
        w_nbr,
        w_rbf,
        w_out,
    )
    calm, side = stream(rest)
    far = lax.ppermute(far, "fluid", link)
    near = lax.ppermute(near, "fluid", chip)
    around = (far_features, features, near_features, nbrs, bonds, w_self, w_nbr, w_rbf, w_out)
    first_pull, first_new = potential(potential_first_kernel, "potential_first", atoms // 2, FIRST_FLOPS, *around)
    mail, first_pull, side = lax.optimization_barrier((mail, first_pull, side))

    reply, slot, wy_hi, wy_lo = look(mail.reshape(slabs, 128), vel)
    reply = lax.all_to_all(reply.reshape(slabs, 1, 128), "fluid", split_axis=0, concat_axis=0, tiled=True)
    moved, late_near, late_far, side = push(axis, slot, wy_hi, wy_lo, side, near, far)
    side = lax.ppermute(side, "group", across)
    late_far = lax.ppermute(late_far, "fluid", link)
    late_near = lax.ppermute(late_near, "fluid", chip)
    first_pull, moved = lax.optimization_barrier((first_pull, moved))
    pull, new_features = potential(
        potential_second_kernel, "potential_second", atoms, SECOND_FLOPS, *around, first_pull, first_new
    )
    pops = gather(calm, moved, near, far, side, late_near, late_far)
    atom_force = finish(reply.reshape(slabs, 128), slab_row, rank, atom_vel, friction_row, pull)
    return pops.reshape(populations.shape), atom_force, new_features


def solution(mesh):
    in_specs = (
        P(None, "fluid", "group", None),
        P(),
        P(("fluid", "group"), None),
        P(("fluid", "group")),
        P(None, ("fluid", "group")),
        P(None, ("fluid", "group")),
        P(("fluid", "group")),
        P(None, ("fluid", "group")),
        P(("fluid", "group"), None),
        P(None, ("fluid", "group"), None),
        P(),
        P(),
        P(),
        P(),
    )
    out_specs = (
        P(None, "fluid", "group", None),
        P(None, ("fluid", "group")),
        P(None, ("fluid", "group")),
    )
    return jax.shard_map(
        functools.partial(body, mesh.shape["fluid"]),
        mesh=mesh,
        in_specs=in_specs,
        out_specs=out_specs,
        check_vma=False,
    )
```

```python
import functools

import jax
import jax.numpy as jnp
from jax import lax
from jax.experimental import pallas as pl
from jax.experimental.pallas import tpu as pltpu
from jax.sharding import PartitionSpec as P

F32 = jnp.float32
BF16 = jnp.bfloat16
I32 = jnp.int32

RADIAL_REACH = 4.0
SLOTS = 8

SPEEDS = (
    (0, 0, 0),
    (1, 0, 0),
    (-1, 0, 0),
    (0, 1, 0),
    (0, -1, 0),
    (0, 0, 1),
    (0, 0, -1),
    (1, 1, 0),
    (-1, -1, 0),
    (1, -1, 0),
    (-1, 1, 0),
    (1, 0, 1),
    (-1, 0, -1),
    (1, 0, -1),
    (-1, 0, 1),
    (0, 1, 1),
    (0, -1, -1),
    (0, 1, -1),
    (0, -1, 1),
)
RISING = (11, 14, 15, 18)
FALLING = (12, 13, 16, 17)
FLAT = (0, 7, 8, 9, 10)
CALM = (0, 7, 8, 9, 10, 11, 12, 13, 14, 15, 16, 17, 18)

EARLY = 5
VMEM_LIMIT = 48 * 1024 * 1024
STREAM_FLOPS = 4_000_000_000
FIRST_FLOPS = 3_500_000_000
SECOND_FLOPS = 500_000_000


def halves(value):
    high = value.astype(BF16)
    low = (value - high.astype(F32)).astype(BF16)
    return high, low


def mm(a, b):
    return jnp.dot(a, b, preferred_element_type=F32)


def mm_nt(a, b):
    return lax.dot_general(a, b, (((1,), (1,)), ((), ())), preferred_element_type=F32)


def iota(shape, dim):
    return lax.broadcasted_iota(I32, shape, dim)


def packed(slab, base, frac_ref, vel_ref, fric, slabs, earlier):
    atoms = slab.shape[1]
    named = iota((slabs, atoms), 0) == slab
    one_hot = jnp.where(named, 1.0, 0.0)
    one_hot_b = one_hot.astype(BF16)
    slab_rows, run = one_hot_b.shape[0], earlier.shape[0]
    runs = [one_hot_b[:, at : at + run] for at in range(0, atoms, run)]
    counts = mm(jnp.concatenate(runs, axis=0), earlier)
    before, total = [], 0.0
    for at in range(len(runs)):
        part = counts[at * slab_rows : (at + 1) * slab_rows]
        before.append(part[:, :run] + total)
        total = total + part[:, run:]
    before = jnp.concatenate(before, axis=1)
    rank = jnp.sum(one_hot * before, axis=0, keepdims=True)
    mine = iota((SLOTS, atoms), 0).astype(F32) == rank
    rows = [frac_ref[c : c + 1, :] for c in range(3)]
    rows += [vel_ref[c : c + 1, :] for c in range(3)]
    rows += [fric, base.astype(F32)]
    spread = [jnp.where(mine, row, 0.0) for row in rows]
    both = mm_nt(one_hot_b, jnp.concatenate(halves(jnp.concatenate(spread, axis=0)), axis=0))
    return both + pltpu.roll(both, both.shape[1] // 2, 1), rank


def moments_of(d):
    m = [None] * 19
    quad = {}
    for name, (pp, nn, pn, np_) in dict(xy=(7, 8, 9, 10), xz=(11, 12, 13, 14), yz=(15, 16, 17, 18)).items():
        same, cross = d[pp] + d[nn], d[pn] + d[np_]
        odd_same, odd_cross = d[pp] - d[nn], d[pn] - d[np_]
        quad[name] = (same + cross, same - cross, odd_same + odd_cross, odd_same - odd_cross)
    sxy, m[4], m[10], m[12] = quad["xy"]
    sxz, m[5], m[11], m[13] = quad["xz"]
    syz, m[6], m[15], m[14] = quad["yz"]
    m[16], m[17], m[18] = sxy, sxz, syz
    ax, ay, az = d[1] + d[2], d[3] + d[4], d[5] + d[6]
    m[0] = (d[0] + ax) + (ay + az) + (sxy + (sxz + syz))
    m[1] = (d[1] - d[2]) + (m[10] + m[11])
    m[2] = (d[3] - d[4]) + (m[12] + m[15])
    m[3] = (d[5] - d[6]) + (m[13] + m[14])
    m[7] = ax + (sxy + sxz)
    m[8] = ay + (sxy + syz)
    m[9] = az + (sxz + syz)
    return m


def populations_of(m):
    f = [None] * 19
    for (pp, nn, pn, np_), (s, c, first, second) in (
        ((7, 8, 9, 10), (m[16], m[4], m[10], m[12])),
        ((11, 12, 13, 14), (m[17], m[5], m[11], m[13])),
        ((15, 16, 17, 18), (m[18], m[6], m[15], m[14])),
    ):
        same, cross = 0.25 * (s + c), 0.25 * (s - c)
        odd_same, odd_cross = 0.25 * (first + second), 0.25 * (first - second)
        f[pp], f[nn] = same + odd_same, same - odd_same
        f[pn], f[np_] = cross + odd_cross, cross - odd_cross
    for plus, minus, square, line, squares, lines in (
        (1, 2, m[7], m[1], (m[16], m[17]), (m[10], m[11])),
        (3, 4, m[8], m[2], (m[16], m[18]), (m[12], m[15])),
        (5, 6, m[9], m[3], (m[17], m[18]), (m[13], m[14])),
    ):
        even = 0.5 * (square - (squares[0] + squares[1]))
        odd = 0.5 * (line - (lines[0] + lines[1]))
        f[plus], f[minus] = even + odd, even - odd
    f[0] = m[0] - (m[7] + (m[8] + m[9])) + (m[16] + (m[17] + m[18]))
    return f


def equilibrium_of(density, u):
    ux, uy, uz = u
    rest = 1.0 - 1.5 * (ux * ux + uy * uy + uz * uz)
    eq = [None] * 19
    eq[0] = (1.0 / 3.0) * density * rest
    scale_axis, scale_diagonal = (1.0 / 18.0) * density, (1.0 / 36.0) * density
    for plus, minus, along, scale in (
        (1, 2, ux, scale_axis),
        (3, 4, uy, scale_axis),
        (5, 6, uz, scale_axis),
        (7, 8, ux + uy, scale_diagonal),
        (9, 10, ux - uy, scale_diagonal),
        (11, 12, ux + uz, scale_diagonal),
        (13, 14, ux - uz, scale_diagonal),
        (15, 16, uy + uz, scale_diagonal),
        (17, 18, uy - uz, scale_diagonal),
    ):
        even = rest + 4.5 * along * along
        odd = 3.0 * along
        eq[plus], eq[minus] = scale * (even + odd), scale * (even - odd)
    return eq


def shifted(plane, number):
    cx, cy, _ = SPEEDS[number]
    if cy:
        plane = pltpu.roll(plane, cy % plane.shape[1], 1)
    if cx:
        plane = pltpu.roll(plane, cx % plane.shape[0], 0)
    return plane


def edge(plane, number):
    width = plane.shape[0]
    return plane[0:1] if SPEEDS[number][0] > 0 else plane[width - 1 : width]


def pack_kernel(
    slab_hbm, base_hbm, frac_hbm, vel_hbm, fric_hbm, mail_ref, rank_ref, slab_ref, base_ref, frac_ref, vel_ref, fric_ref, sems
):
    pairs = (
        (slab_hbm, slab_ref),
        (base_hbm, base_ref),
        (frac_hbm, frac_ref),
        (vel_hbm, vel_ref),
        (fric_hbm, fric_ref),
    )
    copies = [pltpu.make_async_copy(src, dst, sems.at[at]) for at, (src, dst) in enumerate(pairs)]
    for copy in copies:
        copy.start()
    earlier = jnp.where(iota((128, 256), 0) < iota((128, 256), 1), 1.0, 0.0).astype(BF16)
    for copy in copies:
        copy.wait()
    mail, rank = packed(
        slab_ref[...], base_ref[...], frac_ref, vel_ref, fric_ref[...], mail_ref.shape[0], earlier
    )
    mail_ref[...] = mail
    rank_ref[...] = rank


def pack(slab, base, frac, vel, fric, slabs):
    atoms = slab.shape[1]
    vmem = pl.BlockSpec(memory_space=pltpu.VMEM)
    outside = [pltpu.with_memory_space_constraint(x, pltpu.HBM) for x in (slab, base, frac, vel, fric)]
    return pl.pallas_call(
        pack_kernel,
        in_specs=[pl.BlockSpec(memory_space=pltpu.HBM)] * 5,
        out_specs=[vmem] * 2,
        out_shape=(
            jax.ShapeDtypeStruct((slabs, 128), F32),
            jax.ShapeDtypeStruct((1, atoms), F32),
        ),
        scratch_shapes=[
            pltpu.VMEM((1, atoms), I32),
            pltpu.VMEM((1, atoms), I32),
            pltpu.VMEM((3, atoms), F32),
            pltpu.VMEM((3, atoms), F32),
            pltpu.VMEM((1, atoms), F32),
            pltpu.SemaphoreType.DMA((5,)),
        ],
        name="pack",
        compiler_params=pltpu.CompilerParams(vmem_limit_bytes=VMEM_LIMIT),
        cost_estimate=pl.CostEstimate(flops=400_000_000, bytes_accessed=4_000_000, transcendentals=0),
    )(*outside)


def even_device():
    return lax.axis_index("fluid") % 2 == 0


def relax_kernel(rates_ref, pops_ref, *refs):
    rest_ref, axis_ref, vel_ref, near_ref, far_ref = refs[-5:]
    cells = pops_ref.shape[1]
    width = cells // 2

    def chunk(step, carry):
        rows = pl.ds(pl.multiple_of(step * 8, 8), 8)
        f = [pops_ref[i, rows, :] for i in range(19)]
        low = moments_of(f)
        density = low[0]
        inverse = 1.0 / density
        u = [low[c] * inverse for c in (1, 2, 3)]
        for c in range(3):
            vel_ref[c, rows, :] = u[c]
        eq = equilibrium_of(density, u)
        m = moments_of([f[i] - eq[i] for i in range(19)])
        relaxed = populations_of([rates_ref[i] * m[i] for i in range(19)])
        for i in range(19):
            if i in CALM:
                rest_ref[CALM.index(i), rows, :] = f[i] - relaxed[i]
            else:
                axis_ref[i - 1, rows, :] = f[i] - relaxed[i]
        return carry

    lax.fori_loop(0, cells // 8, chunk, 0, unroll=4)

    lanes = pops_ref.shape[2]
    even = even_device()
    for place, (rising, falling) in enumerate(zip(RISING, FALLING)):
        cols = slice(place * lanes, (place + 1) * lanes)
        rises = shifted(rest_ref[CALM.index(rising), width:, :], rising)
        falls = shifted(rest_ref[CALM.index(falling), :width, :], falling)
        near_ref[:, cols] = jnp.where(even, rises, falls).astype(BF16)
        far_ref[:, cols] = jnp.where(even, falls, rises).astype(BF16)


def stream_kernel(rest_ref, calm_ref, side_ref):
    cells, lanes = rest_ref.shape[1:]
    width = cells // 2

    def plane(number, z):
        return shifted(rest_ref[CALM.index(number), z * width : (z + 1) * width, :], number)

    edges = []
    for place, number in enumerate(CALM):
        if number in FLAT:
            for z in (0, 1):
                value = plane(number, z)
                calm_ref[place, z * width : (z + 1) * width, :] = value
                if number:
                    edges.append(edge(value, number))
    for numbers, stays in ((RISING, 1), (FALLING, 0)):
        for number in numbers:
            value = plane(number, 1 - stays)
            calm_ref[CALM.index(number), stays * width : (stays + 1) * width, :] = value
            if SPEEDS[number][0]:
                edges.append(edge(value, number))
    side_ref[...] = jnp.concatenate(edges + [jnp.zeros((16 - len(edges), lanes), F32)], axis=0)


def stream(rest):
    _, cells, lanes = rest.shape
    return pl.pallas_call(
        stream_kernel,
        out_shape=(
            jax.ShapeDtypeStruct((13, cells, lanes), F32),
            jax.ShapeDtypeStruct((16, lanes), F32),
        ),
        name="stream",
        compiler_params=pltpu.CompilerParams(vmem_limit_bytes=VMEM_LIMIT),
        cost_estimate=pl.CostEstimate(flops=STREAM_FLOPS, bytes_accessed=100_000, transcendentals=0),
    )(rest)


def relax(rates, pops, *later):
    _, cells, lanes = pops.shape
    width = cells // 2
    vmem = pl.BlockSpec(memory_space=pltpu.VMEM)
    return pl.pallas_call(
        relax_kernel,
        in_specs=[pl.BlockSpec(memory_space=pltpu.SMEM)] + [vmem] * (1 + len(later)),
        out_specs=[vmem] * 5,
        out_shape=(
            jax.ShapeDtypeStruct((13, cells, lanes), F32),
            jax.ShapeDtypeStruct((6, cells, lanes), F32),
            jax.ShapeDtypeStruct((3, cells, lanes), F32),
            jax.ShapeDtypeStruct((width, 4 * lanes), BF16),
            jax.ShapeDtypeStruct((width, 4 * lanes), BF16),
        ),
        name="relax",
        compiler_params=pltpu.CompilerParams(vmem_limit_bytes=VMEM_LIMIT),
        cost_estimate=pl.CostEstimate(flops=10_000_000, bytes_accessed=6_000_000, transcendentals=0),
    )(rates, pops, *later)


def look_kernel(mail_ref, vel_ref, reply_ref, slot_ref, wy_hi, wy_lo):
    comps, cells, depth = vel_ref.shape
    width = cells // 2
    slots = mail_ref.shape[0]
    t = mail_ref[...].T
    field = lambda v: t[v * SLOTS : (v + 1) * SLOTS, :]
    fx, fy, fz = field(0), field(1), field(2)
    atom_vel = [field(3), field(4), field(5)]
    friction = field(6)
    base = field(7).astype(I32)
    x0 = (base // depth) % width
    y0 = base % depth
    y1 = (y0 + 1) % depth
    gx, gy, gz = 1.0 - fx, 1.0 - fy, 1.0 - fz
    row_y = iota((depth, slots), 0)
    row_x = iota((width, slots), 0)

    v_hi, v_lo = halves(vel_ref[...].reshape(comps * cells, depth))
    v_parts = jnp.concatenate([v_hi, v_lo, v_hi], axis=1)
    values = [[], [], []]
    for first in range(0, SLOTS, 2):
        wx, weights = [], []
        for r in (first, first + 1):
            one = slice(r, r + 1)
            weights.append(
                jnp.where(row_y == y0[one], gy[one], 0.0) + jnp.where(row_y == y1[one], fy[one], 0.0)
            )
            wx.append(jnp.where(row_x == x0[one], gx[one], 0.0) + jnp.where(row_x == x0[one] + 1, fx[one], 0.0))
        hi, lo = halves(jnp.concatenate(weights, axis=1))
        cols = slice(first * slots, (first + 2) * slots)
        wy_hi[:, cols] = hi
        wy_lo[:, cols] = lo
        pair = mm(v_parts, jnp.concatenate([hi, hi, lo], axis=0))
        for r in (first, first + 1):
            one = slice(r, r + 1)
            seen = pair[:, (r - first) * slots : (r - first + 1) * slots]
            for c in range(3):
                close = seen[c * cells : c * cells + width]
                beyond = seen[c * cells + width : (c + 1) * cells]
                value = wx[r - first] * (close * gz[one] + beyond * fz[one])
                values[c].append(jnp.sum(value, axis=0, keepdims=True))
    rows = jnp.concatenate([row for c in range(3) for row in values[c]], axis=0)
    reply_ref[...] = jnp.concatenate([rows, jnp.zeros((128 - 3 * SLOTS, slots), F32)], axis=0).T
    slot_ref[0:SLOTS, :] = x0.astype(F32)
    slot_ref[SLOTS : 2 * SLOTS, :] = fx
    slot_ref[2 * SLOTS : 3 * SLOTS, :] = fz
    for c in range(3):
        pull = friction * (atom_vel[c] - rows[c * SLOTS : (c + 1) * SLOTS])
        slot_ref[(3 + c) * SLOTS : (4 + c) * SLOTS, :] = pull


def look(mail, vel):
    _, _, depth = vel.shape
    slabs = mail.shape[0]
    return pl.pallas_call(
        look_kernel,
        out_shape=(
            jax.ShapeDtypeStruct((slabs, 128), F32),
            jax.ShapeDtypeStruct((6 * SLOTS, slabs), F32),
            jax.ShapeDtypeStruct((depth, SLOTS * slabs), BF16),
            jax.ShapeDtypeStruct((depth, SLOTS * slabs), BF16),
        ),
        name="look",
        compiler_params=pltpu.CompilerParams(vmem_limit_bytes=VMEM_LIMIT),
        cost_estimate=pl.CostEstimate(flops=500_000_000, bytes_accessed=1_000_000, transcendentals=0),
    )(mail, vel)


def halos(near_ref, far_ref):
    lanes = near_ref.shape[1] // 4
    even = even_device()
    below, above = [], []
    for place in range(4):
        cols = slice(place * lanes, (place + 1) * lanes)
        near = near_ref[:, cols].astype(F32)
        far = far_ref[:, cols].astype(F32)
        below.append(jnp.where(even, far, near))
        above.append(jnp.where(even, near, far))
    return below, above


def push_kernel(
    axis_ref,
    slot_ref,
    wy_hi,
    wy_lo,
    early_ref,
    near_ref,
    far_ref,
    moved_ref,
    late_near_ref,
    late_far_ref,
    side_ref,
    force_ref,
    a_hi,
    a_lo,
):
    cells = axis_ref.shape[1]
    width = cells // 2
    slots = slot_ref.shape[1]
    row_x = iota((width, slots), 0)
    for r in range(SLOTS):
        cols = slice(r * slots, (r + 1) * slots)
        row = lambda v: slot_ref[v * SLOTS + r : v * SLOTS + r + 1, :]
        x0, fx, fz = row(0).astype(I32), row(1), row(2)
        wx = jnp.where(row_x == x0, 1.0 - fx, 0.0) + jnp.where(row_x == x0 + 1, fx, 0.0)
        for c in range(3):
            for z, weight in ((0, 1.0 - fz), (1, fz)):
                hi, lo = halves(wx * (weight * row(3 + c)))
                start = c * cells + z * width
                a_hi[start : start + width, cols] = hi
                a_lo[start : start + width, cols] = lo
    for c in (2, 0, 1):
        rows = slice(c * cells, (c + 1) * cells)
        force_ref[c] = mm_nt(a_hi[rows], wy_hi[...]) + (mm_nt(a_lo[rows], wy_hi[...]) + mm_nt(a_hi[rows], wy_lo[...]))
    edges = []
    for number in (5, 6, 1, 2, 3, 4):
        place = number - 1
        sign = 0.5 if number % 2 else -0.5
        for z in (0, 1):
            rows = slice(z * width, (z + 1) * width)
            value = shifted(axis_ref[place, rows, :] + sign * force_ref[place // 2, rows, :], number)
            if number == 5:
                if z == 1:
                    rises = value
                moved_ref[place, (1 - z) * width : (2 - z) * width, :] = value
            elif number == 6:
                if z == 0:
                    falls = value
                moved_ref[place, (1 - z) * width : (2 - z) * width, :] = value
            else:
                moved_ref[place, rows, :] = value
                if number in (1, 2):
                    edges.append(edge(value, number))
    even = even_device()
    late_near_ref[...] = jnp.where(even, rises, falls)
    late_far_ref[...] = jnp.where(even, falls, rises)
    for planes, numbers in zip(halos(near_ref, far_ref), (RISING, FALLING)):
        for plane, number in zip(planes, numbers):
            if SPEEDS[number][0]:
                edges.append(edge(plane, number))
    side_ref[0:16, :] = early_ref[...]
    side_ref[16:24, :] = jnp.concatenate(edges, axis=0)


def push(axis, slot, wy_hi, wy_lo, early, near, far):
    _, cells, lanes = axis.shape
    slots = wy_hi.shape[1]
    width = cells // 2
    return pl.pallas_call(
        push_kernel,
        out_shape=(
            jax.ShapeDtypeStruct((6, cells, lanes), F32),
            jax.ShapeDtypeStruct((width, lanes), F32),
            jax.ShapeDtypeStruct((width, lanes), F32),
            jax.ShapeDtypeStruct((24, lanes), F32),
        ),
        scratch_shapes=[
            pltpu.VMEM((3, cells, lanes), F32),
            pltpu.VMEM((3 * cells, slots), BF16),
            pltpu.VMEM((3 * cells, slots), BF16),
        ],
        name="push",
        compiler_params=pltpu.CompilerParams(vmem_limit_bytes=VMEM_LIMIT),
        cost_estimate=pl.CostEstimate(flops=500_000_000, bytes_accessed=1_500_000, transcendentals=0),
    )(axis, slot, wy_hi, wy_lo, early, near, far)


def gather_kernel(calm_ref, moved_ref, near_ref, far_ref, side_ref, late_near_ref, late_far_ref, out_ref):
    cells = calm_ref.shape[1]
    width = cells // 2

    def put(number, z, at):
        row = z * width + (0 if SPEEDS[number][0] > 0 else width - 1)
        out_ref[number, row : row + 1, :] = side_ref[at : at + 1, :]

    for place, number in enumerate(CALM):
        if number in FLAT:
            out_ref[number] = calm_ref[place]
    for place in range(4):
        out_ref[place + 1] = moved_ref[place]
    even = even_device()
    out_ref[5, width:, :] = moved_ref[4, width:, :]
    out_ref[5, :width, :] = jnp.where(even, late_far_ref[...], late_near_ref[...])
    out_ref[6, :width, :] = moved_ref[5, :width, :]
    out_ref[6, width:, :] = jnp.where(even, late_near_ref[...], late_far_ref[...])
    at, corner = 0, 20
    for number in FLAT[1:]:
        for z in (0, 1):
            put(number, z, at)
            at += 1
    below, above = halos(near_ref, far_ref)
    for arrived, numbers, stays in ((below, RISING, 1), (above, FALLING, 0)):
        for place, number in enumerate(numbers):
            kept, new = stays * width, (1 - stays) * width
            out_ref[number, kept : kept + width, :] = calm_ref[CALM.index(number), kept : kept + width, :]
            out_ref[number, new : new + width, :] = arrived[place]
            if SPEEDS[number][0]:
                put(number, stays, at)
                put(number, 1 - stays, corner)
                at += 1
                corner += 1
    for number in (1, 2):
        for z in (0, 1):
            put(number, z, 16 + 2 * (number - 1) + z)


def gather(calm, moved, near, far, side, late_near, late_far):
    _, cells, lanes = calm.shape
    return pl.pallas_call(
        gather_kernel,
        out_shape=jax.ShapeDtypeStruct((19, cells, lanes), F32),
        name="gather",
        compiler_params=pltpu.CompilerParams(vmem_limit_bytes=VMEM_LIMIT),
        cost_estimate=pl.CostEstimate(flops=1_000, bytes_accessed=3_000_000, transcendentals=0),
    )(calm, moved, near, far, side, late_near, late_far)


def finish_kernel(reply_ref, slab_ref, rank_ref, vel_ref, fric_ref, pull_ref, force_ref):
    slabs, atoms = reply_ref.shape[0], slab_ref.shape[1]
    one_hot = jnp.where(iota((slabs, atoms), 0) == slab_ref[...], 1.0, 0.0).astype(BF16)
    picked = mm(jnp.concatenate(halves(reply_ref[...].T[: 3 * SLOTS]), axis=0), one_hot)
    picked = picked[: 3 * SLOTS] + picked[3 * SLOTS :]
    mine = iota((SLOTS, atoms), 0).astype(F32) == rank_ref[...]
    for c in range(3):
        seen = jnp.sum(jnp.where(mine, picked[c * SLOTS : (c + 1) * SLOTS], 0.0), axis=0, keepdims=True)
        drag = fric_ref[...] * (seen - vel_ref[c : c + 1, :])
        force_ref[c : c + 1, :] = pull_ref[c : c + 1, :] + drag


def finish(reply, slab, rank, vel, fric, pull):
    atoms = slab.shape[1]
    return pl.pallas_call(
        finish_kernel,
        out_shape=jax.ShapeDtypeStruct((3, atoms), F32),
        name="finish",
        compiler_params=pltpu.CompilerParams(vmem_limit_bytes=VMEM_LIMIT),
        cost_estimate=pl.CostEstimate(flops=20_000_000, bytes_accessed=100_000, transcendentals=0),
    )(reply, slab, rank, vel, fric, pull)


def message(table, own_half, rbf, w_out, nbrs, bonds, spacing, basis):
    feats, block = own_half.shape
    atoms = table.shape[1]
    centers = iota((basis, block), 0).astype(F32) * spacing
    rows = iota((atoms, block), 0)
    total, force = None, None
    for nbr, bond in zip(nbrs, bonds):
        place = nbr // atoms
        one_hot = jnp.where(rows == nbr % atoms, 1.0, 0.0).astype(BF16)
        length = jnp.sqrt(bond[0] * bond[0] + bond[1] * bond[1] + bond[2] * bond[2] + 1e-6)
        scaled = (length - centers) * (1.0 / spacing)
        rad_hi, rad_lo = halves(jnp.exp(-scaled * scaled))
        radial = jnp.concatenate([rad_hi, rad_hi, rad_lo, jnp.zeros((feats - 3 * basis, block), BF16)], axis=0)
        seen = mm(table[...], one_hot)
        picked = jnp.where(place == 0, seen[:feats], jnp.where(place == 1, seen[feats : 2 * feats], seen[2 * feats :]))
        half = own_half + picked + mm(rbf, radial)
        hidden = half + half * jnp.tanh(half)
        scalar = jnp.sum(hidden * w_out, axis=0, keepdims=True)
        terms = [scalar * b for b in bond]
        total = hidden if total is None else total + hidden
        force = terms if force is None else [f + t for f, t in zip(force, terms)]
    return total, force


def potential_table(near_ref, own_ref, far_ref, w_self_ref, w_nbr_ref, table, own_half):
    feats = own_ref.shape[0]
    above = jnp.where(even_device(), 2 * feats, 0)
    for start, ref in ((above, near_ref), (feats, own_ref), (2 * feats - above, far_ref)):
        value = mm(w_nbr_ref[...], ref[...]).astype(BF16)
        rows = pl.ds(start if isinstance(start, int) else pl.multiple_of(start, feats), feats)
        table[rows, :] = (value.astype(F32) * 0.5).astype(BF16)
    own_half[...] = 0.5 * mm(w_self_ref[...], own_ref[...])


def potential_sums(cols, ks, own_ref, nbr_ref, bond_ref, w_rbf_ref, w_out_ref, table, own_half):
    basis = w_rbf_ref.shape[0]
    feats = own_ref.shape[0]
    rbf_hi, rbf_lo = halves(0.5 * w_rbf_ref[...])
    rbf_hi, rbf_lo = rbf_hi.astype(F32), rbf_lo.astype(F32)
    rest = jnp.zeros((feats - 3 * basis, feats), F32)
    rbf = jnp.concatenate([rbf_hi, rbf_lo, rbf_hi, rest], axis=0).T.astype(BF16)
    w_out = jnp.broadcast_to(w_out_ref[...], (8, feats)).T[:, 0:1]
    return message(
        table,
        own_half[:, cols],
        rbf,
        w_out,
        [nbr_ref[k : k + 1, cols] for k in ks],
        [[bond_ref[c, k : k + 1, cols] for c in range(3)] for k in ks],
        RADIAL_REACH / (basis - 1),
        basis,
    )


def potential_first_kernel(
    near_ref,
    own_ref,
    far_ref,
    nbr_ref,
    bond_ref,
    w_self_ref,
    w_nbr_ref,
    w_rbf_ref,
    w_out_ref,
    force_ref,
    new_ref,
    part_force_ref,
    part_ref,
    table,
    own_half,
):
    potential_table(near_ref, own_ref, far_ref, w_self_ref, w_nbr_ref, table, own_half)
    atoms, count = own_ref.shape[1], nbr_ref.shape[0]
    args = (own_ref, nbr_ref, bond_ref, w_rbf_ref, w_out_ref, table, own_half)
    cols = slice(0, atoms // 2)
    total, force = potential_sums(cols, range(count), *args)
    for c in range(3):
        force_ref[c : c + 1, :] = force[c]
    new_ref[...] = (own_ref[:, cols].astype(F32) + total * (1.0 / count)).astype(BF16)
    total, force = potential_sums(slice(atoms // 2, atoms), range(EARLY), *args)
    for c in range(3):
        part_force_ref[c : c + 1, :] = force[c]
    part_ref[...] = total


def potential_second_kernel(
    near_ref,
    own_ref,
    far_ref,
    nbr_ref,
    bond_ref,
    w_self_ref,
    w_nbr_ref,
    w_rbf_ref,
    w_out_ref,
    first_force_ref,
    first_new_ref,
    part_force_ref,
    part_ref,
    force_ref,
    new_ref,
    table,
    own_half,
):
    atoms, count = own_ref.shape[1], nbr_ref.shape[0]
    cols = slice(atoms // 2, atoms)
    force_ref[:, : atoms // 2] = first_force_ref[...]
    new_ref[:, : atoms // 2] = first_new_ref[...]
    potential_table(near_ref, own_ref, far_ref, w_self_ref, w_nbr_ref, table, own_half)
    total, force = potential_sums(
        cols, range(EARLY, count), own_ref, nbr_ref, bond_ref, w_rbf_ref, w_out_ref, table, own_half
    )
    for c in range(3):
        force_ref[c : c + 1, cols] = part_force_ref[c : c + 1, :] + force[c]
    new_ref[:, cols] = (own_ref[:, cols].astype(F32) + (part_ref[...] + total) * (1.0 / count)).astype(BF16)


def potential(kernel, name, shapes, flops, *args):
    feats, atoms = args[1].shape
    return pl.pallas_call(
        kernel,
        out_shape=tuple(jax.ShapeDtypeStruct(*shape) for shape in shapes),
        scratch_shapes=[
            pltpu.VMEM((3 * feats, atoms), BF16),
            pltpu.VMEM((feats, atoms), F32),
        ],
        name=name,
        compiler_params=pltpu.CompilerParams(vmem_limit_bytes=VMEM_LIMIT),
        cost_estimate=pl.CostEstimate(flops=flops, bytes_accessed=100_000, transcendentals=0),
    )(*args)


def body(
    slabs,
    populations,
    relax_rates,
    slab,
    stencil_base,
    frac,
    atom_vel,
    friction,
    features,
    neighbors,
    bonds,
    w_self,
    w_nbr,
    w_rbf,
    w_out,
):
    _, planes, width, depth = populations.shape
    atoms = slab.shape[0]
    chip = [(i, i ^ 1) for i in range(slabs)]
    link = [(i, (i - 1 if i % 2 == 0 else i + 1) % slabs) for i in range(slabs)]
    across = [(0, 1), (1, 0)]
    slab_row = slab.reshape(1, atoms)
    friction_row = friction.reshape(1, atoms)

    mail, rank = pack(slab_row, stencil_base.reshape(1, atoms), frac, atom_vel, friction_row, slabs)
    sent = features
    near_features = lax.ppermute(sent, "fluid", chip)
    far_features = lax.ppermute(sent, "fluid", link)
    mail = lax.all_to_all(mail.reshape(slabs, 1, 128), "fluid", split_axis=0, concat_axis=0, tiled=True)
    nbrs, bonds, w_rbf, w_out = neighbors.T, bonds.transpose(0, 2, 1), w_rbf.T, w_out.reshape(1, -1)
    rest, axis, vel, near, far = relax(
        relax_rates,
        populations.reshape(19, planes * width, depth),
        features,
        nbrs,
        bonds,
        w_self,
        w_nbr,
        w_rbf,
        w_out,
    )
    calm, side = stream(rest)
    far = lax.ppermute(far, "fluid", link)
    near = lax.ppermute(near, "fluid", chip)
    around = (near_features, features, far_features, nbrs, bonds, w_self, w_nbr, w_rbf, w_out)
    feats, half = features.shape[0], atoms // 2
    shapes = (((3, half), F32), ((feats, half), BF16), ((3, half), F32), ((feats, half), F32))
    first_pull, first_new, part_pull, part = potential(
        potential_first_kernel, "potential_first", shapes, FIRST_FLOPS, *around
    )
    mail, first_pull, side = lax.optimization_barrier((mail, first_pull, side))

    reply, slot, wy_hi, wy_lo = look(mail.reshape(slabs, 128), vel)
    reply = lax.all_to_all(reply.reshape(slabs, 1, 128), "fluid", split_axis=0, concat_axis=0, tiled=True)
    moved, late_near, late_far, side = push(axis, slot, wy_hi, wy_lo, side, near, far)
    side = lax.ppermute(side, "group", across)
    late_far = lax.ppermute(late_far, "fluid", link)
    late_near = lax.ppermute(late_near, "fluid", chip)
    first_pull, moved = lax.optimization_barrier((first_pull, moved))
    shapes = (((3, atoms), F32), ((feats, atoms), BF16))
    first = (first_pull, first_new, part_pull, part)
    pull, new_features = potential(
        potential_second_kernel, "potential_second", shapes, SECOND_FLOPS, *around, *first
    )
    pops = gather(calm, moved, near, far, side, late_near, late_far)
    atom_force = finish(reply.reshape(slabs, 128), slab_row, rank, atom_vel, friction_row, pull)
    return pops.reshape(populations.shape), atom_force, new_features


def solution(mesh):
    in_specs = (
        P(None, "fluid", "group", None),
        P(),
        P(("fluid", "group"), None),
        P(("fluid", "group")),
        P(None, ("fluid", "group")),
        P(None, ("fluid", "group")),
        P(("fluid", "group")),
        P(None, ("fluid", "group")),
        P(("fluid", "group"), None),
        P(None, ("fluid", "group"), None),
        P(),
        P(),
        P(),
        P(),
    )
    out_specs = (
        P(None, "fluid", "group", None),
        P(None, ("fluid", "group")),
        P(None, ("fluid", "group")),
    )
    return jax.shard_map(
        functools.partial(body, mesh.shape["fluid"]),
        mesh=mesh,
        in_specs=in_specs,
        out_specs=out_specs,
        check_vma=False,
    )
```
